256 devices in a mesh: lat: 8 (over y_hi, x), lon: 32 (over z, y_lo, core).
Axes of the slice: x: 4, y: 4 (y_hi: 2, y_lo: 2; y = y_hi * 2 + y_lo), z: 8, core: 2. Of those that a mesh axis runs over, the one named last changes fastest.
Arguments:
- queries: bfloat16 [128, 256, 768], P('lat', 'lon'), may hold values from -8 to 8
- key_vectors: bfloat16 [128, 256, 768], P('lat', 'lon'), may hold values from -8 to 8
- value_vectors: bfloat16 [128, 256, 768], P('lat', 'lon'), may hold values from -12 to 12
- upstream: bfloat16 [128, 256, 768], P('lat', 'lon'), may hold values from -6 to 6
- w_out: bfloat16 [768, 768], replicated, may hold values from -0.21875 to 0.21875
- neighbours: int32 [16, 32, 4], replicated, may hold values from 0 to 511, as said below
- counts: int32 [16, 32], replicated, may hold values from 2 to 4, as said below
Outputs:
- mixed_out: bfloat16 [128, 256, 768], P('lat', 'lon')
- q_grad: bfloat16 [128, 256, 768], P('lat', 'lon')
- k_grad: bfloat16 [128, 256, 768], P('lat', 'lon')
- v_grad: bfloat16 [128, 256, 768], P('lat', 'lon')
- w_grad: float32 [768, 768], replicated
The draws below stay inside these ranges and needn't reach their ends.
Inputs may be any that keep to these rules, and one draw needn't show every extreme that they name: `neighbours`: entry s of block (i, j) names a block i2 * 32 + j2 with i2 within one of i and j2 within one of j around the longitude circle; slot 0 names the block itself, the entries of slots below counts[i, j] are distinct, and the slots at or beyond counts[i, j] name the block itself. `counts`: every block outside the first and the last row of blocks has 4.
All inputs are finite; a program needn't handle non-finite values.
Results may differ from the reference program's by a relative error of at most 0.03.
Values may be sent and summed in bfloat16 or wider, within the bound.
A program may use at most 64 MiB of HBM per device.

```python
import math
import jax
import jax.numpy as jnp
from jax import lax

HEADS = 12
HEAD_DIM = 64
D = 768
BLK = 8
SLOTS = 4
NBLAT = 16
NBLON = 32
NLAT = 128
NLON = 256
TOKENS = 32768


def draw_queries(key, part):
    return jnp.clip(jax.random.normal(jax.random.fold_in(key, 1), (NLAT, NLON, D), jnp.float32), -6.0, 6.0).astype(jnp.bfloat16)


def draw_key_vectors(key, part):
    return jnp.clip(jax.random.normal(jax.random.fold_in(key, 2), (NLAT, NLON, D), jnp.float32), -6.0, 6.0).astype(jnp.bfloat16)


def neighbour_tables(key):
    base_key = jax.random.fold_in(key, 9)
    step_lat = jnp.array([-1, -1, -1, 0, 0, 1, 1, 1], jnp.int32)
    step_lon = jnp.array([-1, 0, 1, -1, 1, -1, 0, 1], jnp.int32)
    block_lat = jnp.arange(NBLAT, dtype=jnp.int32)[:, None, None]
    block_lon = jnp.arange(NBLON, dtype=jnp.int32)[None, :, None]
    cand_lat = block_lat + step_lat
    cand_lon = (block_lon + step_lon) % NBLON
    inside = (cand_lat >= 0) & (cand_lat < NBLAT)
    ranks = jax.random.randint(jax.random.fold_in(base_key, 1), (NBLAT, NBLON, 8), 0, 4096) * 8 + jnp.arange(8, dtype=jnp.int32)
    ranks = jnp.where(inside, ranks, 65536 + jnp.arange(8, dtype=jnp.int32))
    order = jnp.argsort(ranks, axis=-1)
    cand_index = jnp.broadcast_to(cand_lat * NBLON + cand_lon, (NBLAT, NBLON, 8))
    chosen = jnp.take_along_axis(cand_index, order[:, :, :SLOTS - 1], axis=-1)
    own_index = jnp.broadcast_to(block_lat * NBLON + block_lon, (NBLAT, NBLON, 1))
    polar = (block_lat[:, :, 0] == 0) | (block_lat[:, :, 0] == NBLAT - 1)
    drawn_counts = jax.random.randint(jax.random.fold_in(base_key, 2), (NBLAT, NBLON), 2, SLOTS + 1)
    slot_counts = jnp.where(polar, drawn_counts, SLOTS)
    slot_table = jnp.concatenate([own_index, chosen], axis=-1)
    slot_ids = jnp.arange(SLOTS, dtype=jnp.int32)
    slot_table = jnp.where(slot_ids[None, None, :] < slot_counts[:, :, None], slot_table, own_index)
    return (slot_table.astype(jnp.int32), slot_counts.astype(jnp.int32))


def draw_neighbours(key, part):
    return neighbour_tables(key)[0]


def draw_counts(key, part):
    return neighbour_tables(key)[1]


def levels(key, dims, shards, least, top_value):
    level = 1.0
    for dim, blocks in shards:
        draws = jax.random.uniform(jax.random.fold_in(jax.random.fold_in(key, 6), dim), (blocks,), jnp.float32, least / len(shards), top_value / len(shards))
        level = level * jnp.repeat(jnp.exp(draws), dims[dim] // blocks).reshape((-1,) + (1,) * (len(dims) - 1 - dim))
    return level


def bell_draw(own_key, extent, spread, reach, shards=(), held_as=jnp.bfloat16):
    values = jax.random.normal(own_key, extent, jnp.float32) * spread
    if len(shards) > 0:
        values = levels(own_key, extent, shards, -0.22, 0.18) * values
    return jnp.clip(values, min=-reach, max=reach).astype(held_as)


def setup_inputs(seed: int = 0) -> dict:
    splits = jax.random.split(jax.random.key(seed), 8)
    return {
        "queries": draw_queries(jax.random.fold_in(splits[7], 71), 0),
        "key_vectors": draw_key_vectors(jax.random.fold_in(splits[7], 71), 0),
        "value_vectors": bell_draw(splits[2], (NLAT, NLON, D), 2.0, 12.0, ((0, 8), (1, 32))),
        "upstream": bell_draw(splits[3], (NLAT, NLON, D), 1.0, 6.0, ((0, 8), (1, 32))),
        "w_out": bell_draw(splits[4], (D, D), D ** -0.5, 0.21875),
        "neighbours": draw_neighbours(jax.random.fold_in(splits[7], 71), 0),
        "counts": draw_counts(jax.random.fold_in(splits[7], 71), 0),
    }


def to_blocks(token_grid):
    lat_rows, lon_cols, feat_width = token_grid.shape
    block_tiles = token_grid.reshape(lat_rows // BLK, BLK, lon_cols // BLK, BLK, feat_width).transpose(0, 2, 1, 3, 4)
    return block_tiles.reshape(lat_rows // BLK, lon_cols // BLK, BLK * BLK, feat_width)

def from_blocks(block_tiles):
    lat_blocks, lon_blocks, inner_count, feat_width = block_tiles.shape
    token_grid = block_tiles.reshape(lat_blocks, lon_blocks, BLK, BLK, feat_width).transpose(0, 2, 1, 3, 4)
    return token_grid.reshape(lat_blocks * BLK, lon_blocks * BLK, feat_width)

def heads_of(block_tiles):
    return block_tiles.astype(jnp.float32).reshape(block_tiles.shape[0], block_tiles.shape[1], HEADS, HEAD_DIM)

def row_pass(query_tiles, key_sets, value_sets, key_valid, grad_tiles, w_out):
    score_scale = 1.0 / math.sqrt(HEAD_DIM)
    raw = jnp.einsum('nqhd,nkhd->nhqk', heads_of(query_tiles), heads_of(key_sets)) * score_scale
    masked = jnp.where(key_valid[:, None, None, :], raw, -jnp.inf)
    row_top = lax.optimization_barrier(jnp.max(masked, axis=-1, keepdims=True))
    log_total = row_top + jnp.log(lax.optimization_barrier(jnp.sum(jnp.exp(masked - row_top), axis=-1, keepdims=True)))
    attn_probs = jnp.exp(masked - log_total)
    probs_low = attn_probs.astype(jnp.bfloat16)
    attended = jnp.einsum('nhqk,nkhd->nqhd', probs_low.astype(jnp.float32), heads_of(value_sets))
    attended = attended.astype(jnp.bfloat16).reshape(query_tiles.shape)
    feat_width = query_tiles.shape[-1]
    mixed_row = jnp.dot(attended.reshape(-1, feat_width), w_out, preferred_element_type=jnp.float32).astype(jnp.bfloat16)
    d_att = jnp.dot(grad_tiles.reshape(-1, feat_width), w_out.T, preferred_element_type=jnp.float32).astype(jnp.bfloat16)
    d_att = d_att.reshape(query_tiles.shape)
    row_delta = lax.optimization_barrier(jnp.sum(heads_of(d_att) * heads_of(attended), axis=-1)).transpose(0, 2, 1)
    dprobs = jnp.einsum('nqhd,nkhd->nhqk', heads_of(d_att), heads_of(value_sets))
    dscores = (attn_probs * (dprobs - row_delta[..., None]) * score_scale).astype(jnp.bfloat16)
    query_grad = jnp.einsum('nhqk,nkhd->nqhd', dscores.astype(jnp.float32), heads_of(key_sets))
    query_grad = query_grad.astype(jnp.bfloat16).reshape(query_tiles.shape)
    key_terms = jnp.einsum('nhqk,nqhd->nkhd', dscores.astype(jnp.float32), heads_of(query_tiles)).reshape(key_sets.shape)
    value_terms = jnp.einsum('nhqk,nqhd->nkhd', probs_low.astype(jnp.float32), heads_of(d_att)).reshape(key_sets.shape)
    return (mixed_row.reshape(query_tiles.shape), query_grad, key_terms, value_terms, attended)

def reference(queries, key_vectors, value_vectors, upstream, w_out, neighbours, counts):
    feat_width = queries.shape[-1]
    query_tiles = to_blocks(queries)
    grad_tiles = to_blocks(upstream)
    key_flat = to_blocks(key_vectors).reshape(NBLAT * NBLON, BLK * BLK, feat_width)
    value_flat = to_blocks(value_vectors).reshape(NBLAT * NBLON, BLK * BLK, feat_width)
    slot_ok = jnp.arange(SLOTS, dtype=jnp.int32)[None, None, :] < counts[:, :, None]

    def row_step(carry, row_inputs):
        key_acc, value_acc = carry
        query_row, grad_row, index_row, ok_row = row_inputs
        flat_index = index_row.reshape(-1).astype(jnp.int32)
        key_sets = jnp.take(key_flat, flat_index, axis=0).reshape(NBLON, SLOTS * BLK * BLK, feat_width)
        value_sets = jnp.take(value_flat, flat_index, axis=0).reshape(NBLON, SLOTS * BLK * BLK, feat_width)
        key_valid = jnp.repeat(ok_row, BLK * BLK, axis=1)
        mixed_row, query_grad, key_terms, value_terms, attended = row_pass(query_row, key_sets, value_sets, key_valid, grad_row, w_out)
        key_acc = key_acc.at[flat_index].add(key_terms.reshape(NBLON * SLOTS, BLK * BLK, feat_width))
        value_acc = value_acc.at[flat_index].add(value_terms.reshape(NBLON * SLOTS, BLK * BLK, feat_width))
        return ((key_acc, value_acc), (mixed_row, query_grad, attended))
    zero_acc = jnp.zeros((NBLAT * NBLON, BLK * BLK, feat_width), jnp.float32)
    (key_acc, value_acc), (mixed_rows, query_rows, attended_rows) = lax.scan(row_step, (zero_acc, zero_acc), (query_tiles, grad_tiles, neighbours, slot_ok))
    w_grad = jnp.dot(attended_rows.reshape(-1, feat_width).T, grad_tiles.reshape(-1, feat_width), preferred_element_type=jnp.float32) / math.sqrt(TOKENS)
    k_grad = from_blocks(key_acc.astype(jnp.bfloat16).reshape(NBLAT, NBLON, BLK * BLK, feat_width))
    v_grad = from_blocks(value_acc.astype(jnp.bfloat16).reshape(NBLAT, NBLON, BLK * BLK, feat_width))
    return (from_blocks(mixed_rows), from_blocks(query_rows), k_grad, v_grad, w_grad)
```

```python
import math

import jax
import jax.numpy as jnp
from jax import lax
from jax.experimental import pallas as pl
from jax.experimental.pallas import tpu as pltpu
from jax.sharding import PartitionSpec as P

F32 = jnp.float32
BF16 = jnp.bfloat16
MESH = pl.DeviceIdType.MESH

HEAD_DIM = 64
SLOTS = 4
TOK = 64
D = 768
PAIRS = 6
NLON = 32
NLAT = 8
TOKENS = 32768
HALF = D // 2
GROUP = 16
FLAT = HALF * (D // 128)
CHUNK = FLAT // GROUP
OWNERS = 3
PIECE = CHUNK // OWNERS
DEPTH = 8
NT = (((1,), (1,)), ((), ()))
TN = (((0,), (0,)), ((), ()))


def remote(src, dst, send_sem, recv_sem, device):
    return pltpu.make_async_remote_copy(
        src_ref=src,
        dst_ref=dst,
        send_sem=send_sem,
        recv_sem=recv_sem,
        device_id=device,
        device_id_type=MESH,
    )


def kernel(
    q_ref,
    k_ref,
    v_ref,
    u_ref,
    w_ref,
    nb_ref,
    ct_ref,
    mixed_ref,
    dq_ref,
    dk_ref,
    dv_ref,
    wg_ref,
    kvb,
    ucat,
    datt,
    probs,
    att2,
    att_in,
    att_t,
    cb,
    gsp,
    grp,
    gsl,
    grl,
    gso,
    gro,
    wbuf,
    rsin,
    zsum,
    zin,
    wch,
    wfin,
    halo_s,
    halo_r,
    u_s,
    u_r,
    gp_s,
    gp_r,
    gl_s,
    gl_r,
    go_s,
    go_r,
    rs_s,
    rs_r,
    z_s,
    z_r,
    zg_s,
    zg_r,
    ag_s,
    ag_r,
    fw_s,
    fw_r,
):
    a = lax.axis_index("lat")
    b = lax.axis_index("lon")
    core = lax.rem(b, 2)
    ylo = lax.rem(b // 2, 2)
    z = b // 4
    has_up = a > 0
    has_down = a < NLAT - 1
    mate = (a, b + 1 - 2 * core)
    beyond = (a, lax.rem(b + NLON - 1 + 2 * core, NLON))
    up = (a - 1, b)
    down = (a + 1, b)
    oc = 2 * core
    ic = 2 - oc
    n = a * 2 + ylo

    def peer(k):
        m = lax.rem(n + k, GROUP)
        return (m // 2, z * 4 + lax.rem(m, 2) * 2 + core), m

    def zpeer(zz):
        return (a, zz * 4 + ylo * 2 + core)

    barrier = pltpu.get_barrier_semaphore()

    def greet(device):
        pl.semaphore_signal(barrier, inc=1, device_id=device, device_id_type=MESH)

    greet(mate)
    greet(beyond)

    @pl.loop(1, GROUP)
    def _(k):
        greet(peer(k)[0])

    @pl.loop(1, DEPTH)
    def _(k):
        greet(zpeer(lax.rem(z + k, DEPTH)))

    kvb[0, 1, 1:3] = k_ref[...]
    kvb[1, 1, 1:3] = v_ref[...]
    ucat[0:128] = u_ref[...]
    pl.semaphore_wait(barrier, 2 + GROUP - 1 + DEPTH - 1)

    def halo(t, i, src, dst, device):
        return remote(src, dst, halo_s.at[t, i], halo_r.at[t, i], device)

    ins = (k_ref, v_ref)

    def first(t):
        src = ins[t]
        return (
            halo(t, 1, src, kvb.at[t, ic, pl.ds(1, 2)], beyond),
            halo(t, 2, src.at[0], kvb.at[t, 1, 3], up),
            halo(t, 3, src.at[1], kvb.at[t, 1, 0], down),
            halo(t, 0, src, kvb.at[t, oc, pl.ds(1, 2)], mate),
        )

    def second(t):
        return (
            halo(t, 4, kvb.at[t, oc, 1], kvb.at[t, oc, 3], up),
            halo(t, 5, kvb.at[t, oc, 2], kvb.at[t, oc, 0], down),
            halo(t, 6, kvb.at[t, 1, 0], kvb.at[t, oc, 0], mate),
            halo(t, 7, kvb.at[t, 1, 3], kvb.at[t, oc, 3], mate),
        )

    for t in range(2):
        c = first(t)
        c[0].start()
        pl.when(has_up)(c[1].start)
        pl.when(has_down)(c[2].start)
        c[3].start()
    send_u = remote(u_ref, ucat.at[pl.ds(128, 128)], u_s.at[0], u_r.at[0], mate)
    send_u.start()

    datt[...] = lax.dot_general(
        u_ref[...], w_ref[...], NT, preferred_element_type=F32
    ).astype(BF16)
    for t in range(2):
        for s in range(2):
            cb[t, s, SLOTS] = jnp.zeros((TOK, D), F32)

    for t in range(2):
        c = second(t)
        halo(t, 1, k_ref, kvb.at[t, oc, pl.ds(1, 2)], beyond).wait_recv()
        pl.when(has_up)(c[0].start)
        pl.when(has_down)(c[1].start)

        @pl.when(has_up)
        def _():
            halo(t, 3, k_ref.at[0], kvb.at[t, 1, 0], up).wait_recv()
            c[2].start()

        @pl.when(has_down)
        def _():
            halo(t, 2, k_ref.at[0], kvb.at[t, 1, 3], down).wait_recv()
            c[3].start()

    for t in range(2):
        halo(t, 0, k_ref, kvb.at[t, ic, pl.ds(1, 2)], mate).wait_recv()

        @pl.when(has_up)
        def _():
            halo(t, 5, k_ref.at[0], kvb.at[t, oc, 0], up).wait_recv()
            halo(t, 6, k_ref.at[0], kvb.at[t, ic, 0], mate).wait_recv()

        @pl.when(has_down)
        def _():
            halo(t, 4, k_ref.at[0], kvb.at[t, oc, 3], down).wait_recv()
            halo(t, 7, k_ref.at[0], kvb.at[t, ic, 3], mate).wait_recv()

    def places(s_block):
        i = 2 * a + s_block
        out = []
        for s in range(SLOTS):
            name = nb_ref[i, b, s]
            row = lax.div(name, NLON) - i + 1
            col = lax.rem(lax.rem(name, NLON) - b + 1 + NLON, NLON)
            out.append((jnp.clip(col, 0, 2), jnp.clip(row, 0, 2)))
        return out, ct_ref[i, b]

    def blocks_of(t, place, s_block, j):
        return jnp.concatenate(
            [kvb[t, col, row + s_block, :, pl.ds(j * 128, 128)] for col, row in place], axis=0
        )

    low = lax.broadcasted_iota(jnp.int32, (TOK, 128), 1) < HEAD_DIM

    def stacked(x):
        zero = jnp.zeros_like(x)
        return jnp.concatenate([jnp.where(low, x, zero), jnp.where(low, zero, x)], axis=0)

    def queries_of(s_block, j):
        x = q_ref[s_block, :, pl.ds(j * 128, 128)]
        return stacked(x * jnp.asarray(0.125, BF16))

    def unstacked(x):
        return jnp.where(low, x[:TOK], x[TOK:])

    @pl.loop(0, 2)
    def _(s):
        place, count = places(s)
        kept = lax.broadcasted_iota(jnp.int32, (2 * TOK, SLOTS * TOK), 1) < count * TOK
        rows = pl.ds(pl.multiple_of(s * TOK, TOK), TOK)
        scores = []
        for j in range(PAIRS):
            scores.append(
                lax.dot_general(
                    queries_of(s, j), blocks_of(0, place, s, j), NT, preferred_element_type=F32
                )
            )
        for j in range(PAIRS):
            masked = jnp.where(kept, scores[j], -1e30)
            top = jnp.max(masked, axis=-1, keepdims=True)
            e = jnp.exp(masked - top)
            probs[s, j] = e * (1.0 / jnp.sum(e, axis=-1, keepdims=True))
        for j in range(PAIRS):
            o = jnp.dot(
                probs[s, j].astype(BF16), blocks_of(1, place, s, j), preferred_element_type=F32
            )
            att2[j // 3, rows, (j % 3) * 128 : (j % 3) * 128 + 128] = unstacked(o).astype(BF16)

    send_att = remote(att2.at[1 - core], att_in, u_s.at[1], u_r.at[1], mate)
    send_att.start()
    att_t[:, 0:128] = att2[core].T
    att = jnp.concatenate([att2[0], att2[1]], axis=1)
    mixed_ref[...] = jnp.dot(att, w_ref[...], preferred_element_type=F32).astype(BF16)
    remote(u_ref, ucat.at[pl.ds(128, 128)], u_s.at[0], u_r.at[0], mate).wait_recv()
    send_att.wait_recv()
    att_t[:, 128:256] = att_in[...].T
    for g in range(3):
        term = jnp.dot(
            att_t[...], ucat[:, g * 256 : g * 256 + 256], preferred_element_type=F32
        ).astype(BF16)
        wbuf[2 * g * HALF : (2 * g + 1) * HALF] = term[:, :128]
        wbuf[(2 * g + 1) * HALF : (2 * g + 2) * HALF] = term[:, 128:]

    def chunk(m):
        return pl.ds(pl.multiple_of(m * CHUNK, 16), CHUNK)

    def reduce_copy(k):
        device, m = peer(k)
        return remote(wbuf.at[chunk(m)], rsin.at[k], rs_s.at[k], rs_r.at[k], device)

    @pl.loop(1, GROUP)
    def _(k):
        reduce_copy(k).start()

    @pl.loop(0, 2)
    def _(s):
        place, _ = places(s)
        rows = pl.ds(pl.multiple_of(s * TOK, TOK), TOK)
        for j in range(PAIRS):
            lanes = pl.ds(j * 128, 128)
            qs = queries_of(s, j)
            ks = blocks_of(0, place, s, j)
            vs = blocks_of(1, place, s, j)
            da = stacked(datt[rows, lanes])
            at = att2[j // 3, rows, (j % 3) * 128 : (j % 3) * 128 + 128]
            at = jnp.concatenate([at, at], axis=0)
            delta = jnp.sum(da.astype(F32) * at.astype(F32), axis=-1, keepdims=True)
            p = probs[s, j]
            dp = lax.dot_general(da, vs, NT, preferred_element_type=F32)
            ds = (p * (dp - delta)).astype(BF16)
            dq = unstacked(jnp.dot(ds, ks, preferred_element_type=F32)) * 0.125
            dq_ref[s, :, lanes] = dq.astype(BF16)
            dk = lax.dot_general(ds, qs, TN, preferred_element_type=F32)
            dv = lax.dot_general(p.astype(BF16), da, TN, preferred_element_type=F32)
            for i in range(SLOTS):
                cb[0, s, i, :, lanes] = dk[i * TOK : (i + 1) * TOK]
                cb[1, s, i, :, lanes] = dv[i * TOK : (i + 1) * TOK]

    placed = [places(s) for s in range(2)]

    def slot_of(s, row, col):
        slot = jnp.int32(SLOTS)
        place, count = placed[s]
        for i in range(SLOTS):
            hit = (place[i][0] == col) & (place[i][1] == row) & (i < count)
            slot = jnp.where(hit, i, slot)
        return slot

    def terms(t, col, row):
        total = None
        for s in range(2):
            if 0 <= row - s <= 2:
                x = cb[t, s, slot_of(s, row - s, col)]
                total = x if total is None else total + x
        return total

    def to_mate(t):
        return remote(gsp.at[t], grp.at[t], gp_s.at[t], gp_r.at[t], mate)

    def to_lat(t, way, which):
        device = (up, down)[way]
        return remote(
            gsl.at[t, way, which],
            grl.at[t, way, which],
            gl_s.at[t, way, which],
            gl_r.at[t, way, which],
            device,
        )

    def to_beyond(t):
        return remote(gso.at[t], gro.at[t], go_s.at[t], go_r.at[t], beyond)

    conds = (has_up, has_down)
    from_conds = (has_down, has_up)
    for t in range(2):
        for r in range(4):
            gsp[t, r] = terms(t, ic, r).astype(BF16)
        to_mate(t).start()
        for way in range(2):

            @pl.when(conds[way])
            def _():
                gsl[t, way, 0] = terms(t, oc, 3 * way).astype(BF16)
                to_lat(t, way, 0).start()

    total = wbuf[chunk(n), :].astype(F32)
    for k in range(1, GROUP):
        reduce_copy(k).wait_recv()
        total = total + rsin[k].astype(F32)
    zsum[...] = total.astype(BF16)

    def owner_z(o):
        return 3 * o

    def z_copy(o):
        k = lax.rem(owner_z(o) - z + DEPTH, DEPTH)
        return remote(
            zsum.at[pl.ds(o * PIECE, PIECE)], zin.at[k], z_s.at[o], z_r.at[k], zpeer(owner_z(o))
        )

    for o in range(OWNERS):
        pl.when(z != owner_z(o))(z_copy(o).start)

    for t in range(2):
        to_mate(t).wait_recv()
        for way in range(2):

            @pl.when(conds[way])
            def _():
                x = terms(t, 1, 3 * way) + grp[t, 3 * way].astype(F32)
                gsl[t, way, 1] = x.astype(BF16)
                to_lat(t, way, 1).start()

    def z_gather(o, k):
        return remote(
            wch.at[pl.ds(o * PIECE, PIECE)],
            wch.at[pl.ds(o * PIECE, PIECE)],
            zg_s.at[k],
            zg_r.at[o],
            zpeer(lax.rem(owner_z(o) + k, DEPTH)),
        )

    for o in range(OWNERS):

        @pl.when(z == owner_z(o))
        def _():
            acc = zsum[o * PIECE : (o + 1) * PIECE].astype(F32)
            for k in range(1, DEPTH):
                remote(
                    zsum.at[pl.ds(o * PIECE, PIECE)],
                    zin.at[k],
                    z_s.at[o],
                    z_r.at[k],
                    zpeer(lax.rem(z + DEPTH - k, DEPTH)),
                ).wait_recv()
                acc = acc + zin[k].astype(F32)
            wch[o * PIECE : (o + 1) * PIECE] = (acc * (1.0 / math.sqrt(TOKENS))).astype(BF16)
            for k in range(1, DEPTH):
                z_gather(o, k).start()

    for t in range(2):
        for r in range(2):
            x = terms(t, oc, 1 + r)
            gso[t, r] = x.astype(BF16)
        for way in range(2):

            @pl.when(from_conds[way])
            def _():
                to_lat(t, way, 0).wait_recv()
                r = 1 - way
                x = terms(t, oc, 1 + r) + grl[t, way, 0].astype(F32)
                gso[t, r] = x.astype(BF16)

        to_beyond(t).start()

    for o in range(OWNERS):
        pl.when(z != owner_z(o))(z_gather(o, 1).wait_recv)

    def gather_copy(k):
        device, _ = peer(k)
        return remote(wch, wfin.at[core, chunk(n)], ag_s.at[k], ag_r.at[k], device)

    @pl.loop(1, GROUP)
    def _(k):
        gather_copy(k).start()

    wfin[core, chunk(n), :] = wch[...]

    def pass_on(k, half):
        m = lax.rem(n + GROUP - k, GROUP)
        return remote(
            wfin.at[half, chunk(m)], wfin.at[half, chunk(m)], fw_s.at[k], fw_r.at[k], mate
        )

    pass_on(0, core).start()

    outs = (dk_ref, dv_ref)
    for t in range(2):
        to_beyond(t).wait_recv()
        for r in range(2):
            x = terms(t, 1, 1 + r) + grp[t, 1 + r].astype(F32) + gro[t, r].astype(F32)
            outs[t][r] = x.astype(BF16)
        for way in range(2):

            @pl.when(from_conds[way])
            def _():
                to_lat(t, way, 1).wait_recv()
                r = 1 - way
                x = terms(t, 1, 1 + r) + grp[t, 1 + r].astype(F32) + gro[t, r].astype(F32)
                outs[t][r] = (x + grl[t, way, 1].astype(F32)).astype(BF16)

    @pl.loop(1, GROUP)
    def _(k):
        m = lax.rem(n + GROUP - k, GROUP)
        device = (m // 2, z * 4 + lax.rem(m, 2) * 2 + core)
        remote(wch, wfin.at[core, chunk(m)], ag_s.at[k], ag_r.at[k], device).wait_recv()
        pass_on(k, core).start()

    rows_of = pl.ds(pl.multiple_of(core * HALF, HALF), HALF)
    for g in range(D // 128):
        wg_ref[rows_of, g * 128 : g * 128 + 128] = wfin[
            core, g * HALF : (g + 1) * HALF
        ].astype(F32)

    @pl.loop(0, GROUP)
    def _(k):
        pass_on(k, 1 - core).wait_recv()

    rows_of = pl.ds(pl.multiple_of((1 - core) * HALF, HALF), HALF)
    for g in range(D // 128):
        wg_ref[rows_of, g * 128 : g * 128 + 128] = wfin[
            1 - core, g * HALF : (g + 1) * HALF
        ].astype(F32)

    for t in range(2):
        c = first(t)
        c[0].wait_send()
        c[3].wait_send()
        d = second(t)
        for x in (c[1], d[0], d[2]):
            pl.when(has_up)(x.wait_send)
        for x in (c[2], d[1], d[3]):
            pl.when(has_down)(x.wait_send)
        to_mate(t).wait_send()
        to_beyond(t).wait_send()
        for way in range(2):
            for which in range(2):
                pl.when(conds[way])(to_lat(t, way, which).wait_send)
    send_u.wait_send()
    send_att.wait_send()
    for o in range(OWNERS):
        pl.when(z != owner_z(o))(z_copy(o).wait_send)

        @pl.when(z == owner_z(o))
        def _():
            for k in range(1, DEPTH):
                z_gather(o, k).wait_send()

    @pl.loop(1, GROUP)
    def _(k):
        reduce_copy(k).wait_send()
        gather_copy(k).wait_send()

    @pl.loop(0, GROUP)
    def _(k):
        pass_on(k, core).wait_send()


def on_device(queries, key_vectors, value_vectors, upstream, w_out, neighbours, counts):
    shape = queries.shape
    vmem = pl.BlockSpec(memory_space=pltpu.VMEM)
    smem = pl.BlockSpec(memory_space=pltpu.SMEM)
    blocks = jax.ShapeDtypeStruct((2, TOK, D), BF16)
    dma = pltpu.SemaphoreType.DMA
    mixed, dq, dk, dv, wg = pl.pallas_call(
        kernel,
        out_shape=(
            jax.ShapeDtypeStruct((2 * TOK, D), BF16),
            blocks,
            blocks,
            blocks,
            jax.ShapeDtypeStruct((D, D), F32),
        ),
        in_specs=[vmem] * 5 + [smem] * 2,
        out_specs=(vmem,) * 5,
        scratch_shapes=[
            pltpu.VMEM((2, 3, 4, TOK, D), BF16),
            pltpu.VMEM((256, D), BF16),
            pltpu.VMEM((128, D), BF16),
            pltpu.VMEM((2, PAIRS, 128, 256), F32),
            pltpu.VMEM((2, 128, HALF), BF16),
            pltpu.VMEM((128, HALF), BF16),
            pltpu.VMEM((HALF, 256), BF16),
            pltpu.VMEM((2, 2, SLOTS + 1, TOK, D), F32),
            pltpu.VMEM((2, 4, TOK, D), BF16),
            pltpu.VMEM((2, 4, TOK, D), BF16),
            pltpu.VMEM((2, 2, 2, TOK, D), BF16),
            pltpu.VMEM((2, 2, 2, TOK, D), BF16),
            pltpu.VMEM((2, 2, TOK, D), BF16),
            pltpu.VMEM((2, 2, TOK, D), BF16),
            pltpu.VMEM((FLAT, 128), BF16),
            pltpu.VMEM((GROUP, CHUNK, 128), BF16),
            pltpu.VMEM((CHUNK, 128), BF16),
            pltpu.VMEM((DEPTH, PIECE, 128), BF16),
            pltpu.VMEM((CHUNK, 128), BF16),
            pltpu.VMEM((2, FLAT, 128), BF16),
            dma((2, 8)),
            dma((2, 8)),
            dma((2,)),
            dma((2,)),
            dma((2,)),
            dma((2,)),
            dma((2, 2, 2)),
            dma((2, 2, 2)),
            dma((2,)),
            dma((2,)),
            dma((GROUP,)),
            dma((GROUP,)),
            dma((OWNERS,)),
            dma((DEPTH,)),
            dma((DEPTH,)),
            dma((OWNERS,)),
            dma((GROUP,)),
            dma((GROUP,)),
            dma((GROUP,)),
            dma((GROUP,)),
        ],
        compiler_params=pltpu.CompilerParams(
            collective_id=0, has_side_effects=True, vmem_limit_bytes=48 * 2**20
        ),
    )(
        queries.reshape(2, TOK, D),
        key_vectors.reshape(2, TOK, D),
        value_vectors.reshape(2, TOK, D),
        upstream.reshape(2 * TOK, D),
        w_out,
        neighbours,
        counts,
    )
    return (mixed.reshape(shape), dq.reshape(shape), dk.reshape(shape), dv.reshape(shape), wg)


def solution(mesh):
    grid = P("lat", "lon", None)
    return jax.shard_map(
        on_device,
        mesh=mesh,
        in_specs=(grid, grid, grid, grid, P(), P(), P()),
        out_specs=(grid, grid, grid, grid, P()),
        check_vma=False,
    )
```

```python
import math

import jax
import jax.numpy as jnp
from jax import lax
from jax.experimental import pallas as pl
from jax.experimental.pallas import tpu as pltpu
from jax.sharding import PartitionSpec as P

F32 = jnp.float32
BF16 = jnp.bfloat16
MESH = pl.DeviceIdType.MESH

HEAD_DIM = 64
SLOTS = 4
TOK = 64
D = 768
PAIRS = 6
NLON = 32
NLAT = 8
TOKENS = 32768
HALF = D // 2
GROUP = 16
FLAT = HALF * (D // 128)
CHUNK = FLAT // GROUP
OWNERS = 3
PIECE = CHUNK // OWNERS
DEPTH = 8
VMEM = 58 * 2**20
NT = (((1,), (1,)), ((), ()))
TN = (((0,), (0,)), ((), ()))


def remote(src, dst, send_sem, recv_sem, device):
    return pltpu.make_async_remote_copy(
        src_ref=src,
        dst_ref=dst,
        send_sem=send_sem,
        recv_sem=recv_sem,
        device_id=device,
        device_id_type=MESH,
    )


def kernel(
    q_hbm,
    k_hbm,
    v_hbm,
    u_hbm,
    w_hbm,
    nb_hbm,
    ct_hbm,
    mixed_hbm,
    dq_hbm,
    dk_hbm,
    dv_hbm,
    wfin_hbm,
    mixed_ref,
    dq_ref,
    dk_ref,
    dv_ref,
    wfin,
    q_ref,
    w_ref,
    nb_ref,
    ct_ref,
    kvb,
    ucat,
    datt,
    probs,
    att2,
    att_in,
    att_t,
    cb,
    gsp,
    grp,
    gsl,
    grl,
    gso,
    gro,
    wbuf,
    rsin,
    zsum,
    zin,
    wch,
    in_s,
    out_s,
    halo_s,
    halo_r,
    u_s,
    u_r,
    gp_s,
    gp_r,
    gl_s,
    gl_r,
    go_s,
    go_r,
    rs_s,
    rs_r,
    z_s,
    z_r,
    zg_s,
    zg_r,
    ag_s,
    ag_r,
    fw_s,
    fw_r,
):
    a = lax.axis_index("lat")
    b = lax.axis_index("lon")
    core = lax.rem(b, 2)
    ylo = lax.rem(b // 2, 2)
    z = b // 4
    has_up = a > 0
    has_down = a < NLAT - 1
    mate = (a, b + 1 - 2 * core)
    beyond = (a, lax.rem(b + NLON - 1 + 2 * core, NLON))
    up = (a - 1, b)
    down = (a + 1, b)
    oc = 2 * core
    ic = 2 - oc
    n = a * 2 + ylo

    def peer(k):
        m = lax.rem(n + k, GROUP)
        return (m // 2, z * 4 + lax.rem(m, 2) * 2 + core), m

    def zpeer(zz):
        return (a, zz * 4 + ylo * 2 + core)

    barrier = pltpu.get_barrier_semaphore()

    def greet(device):
        pl.semaphore_signal(barrier, inc=1, device_id=device, device_id_type=MESH)

    greet(mate)
    greet(beyond)

    @pl.loop(1, GROUP)
    def _(k):
        greet(peer(k)[0])

    @pl.loop(1, DEPTH)
    def _(k):
        greet(zpeer(lax.rem(z + k, DEPTH)))

    own_u = ucat.at[pl.ds(0, 128)]
    loads = [
        pltpu.make_async_copy(src, dst, in_s.at[i])
        for i, (src, dst) in enumerate(
            (
                (u_hbm, own_u),
                (w_hbm, w_ref),
                (k_hbm, kvb.at[0, 1, pl.ds(1, 2)]),
                (v_hbm, kvb.at[1, 1, pl.ds(1, 2)]),
                (q_hbm, q_ref),
                (nb_hbm, nb_ref),
                (ct_hbm, ct_ref),
            )
        )
    ]
    for load in loads:
        load.start()
    pl.semaphore_wait(barrier, 2 + GROUP - 1 + DEPTH - 1)

    stores = [
        pltpu.make_async_copy(src, dst, out_s.at[i])
        for i, (src, dst) in enumerate(
            (
                (mixed_ref, mixed_hbm),
                (dq_ref, dq_hbm),
                (dk_ref, dk_hbm),
                (dv_ref, dv_hbm),
                (wfin, wfin_hbm),
            )
        )
    ]

    def halo(t, i, src, dst, device):
        return remote(src, dst, halo_s.at[t, i], halo_r.at[t, i], device)

    ins = (k_hbm, v_hbm)

    def first(t):
        src = ins[t]
        return (
            halo(t, 1, src, kvb.at[t, ic, pl.ds(1, 2)], beyond),
            halo(t, 2, src.at[0], kvb.at[t, 1, 3], up),
            halo(t, 3, src.at[1], kvb.at[t, 1, 0], down),
            halo(t, 0, src, kvb.at[t, oc, pl.ds(1, 2)], mate),
        )

    def second(t):
        return (
            halo(t, 4, kvb.at[t, oc, 1], kvb.at[t, oc, 3], up),
            halo(t, 5, kvb.at[t, oc, 2], kvb.at[t, oc, 0], down),
            halo(t, 6, kvb.at[t, 1, 0], kvb.at[t, oc, 0], mate),
            halo(t, 7, kvb.at[t, 1, 3], kvb.at[t, oc, 3], mate),
        )

    for t in range(2):
        c = first(t)
        c[0].start()
        pl.when(has_up)(c[1].start)
        pl.when(has_down)(c[2].start)
        c[3].start()
    send_u = remote(u_hbm, ucat.at[pl.ds(128, 128)], u_s.at[0], u_r.at[0], mate)
    send_u.start()

    loads[0].wait()
    loads[1].wait()
    datt[...] = lax.dot_general(
        own_u[...], w_ref[...], NT, preferred_element_type=F32
    ).astype(BF16)
    for t in range(2):
        for s in range(2):
            cb[t, s, SLOTS] = jnp.zeros((TOK, D), F32)

    for load in loads[2:]:
        load.wait()
    for t in range(2):
        c = second(t)
        halo(t, 1, k_hbm, kvb.at[t, oc, pl.ds(1, 2)], beyond).wait_recv()
        pl.when(has_up)(c[0].start)
        pl.when(has_down)(c[1].start)

        @pl.when(has_up)
        def _():
            halo(t, 3, k_hbm.at[0], kvb.at[t, 1, 0], up).wait_recv()
            c[2].start()

        @pl.when(has_down)
        def _():
            halo(t, 2, k_hbm.at[0], kvb.at[t, 1, 3], down).wait_recv()
            c[3].start()

    for t in range(2):
        halo(t, 0, k_hbm, kvb.at[t, ic, pl.ds(1, 2)], mate).wait_recv()

        @pl.when(has_up)
        def _():
            halo(t, 5, k_hbm.at[0], kvb.at[t, oc, 0], up).wait_recv()
            halo(t, 6, k_hbm.at[0], kvb.at[t, ic, 0], mate).wait_recv()

        @pl.when(has_down)
        def _():
            halo(t, 4, k_hbm.at[0], kvb.at[t, oc, 3], down).wait_recv()
            halo(t, 7, k_hbm.at[0], kvb.at[t, ic, 3], mate).wait_recv()

    def places(s_block):
        i = 2 * a + s_block
        out = []
        for s in range(SLOTS):
            name = nb_ref[i, s, b]
            row = lax.div(name, NLON) - i + 1
            col = lax.rem(lax.rem(name, NLON) - b + 1 + NLON, NLON)
            out.append((jnp.clip(col, 0, 2), jnp.clip(row, 0, 2)))
        return out, ct_ref[i, b]

    def blocks_of(t, place, s_block, j):
        return jnp.concatenate(
            [kvb[t, col, row + s_block, :, pl.ds(j * 128, 128)] for col, row in place], axis=0
        )

    low = lax.broadcasted_iota(jnp.int32, (TOK, 128), 1) < HEAD_DIM

    def stacked(x):
        zero = jnp.zeros_like(x)
        return jnp.concatenate([jnp.where(low, x, zero), jnp.where(low, zero, x)], axis=0)

    def queries_of(s_block, j):
        x = q_ref[s_block, :, pl.ds(j * 128, 128)]
        return stacked(x * jnp.asarray(0.125, BF16))

    def unstacked(x):
        return jnp.where(low, x[:TOK], x[TOK:])

    @pl.loop(0, 2)
    def _(s):
        place, count = places(s)
        kept = lax.broadcasted_iota(jnp.int32, (2 * TOK, SLOTS * TOK), 1) < count * TOK
        rows = pl.ds(pl.multiple_of(s * TOK, TOK), TOK)
        scores = []
        for j in range(PAIRS):
            scores.append(
                lax.dot_general(
                    queries_of(s, j), blocks_of(0, place, s, j), NT, preferred_element_type=F32
                )
            )
        for j in range(PAIRS):
            masked = jnp.where(kept, scores[j], -1e30)
            top = jnp.max(masked, axis=-1, keepdims=True)
            e = jnp.exp(masked - top)
            probs[s, j] = e * (1.0 / jnp.sum(e, axis=-1, keepdims=True))
        for j in range(PAIRS):
            o = jnp.dot(
                probs[s, j].astype(BF16), blocks_of(1, place, s, j), preferred_element_type=F32
            )
            att2[j // 3, rows, (j % 3) * 128 : (j % 3) * 128 + 128] = unstacked(o).astype(BF16)

    send_att = remote(att2.at[1 - core], att_in, u_s.at[1], u_r.at[1], mate)
    send_att.start()
    att_t[:, 0:128] = att2[core].T
    att = jnp.concatenate([att2[0], att2[1]], axis=1)
    mixed_ref[...] = jnp.dot(att, w_ref[...], preferred_element_type=F32).astype(BF16)
    stores[0].start()
    remote(u_hbm, ucat.at[pl.ds(128, 128)], u_s.at[0], u_r.at[0], mate).wait_recv()
    send_att.wait_recv()
    att_t[:, 128:256] = att_in[...].T
    for g in range(3):
        term = jnp.dot(
            att_t[...], ucat[:, g * 256 : g * 256 + 256], preferred_element_type=F32
        ).astype(BF16)
        wbuf[2 * g * HALF : (2 * g + 1) * HALF] = term[:, :128]
        wbuf[(2 * g + 1) * HALF : (2 * g + 2) * HALF] = term[:, 128:]

    def chunk(m):
        return pl.ds(pl.multiple_of(m * CHUNK, 16), CHUNK)

    def reduce_copy(k):
        device, m = peer(k)
        return remote(wbuf.at[chunk(m)], rsin.at[k], rs_s.at[k], rs_r.at[k], device)

    @pl.loop(1, GROUP)
    def _(k):
        reduce_copy(k).start()

    @pl.loop(0, 2)
    def _(s):
        place, _ = places(s)
        rows = pl.ds(pl.multiple_of(s * TOK, TOK), TOK)
        for j in range(PAIRS):
            lanes = pl.ds(j * 128, 128)
            qs = queries_of(s, j)
            ks = blocks_of(0, place, s, j)
            vs = blocks_of(1, place, s, j)
            da = stacked(datt[rows, lanes])
            at = att2[j // 3, rows, (j % 3) * 128 : (j % 3) * 128 + 128]
            at = jnp.concatenate([at, at], axis=0)
            delta = jnp.sum(da.astype(F32) * at.astype(F32), axis=-1, keepdims=True)
            p = probs[s, j]
            dp = lax.dot_general(da, vs, NT, preferred_element_type=F32)
            ds = (p * (dp - delta)).astype(BF16)
            dq = unstacked(jnp.dot(ds, ks, preferred_element_type=F32)) * 0.125
            dq_ref[s, :, lanes] = dq.astype(BF16)
            dk = lax.dot_general(ds, qs, TN, preferred_element_type=F32)
            dv = lax.dot_general(p.astype(BF16), da, TN, preferred_element_type=F32)
            for i in range(SLOTS):
                cb[0, s, i, :, lanes] = dk[i * TOK : (i + 1) * TOK]
                cb[1, s, i, :, lanes] = dv[i * TOK : (i + 1) * TOK]

    stores[1].start()
    placed = [places(s) for s in range(2)]

    def slot_of(s, row, col):
        slot = jnp.int32(SLOTS)
        place, count = placed[s]
        for i in range(SLOTS):
            hit = (place[i][0] == col) & (place[i][1] == row) & (i < count)
            slot = jnp.where(hit, i, slot)
        return slot

    def terms(t, col, row):
        total = None
        for s in range(2):
            if 0 <= row - s <= 2:
                x = cb[t, s, slot_of(s, row - s, col)]
                total = x if total is None else total + x
        return total

    def to_mate(t):
        return remote(gsp.at[t], grp.at[t], gp_s.at[t], gp_r.at[t], mate)

    def to_lat(t, way, which):
        device = (up, down)[way]
        return remote(
            gsl.at[t, way, which],
            grl.at[t, way, which],
            gl_s.at[t, way, which],
            gl_r.at[t, way, which],
            device,
        )

    def to_beyond(t):
        return remote(gso.at[t], gro.at[t], go_s.at[t], go_r.at[t], beyond)

    conds = (has_up, has_down)
    from_conds = (has_down, has_up)
    for t in range(2):
        for r in range(4):
            gsp[t, r] = terms(t, ic, r).astype(BF16)
        to_mate(t).start()
        for way in range(2):

            @pl.when(conds[way])
            def _():
                gsl[t, way, 0] = terms(t, oc, 3 * way).astype(BF16)
                to_lat(t, way, 0).start()

    total = wbuf[chunk(n), :].astype(F32)
    for k in range(1, GROUP):
        reduce_copy(k).wait_recv()
        total = total + rsin[k].astype(F32)
    zsum[...] = total.astype(BF16)

    def owner_z(o):
        return 3 * o

    def z_copy(o):
        k = lax.rem(owner_z(o) - z + DEPTH, DEPTH)
        return remote(
            zsum.at[pl.ds(o * PIECE, PIECE)], zin.at[k], z_s.at[o], z_r.at[k], zpeer(owner_z(o))
        )

    for o in range(OWNERS):
        pl.when(z != owner_z(o))(z_copy(o).start)

    for t in range(2):
        to_mate(t).wait_recv()
        for way in range(2):

            @pl.when(conds[way])
            def _():
                x = terms(t, 1, 3 * way) + grp[t, 3 * way].astype(F32)
                gsl[t, way, 1] = x.astype(BF16)
                to_lat(t, way, 1).start()

    def z_gather(o, k):
        return remote(
            wch.at[pl.ds(o * PIECE, PIECE)],
            wch.at[pl.ds(o * PIECE, PIECE)],
            zg_s.at[k],
            zg_r.at[o],
            zpeer(lax.rem(owner_z(o) + k, DEPTH)),
        )

    for o in range(OWNERS):

        @pl.when(z == owner_z(o))
        def _():
            acc = zsum[o * PIECE : (o + 1) * PIECE].astype(F32)
            for k in range(1, DEPTH):
                remote(
                    zsum.at[pl.ds(o * PIECE, PIECE)],
                    zin.at[k],
                    z_s.at[o],
                    z_r.at[k],
                    zpeer(lax.rem(z + DEPTH - k, DEPTH)),
                ).wait_recv()
                acc = acc + zin[k].astype(F32)
            wch[o * PIECE : (o + 1) * PIECE] = (acc * (1.0 / math.sqrt(TOKENS))).astype(BF16)
            for k in range(1, DEPTH):
                z_gather(o, k).start()

    for t in range(2):
        for r in range(2):
            x = terms(t, oc, 1 + r)
            gso[t, r] = x.astype(BF16)
        for way in range(2):

            @pl.when(from_conds[way])
            def _():
                to_lat(t, way, 0).wait_recv()
                r = 1 - way
                x = terms(t, oc, 1 + r) + grl[t, way, 0].astype(F32)
                gso[t, r] = x.astype(BF16)

        to_beyond(t).start()

    for o in range(OWNERS):
        pl.when(z != owner_z(o))(z_gather(o, 1).wait_recv)

    def gather_copy(k):
        device, _ = peer(k)
        return remote(wch, wfin.at[core, chunk(n)], ag_s.at[k], ag_r.at[k], device)

    @pl.loop(1, GROUP)
    def _(k):
        gather_copy(k).start()

    wfin[core, chunk(n), :] = wch[...]

    def pass_on(k, half):
        m = lax.rem(n + GROUP - k, GROUP)
        return remote(
            wfin.at[half, chunk(m)], wfin.at[half, chunk(m)], fw_s.at[k], fw_r.at[k], mate
        )

    pass_on(0, core).start()

    outs = (dk_ref, dv_ref)
    for t in range(2):
        to_beyond(t).wait_recv()
        for r in range(2):
            x = terms(t, 1, 1 + r) + grp[t, 1 + r].astype(F32) + gro[t, r].astype(F32)
            outs[t][r] = x.astype(BF16)
        for way in range(2):

            @pl.when(from_conds[way])
            def _():
                to_lat(t, way, 1).wait_recv()
                r = 1 - way
                x = terms(t, 1, 1 + r) + grp[t, 1 + r].astype(F32) + gro[t, r].astype(F32)
                outs[t][r] = (x + grl[t, way, 1].astype(F32)).astype(BF16)

        stores[2 + t].start()

    @pl.loop(1, GROUP)
    def _(k):
        m = lax.rem(n + GROUP - k, GROUP)
        device = (m // 2, z * 4 + lax.rem(m, 2) * 2 + core)
        remote(wch, wfin.at[core, chunk(m)], ag_s.at[k], ag_r.at[k], device).wait_recv()
        pass_on(k, core).start()

    @pl.loop(0, GROUP)
    def _(k):
        pass_on(k, 1 - core).wait_recv()

    stores[4].start()

    for t in range(2):
        c = first(t)
        c[0].wait_send()
        c[3].wait_send()
        d = second(t)
        for x in (c[1], d[0], d[2]):
            pl.when(has_up)(x.wait_send)
        for x in (c[2], d[1], d[3]):
            pl.when(has_down)(x.wait_send)
        to_mate(t).wait_send()
        to_beyond(t).wait_send()
        for way in range(2):
            for which in range(2):
                pl.when(conds[way])(to_lat(t, way, which).wait_send)
    send_u.wait_send()
    send_att.wait_send()
    for o in range(OWNERS):
        pl.when(z != owner_z(o))(z_copy(o).wait_send)

        @pl.when(z == owner_z(o))
        def _():
            for k in range(1, DEPTH):
                z_gather(o, k).wait_send()

    @pl.loop(1, GROUP)
    def _(k):
        reduce_copy(k).wait_send()
        gather_copy(k).wait_send()

    @pl.loop(0, GROUP)
    def _(k):
        pass_on(k, core).wait_send()

    for store in stores:
        store.wait()


def finish(mixed, dq, dk, dv, wfin, mixed_out, dq_out, dk_out, dv_out, wg_out, narrow, wide, sems):
    large = [pltpu.make_async_copy(wfin.at[h], narrow.at[h], sems.at[h]) for h in range(2)]
    small = [
        pltpu.make_async_copy(src, dst, sems.at[2 + i])
        for i, (src, dst) in enumerate(
            ((mixed, mixed_out), (dq, dq_out), (dk, dk_out), (dv, dv_out))
        )
    ]
    for copy in large + small:
        copy.start()
    for h in range(2):
        rows = pl.ds(h * HALF, HALF)
        large[h].wait()
        for g in range(D // 128):
            wide[rows, g * 128 : g * 128 + 128] = narrow[h, g * HALF : (g + 1) * HALF].astype(F32)
        large.append(pltpu.make_async_copy(wide.at[rows], wg_out.at[rows], sems.at[6 + h]))
        large[2 + h].start()
    for copy in small + large[2:]:
        copy.wait()


def on_device(queries, key_vectors, value_vectors, upstream, w_out, neighbours, counts):
    shape = queries.shape
    hbm = pl.BlockSpec(memory_space=pltpu.HBM)
    blocks = jax.ShapeDtypeStruct((2, TOK, D), BF16)
    dma = pltpu.SemaphoreType.DMA
    results = pl.pallas_call(
        kernel,
        out_shape=(
            jax.ShapeDtypeStruct((2 * TOK, D), BF16),
            blocks,
            blocks,
            blocks,
            jax.ShapeDtypeStruct((2, FLAT, 128), BF16),
        ),
        in_specs=[hbm] * 7,
        out_specs=(hbm,) * 5,
        scratch_shapes=[
            pltpu.VMEM((2 * TOK, D), BF16),
            pltpu.VMEM((2, TOK, D), BF16),
            pltpu.VMEM((2, TOK, D), BF16),
            pltpu.VMEM((2, TOK, D), BF16),
            pltpu.VMEM((2, FLAT, 128), BF16),
            pltpu.VMEM((2, TOK, D), BF16),
            pltpu.VMEM((D, D), BF16),
            pltpu.SMEM((16, SLOTS, NLON), jnp.int32),
            pltpu.SMEM((16, NLON), jnp.int32),
            pltpu.VMEM((2, 3, 4, TOK, D), BF16),
            pltpu.VMEM((256, D), BF16),
            pltpu.VMEM((128, D), BF16),
            pltpu.VMEM((2, PAIRS, 128, 256), F32),
            pltpu.VMEM((2, 128, HALF), BF16),
            pltpu.VMEM((128, HALF), BF16),
            pltpu.VMEM((HALF, 256), BF16),
            pltpu.VMEM((2, 2, SLOTS + 1, TOK, D), F32),
            pltpu.VMEM((2, 4, TOK, D), BF16),
            pltpu.VMEM((2, 4, TOK, D), BF16),
            pltpu.VMEM((2, 2, 2, TOK, D), BF16),
            pltpu.VMEM((2, 2, 2, TOK, D), BF16),
            pltpu.VMEM((2, 2, TOK, D), BF16),
            pltpu.VMEM((2, 2, TOK, D), BF16),
            pltpu.VMEM((FLAT, 128), BF16),
            pltpu.VMEM((GROUP, CHUNK, 128), BF16),
            pltpu.VMEM((CHUNK, 128), BF16),
            pltpu.VMEM((DEPTH, PIECE, 128), BF16),
            pltpu.VMEM((CHUNK, 128), BF16),
            dma((7,)),
            dma((5,)),
            dma((2, 8)),
            dma((2, 8)),
            dma((2,)),
            dma((2,)),
            dma((2,)),
            dma((2,)),
            dma((2, 2, 2)),
            dma((2, 2, 2)),
            dma((2,)),
            dma((2,)),
            dma((GROUP,)),
            dma((GROUP,)),
            dma((OWNERS,)),
            dma((DEPTH,)),
            dma((DEPTH,)),
            dma((OWNERS,)),
            dma((GROUP,)),
            dma((GROUP,)),
            dma((GROUP,)),
            dma((GROUP,)),
        ],
        compiler_params=pltpu.CompilerParams(
            collective_id=0, has_side_effects=True, vmem_limit_bytes=VMEM
        ),
    )(
        queries.reshape(2, TOK, D),
        key_vectors.reshape(2, TOK, D),
        value_vectors.reshape(2, TOK, D),
        upstream.reshape(2 * TOK, D),
        w_out,
        neighbours.transpose(0, 2, 1),
        counts,
    )
    mixed, dq, dk, dv, wg = pl.pallas_call(
        finish,
        out_shape=(
            jax.ShapeDtypeStruct((2 * TOK, D), BF16),
            blocks,
            blocks,
            blocks,
            jax.ShapeDtypeStruct((D, D), F32),
        ),
        in_specs=[hbm] * 5,
        out_specs=(hbm,) * 5,
        scratch_shapes=[
            pltpu.VMEM((2, FLAT, 128), BF16),
            pltpu.VMEM((D, D), F32),
            dma((8,)),
        ],
        compiler_params=pltpu.CompilerParams(vmem_limit_bytes=VMEM),
    )(*results)
    return (mixed.reshape(shape), dq.reshape(shape), dk.reshape(shape), dv.reshape(shape), wg)


def solution(mesh):
    grid = P("lat", "lon", None)
    return jax.shard_map(
        on_device,
        mesh=mesh,
        in_specs=(grid, grid, grid, grid, P(), P(), P()),
        out_specs=(grid, grid, grid, grid, P()),
        check_vma=False,
    )
```

```python
import math

import jax
import jax.numpy as jnp
from jax import lax
from jax.experimental import pallas as pl
from jax.experimental.pallas import tpu as pltpu
from jax.sharding import PartitionSpec as P

F32 = jnp.float32
BF16 = jnp.bfloat16
MESH = pl.DeviceIdType.MESH

HEAD_DIM = 64
SLOTS = 4
TOK = 64
D = 768
PAIRS = 6
NLON = 32
NLAT = 8
TOKENS = 32768
HALF = D // 2
GROUP = 16
FLAT = HALF * (D // 128)
CHUNK = FLAT // GROUP
OWNERS = 3
PIECE = CHUNK // OWNERS
DEPTH = 8
VMEM = 58 * 2**20
NT = (((1,), (1,)), ((), ()))
TN = (((0,), (0,)), ((), ()))


def remote(src, dst, send_sem, recv_sem, device):
    return pltpu.make_async_remote_copy(
        src_ref=src,
        dst_ref=dst,
        send_sem=send_sem,
        recv_sem=recv_sem,
        device_id=device,
        device_id_type=MESH,
    )


def kernel(
    q_hbm,
    k_hbm,
    v_hbm,
    u_hbm,
    w_hbm,
    nb_hbm,
    ct_hbm,
    mixed_hbm,
    dq_hbm,
    dk_hbm,
    dv_hbm,
    wfin_hbm,
    mixed_ref,
    dq_ref,
    dk_ref,
    dv_ref,
    wfin,
    q_ref,
    w_ref,
    nb_ref,
    ct_ref,
    kvb,
    ucat,
    datt,
    probs,
    att2,
    att_in,
    att_t,
    cb,
    gsp,
    grp,
    gsl,
    grl,
    gso,
    gro,
    wbuf,
    rsin,
    zsum,
    zin,
    wch,
    in_s,
    out_s,
    halo_s,
    halo_r,
    u_s,
    u_r,
    gp_s,
    gp_r,
    gl_s,
    gl_r,
    go_s,
    go_r,
    rs_s,
    rs_r,
    z_s,
    z_r,
    zg_s,
    zg_r,
    ag_s,
    ag_r,
    fw_s,
    fw_r,
):
    a = lax.axis_index("lat")
    b = lax.axis_index("lon")
    core = lax.rem(b, 2)
    ylo = lax.rem(b // 2, 2)
    z = b // 4
    has_up = a > 0
    has_down = a < NLAT - 1
    mate = (a, b + 1 - 2 * core)
    beyond = (a, lax.rem(b + NLON - 1 + 2 * core, NLON))
    up = (a - 1, b)
    down = (a + 1, b)
    oc = 2 * core
    ic = 2 - oc
    n = a * 2 + ylo

    def peer(k):
        m = lax.rem(n + k, GROUP)
        return (m // 2, z * 4 + lax.rem(m, 2) * 2 + core), m

    def zpeer(zz):
        return (a, zz * 4 + ylo * 2 + core)

    barrier = pltpu.get_barrier_semaphore()

    def greet(device):
        pl.semaphore_signal(barrier, inc=1, device_id=device, device_id_type=MESH)

    greet(mate)
    greet(beyond)

    @pl.loop(1, GROUP)
    def _(k):
        greet(peer(k)[0])

    @pl.loop(1, DEPTH)
    def _(k):
        greet(zpeer(lax.rem(z + k, DEPTH)))

    own_u = ucat.at[pl.ds(0, 128)]
    loads = [
        pltpu.make_async_copy(src, dst, in_s.at[i])
        for i, (src, dst) in enumerate(
            (
                (u_hbm, own_u),
                (w_hbm, w_ref),
                (k_hbm, kvb.at[0, 1, pl.ds(1, 2)]),
                (v_hbm, kvb.at[1, 1, pl.ds(1, 2)]),
                (q_hbm, q_ref),
                (nb_hbm, nb_ref),
                (ct_hbm, ct_ref),
            )
        )
    ]
    for load in loads:
        load.start()
    pl.semaphore_wait(barrier, 2 + GROUP - 1 + DEPTH - 1)

    stores = [
        pltpu.make_async_copy(src, dst, out_s.at[i])
        for i, (src, dst) in enumerate(
            (
                (mixed_ref, mixed_hbm),
                (dq_ref, dq_hbm),
                (dk_ref, dk_hbm),
                (dv_ref, dv_hbm),
                (wfin, wfin_hbm),
            )
        )
    ]

    def halo(t, i, src, dst, device):
        return remote(src, dst, halo_s.at[t, i], halo_r.at[t, i], device)

    ins = (k_hbm, v_hbm)

    def first(t):
        src = ins[t]
        return (
            halo(t, 1, src, kvb.at[t, ic, pl.ds(1, 2)], beyond),
            halo(t, 2, src.at[0], kvb.at[t, 1, 3], up),
            halo(t, 3, src.at[1], kvb.at[t, 1, 0], down),
            halo(t, 0, src, kvb.at[t, oc, pl.ds(1, 2)], mate),
        )

    def second(t):
        return (
            halo(t, 4, kvb.at[t, oc, 1], kvb.at[t, oc, 3], up),
            halo(t, 5, kvb.at[t, oc, 2], kvb.at[t, oc, 0], down),
            halo(t, 6, kvb.at[t, 1, 0], kvb.at[t, oc, 0], mate),
            halo(t, 7, kvb.at[t, 1, 3], kvb.at[t, oc, 3], mate),
        )

    for t in range(2):
        c = first(t)
        c[0].start()
        pl.when(has_up)(c[1].start)
        pl.when(has_down)(c[2].start)
        c[3].start()
    send_u = remote(u_hbm, ucat.at[pl.ds(128, 128)], u_s.at[0], u_r.at[0], mate)
    send_u.start()

    loads[0].wait()
    loads[1].wait()
    datt[...] = lax.dot_general(
        own_u[...], w_ref[...], NT, preferred_element_type=F32
    ).astype(BF16)
    for t in range(2):
        for s in range(2):
            cb[t, s, SLOTS] = jnp.zeros((TOK, D), F32)

    for load in loads[2:]:
        load.wait()
    for t in range(2):
        c = second(t)
        halo(t, 1, k_hbm, kvb.at[t, oc, pl.ds(1, 2)], beyond).wait_recv()
        pl.when(has_up)(c[0].start)
        pl.when(has_down)(c[1].start)

        @pl.when(has_up)
        def _():
            halo(t, 3, k_hbm.at[0], kvb.at[t, 1, 0], up).wait_recv()
            c[2].start()

        @pl.when(has_down)
        def _():
            halo(t, 2, k_hbm.at[0], kvb.at[t, 1, 3], down).wait_recv()
            c[3].start()

    for t in range(2):
        halo(t, 0, k_hbm, kvb.at[t, ic, pl.ds(1, 2)], mate).wait_recv()

        @pl.when(has_up)
        def _():
            halo(t, 5, k_hbm.at[0], kvb.at[t, oc, 0], up).wait_recv()
            halo(t, 6, k_hbm.at[0], kvb.at[t, ic, 0], mate).wait_recv()

        @pl.when(has_down)
        def _():
            halo(t, 4, k_hbm.at[0], kvb.at[t, oc, 3], down).wait_recv()
            halo(t, 7, k_hbm.at[0], kvb.at[t, ic, 3], mate).wait_recv()

    def places(s_block):
        i = 2 * a + s_block
        out = []
        for s in range(SLOTS):
            name = nb_ref[i, s, b]
            row = lax.div(name, NLON) - i + 1
            col = lax.rem(lax.rem(name, NLON) - b + 1 + NLON, NLON)
            out.append((jnp.clip(col, 0, 2), jnp.clip(row, 0, 2)))
        return out, ct_ref[i, b]

    def blocks_of(t, place, s_block, j):
        return jnp.concatenate(
            [kvb[t, col, row + s_block, :, pl.ds(j * 128, 128)] for col, row in place], axis=0
        )

    low = lax.broadcasted_iota(jnp.int32, (TOK, 128), 1) < HEAD_DIM

    def stacked(x):
        zero = jnp.zeros_like(x)
        return jnp.concatenate([jnp.where(low, x, zero), jnp.where(low, zero, x)], axis=0)

    def queries_of(s_block, j):
        x = q_ref[s_block, :, pl.ds(j * 128, 128)]
        return stacked(x * jnp.asarray(0.125, BF16))

    def unstacked(x):
        return jnp.where(low, x[:TOK], x[TOK:])

    @pl.loop(0, 2)
    def _(s):
        place, count = places(s)
        kept = lax.broadcasted_iota(jnp.int32, (2 * TOK, SLOTS * TOK), 1) < count * TOK
        rows = pl.ds(pl.multiple_of(s * TOK, TOK), TOK)
        scores = []
        for j in range(PAIRS):
            scores.append(
                lax.dot_general(
                    queries_of(s, j), blocks_of(0, place, s, j), NT, preferred_element_type=F32
                )
            )
        for j in range(PAIRS):
            masked = jnp.where(kept, scores[j], -1e30)
            top = jnp.max(masked, axis=-1, keepdims=True)
            e = jnp.exp(masked - top)
            probs[s, j] = e * (1.0 / jnp.sum(e, axis=-1, keepdims=True))
        for j in range(PAIRS):
            o = jnp.dot(
                probs[s, j].astype(BF16), blocks_of(1, place, s, j), preferred_element_type=F32
            )
            att2[j // 3, rows, (j % 3) * 128 : (j % 3) * 128 + 128] = unstacked(o).astype(BF16)

    send_att = remote(att2.at[1 - core], att_in, u_s.at[1], u_r.at[1], mate)
    send_att.start()
    att_t[:, 0:128] = att2[core].T
    att = jnp.concatenate([att2[0], att2[1]], axis=1)
    mixed = jnp.dot(att, w_ref[...], preferred_element_type=F32).astype(BF16)
    mixed_ref[0] = mixed[:TOK]
    mixed_ref[1] = mixed[TOK:]
    stores[0].start()
    remote(u_hbm, ucat.at[pl.ds(128, 128)], u_s.at[0], u_r.at[0], mate).wait_recv()
    send_att.wait_recv()
    att_t[:, 128:256] = att_in[...].T
    for g in range(3):
        term = jnp.dot(
            att_t[...], ucat[:, g * 256 : g * 256 + 256], preferred_element_type=F32
        ).astype(BF16)
        wbuf[2 * g * HALF : (2 * g + 1) * HALF] = term[:, :128]
        wbuf[(2 * g + 1) * HALF : (2 * g + 2) * HALF] = term[:, 128:]

    def chunk(m):
        return pl.ds(pl.multiple_of(m * CHUNK, 16), CHUNK)

    def reduce_copy(k):
        device, m = peer(k)
        return remote(wbuf.at[chunk(m)], rsin.at[k], rs_s.at[k], rs_r.at[k], device)

    @pl.loop(1, GROUP)
    def _(k):
        reduce_copy(k).start()

    @pl.loop(0, 2)
    def _(s):
        place, _ = places(s)
        rows = pl.ds(pl.multiple_of(s * TOK, TOK), TOK)
        for j in range(PAIRS):
            lanes = pl.ds(j * 128, 128)
            qs = queries_of(s, j)
            ks = blocks_of(0, place, s, j)
            vs = blocks_of(1, place, s, j)
            da = stacked(datt[rows, lanes])
            at = att2[j // 3, rows, (j % 3) * 128 : (j % 3) * 128 + 128]
            at = jnp.concatenate([at, at], axis=0)
            delta = jnp.sum(da.astype(F32) * at.astype(F32), axis=-1, keepdims=True)
            p = probs[s, j]
            dp = lax.dot_general(da, vs, NT, preferred_element_type=F32)
            ds = (p * (dp - delta)).astype(BF16)
            dq = unstacked(jnp.dot(ds, ks, preferred_element_type=F32)) * 0.125
            dq_ref[s, :, lanes] = dq.astype(BF16)
            dk = lax.dot_general(ds, qs, TN, preferred_element_type=F32)
            dv = lax.dot_general(p.astype(BF16), da, TN, preferred_element_type=F32)
            for i in range(SLOTS):
                cb[0, s, i, :, lanes] = dk[i * TOK : (i + 1) * TOK]
                cb[1, s, i, :, lanes] = dv[i * TOK : (i + 1) * TOK]

    stores[1].start()
    placed = [places(s) for s in range(2)]

    def slot_of(s, row, col):
        slot = jnp.int32(SLOTS)
        place, count = placed[s]
        for i in range(SLOTS):
            hit = (place[i][0] == col) & (place[i][1] == row) & (i < count)
            slot = jnp.where(hit, i, slot)
        return slot

    def terms(t, col, row):
        total = None
        for s in range(2):
            if 0 <= row - s <= 2:
                x = cb[t, s, slot_of(s, row - s, col)]
                total = x if total is None else total + x
        return total

    def to_mate(t):
        return remote(gsp.at[t], grp.at[t], gp_s.at[t], gp_r.at[t], mate)

    def to_lat(t, way, which):
        device = (up, down)[way]
        return remote(
            gsl.at[t, way, which],
            grl.at[t, way, which],
            gl_s.at[t, way, which],
            gl_r.at[t, way, which],
            device,
        )

    def to_beyond(t):
        return remote(gso.at[t], gro.at[t], go_s.at[t], go_r.at[t], beyond)

    conds = (has_up, has_down)
    from_conds = (has_down, has_up)
    for t in range(2):
        for r in range(4):
            gsp[t, r] = terms(t, ic, r).astype(BF16)
        to_mate(t).start()
        for way in range(2):

            @pl.when(conds[way])
            def _():
                gsl[t, way, 0] = terms(t, oc, 3 * way).astype(BF16)
                to_lat(t, way, 0).start()

    total = wbuf[chunk(n), :].astype(F32)
    for k in range(1, GROUP):
        reduce_copy(k).wait_recv()
        total = total + rsin[k].astype(F32)
    zsum[...] = total.astype(BF16)

    def owner_z(o):
        return 3 * o

    def z_copy(o):
        k = lax.rem(owner_z(o) - z + DEPTH, DEPTH)
        return remote(
            zsum.at[pl.ds(o * PIECE, PIECE)], zin.at[k], z_s.at[o], z_r.at[k], zpeer(owner_z(o))
        )

    for o in range(OWNERS):
        pl.when(z != owner_z(o))(z_copy(o).start)

    for t in range(2):
        to_mate(t).wait_recv()
        for way in range(2):

            @pl.when(conds[way])
            def _():
                x = terms(t, 1, 3 * way) + grp[t, 3 * way].astype(F32)
                gsl[t, way, 1] = x.astype(BF16)
                to_lat(t, way, 1).start()

    def z_gather(o, k):
        return remote(
            wch.at[pl.ds(o * PIECE, PIECE)],
            wch.at[pl.ds(o * PIECE, PIECE)],
            zg_s.at[k],
            zg_r.at[o],
            zpeer(lax.rem(owner_z(o) + k, DEPTH)),
        )

    for o in range(OWNERS):

        @pl.when(z == owner_z(o))
        def _():
            acc = zsum[o * PIECE : (o + 1) * PIECE].astype(F32)
            for k in range(1, DEPTH):
                remote(
                    zsum.at[pl.ds(o * PIECE, PIECE)],
                    zin.at[k],
                    z_s.at[o],
                    z_r.at[k],
                    zpeer(lax.rem(z + DEPTH - k, DEPTH)),
                ).wait_recv()
                acc = acc + zin[k].astype(F32)
            wch[o * PIECE : (o + 1) * PIECE] = (acc * (1.0 / math.sqrt(TOKENS))).astype(BF16)
            for k in range(1, DEPTH):
                z_gather(o, k).start()

    for t in range(2):
        for r in range(2):
            x = terms(t, oc, 1 + r)
            gso[t, r] = x.astype(BF16)
        for way in range(2):

            @pl.when(from_conds[way])
            def _():
                to_lat(t, way, 0).wait_recv()
                r = 1 - way
                x = terms(t, oc, 1 + r) + grl[t, way, 0].astype(F32)
                gso[t, r] = x.astype(BF16)

        to_beyond(t).start()

    for o in range(OWNERS):
        pl.when(z != owner_z(o))(z_gather(o, 1).wait_recv)

    def gather_copy(k):
        device, _ = peer(k)
        return remote(wch, wfin.at[core, chunk(n)], ag_s.at[k], ag_r.at[k], device)

    @pl.loop(1, GROUP)
    def _(k):
        gather_copy(k).start()

    wfin[core, chunk(n), :] = wch[...]

    def pass_on(k, half):
        m = lax.rem(n + GROUP - k, GROUP)
        return remote(
            wfin.at[half, chunk(m)], wfin.at[half, chunk(m)], fw_s.at[k], fw_r.at[k], mate
        )

    pass_on(0, core).start()

    outs = (dk_ref, dv_ref)
    for t in range(2):
        to_beyond(t).wait_recv()
        for r in range(2):
            x = terms(t, 1, 1 + r) + grp[t, 1 + r].astype(F32) + gro[t, r].astype(F32)
            outs[t][r] = x.astype(BF16)
        for way in range(2):

            @pl.when(from_conds[way])
            def _():
                to_lat(t, way, 1).wait_recv()
                r = 1 - way
                x = terms(t, 1, 1 + r) + grp[t, 1 + r].astype(F32) + gro[t, r].astype(F32)
                outs[t][r] = (x + grl[t, way, 1].astype(F32)).astype(BF16)

        stores[2 + t].start()

    @pl.loop(1, GROUP)
    def _(k):
        m = lax.rem(n + GROUP - k, GROUP)
        device = (m // 2, z * 4 + lax.rem(m, 2) * 2 + core)
        remote(wch, wfin.at[core, chunk(m)], ag_s.at[k], ag_r.at[k], device).wait_recv()
        pass_on(k, core).start()

    @pl.loop(0, GROUP)
    def _(k):
        pass_on(k, 1 - core).wait_recv()

    stores[4].start()

    for t in range(2):
        c = first(t)
        c[0].wait_send()
        c[3].wait_send()
        d = second(t)
        for x in (c[1], d[0], d[2]):
            pl.when(has_up)(x.wait_send)
        for x in (c[2], d[1], d[3]):
            pl.when(has_down)(x.wait_send)
        to_mate(t).wait_send()
        to_beyond(t).wait_send()
        for way in range(2):
            for which in range(2):
                pl.when(conds[way])(to_lat(t, way, which).wait_send)
    send_u.wait_send()
    send_att.wait_send()
    for o in range(OWNERS):
        pl.when(z != owner_z(o))(z_copy(o).wait_send)

        @pl.when(z == owner_z(o))
        def _():
            for k in range(1, DEPTH):
                z_gather(o, k).wait_send()

    @pl.loop(1, GROUP)
    def _(k):
        reduce_copy(k).wait_send()
        gather_copy(k).wait_send()

    @pl.loop(0, GROUP)
    def _(k):
        pass_on(k, core).wait_send()

    for store in stores:
        store.wait()


def finish(mixed, dq, dk, dv, wfin, mixed_out, dq_out, dk_out, dv_out, wg_out, *scratch):
    held, narrow, wide, in_s, out_s = scratch
    large = [pltpu.make_async_copy(wfin.at[h], narrow.at[h], in_s.at[h]) for h in range(2)]
    small = [
        pltpu.make_async_copy(src, held.at[i], in_s.at[2 + i])
        for i, src in enumerate((mixed, dq, dk, dv))
    ]
    for copy in large + small:
        copy.start()
    out = []
    for h in range(2):
        rows = pl.ds(h * HALF, HALF)
        large[h].wait()
        for g in range(D // 128):
            wide[rows, g * 128 : g * 128 + 128] = narrow[h, g * HALF : (g + 1) * HALF].astype(F32)
        out.append(pltpu.make_async_copy(wide.at[rows], wg_out.at[rows], out_s.at[h]))
        out[h].start()
    for i, dst in enumerate((mixed_out, dq_out, dk_out, dv_out)):
        small[i].wait()
        out.append(pltpu.make_async_copy(held.at[i], dst, out_s.at[2 + i]))
        out[2 + i].start()
    for copy in out:
        copy.wait()


def on_device(queries, key_vectors, value_vectors, upstream, w_out, neighbours, counts):
    shape = queries.shape
    hbm = pl.BlockSpec(memory_space=pltpu.HBM)
    blocks = jax.ShapeDtypeStruct((2, TOK, D), BF16)
    dma = pltpu.SemaphoreType.DMA
    results = pl.pallas_call(
        kernel,
        out_shape=(
            blocks,
            blocks,
            blocks,
            blocks,
            jax.ShapeDtypeStruct((2, FLAT, 128), BF16),
        ),
        in_specs=[hbm] * 7,
        out_specs=(hbm,) * 5,
        scratch_shapes=[
            pltpu.VMEM((2, TOK, D), BF16),
            pltpu.VMEM((2, TOK, D), BF16),
            pltpu.VMEM((2, TOK, D), BF16),
            pltpu.VMEM((2, TOK, D), BF16),
            pltpu.VMEM((2, FLAT, 128), BF16),
            pltpu.VMEM((2, TOK, D), BF16),
            pltpu.VMEM((D, D), BF16),
            pltpu.SMEM((16, SLOTS, NLON), jnp.int32),
            pltpu.SMEM((16, NLON), jnp.int32),
            pltpu.VMEM((2, 3, 4, TOK, D), BF16),
            pltpu.VMEM((256, D), BF16),
            pltpu.VMEM((128, D), BF16),
            pltpu.VMEM((2, PAIRS, 128, 256), F32),
            pltpu.VMEM((2, 128, HALF), BF16),
            pltpu.VMEM((128, HALF), BF16),
            pltpu.VMEM((HALF, 256), BF16),
            pltpu.VMEM((2, 2, SLOTS + 1, TOK, D), F32),
            pltpu.VMEM((2, 4, TOK, D), BF16),
            pltpu.VMEM((2, 4, TOK, D), BF16),
            pltpu.VMEM((2, 2, 2, TOK, D), BF16),
            pltpu.VMEM((2, 2, 2, TOK, D), BF16),
            pltpu.VMEM((2, 2, TOK, D), BF16),
            pltpu.VMEM((2, 2, TOK, D), BF16),
            pltpu.VMEM((FLAT, 128), BF16),
            pltpu.VMEM((GROUP, CHUNK, 128), BF16),
            pltpu.VMEM((CHUNK, 128), BF16),
            pltpu.VMEM((DEPTH, PIECE, 128), BF16),
            pltpu.VMEM((CHUNK, 128), BF16),
            dma((7,)),
            dma((5,)),
            dma((2, 8)),
            dma((2, 8)),
            dma((2,)),
            dma((2,)),
            dma((2,)),
            dma((2,)),
            dma((2, 2, 2)),
            dma((2, 2, 2)),
            dma((2,)),
            dma((2,)),
            dma((GROUP,)),
            dma((GROUP,)),
            dma((OWNERS,)),
            dma((DEPTH,)),
            dma((DEPTH,)),
            dma((OWNERS,)),
            dma((GROUP,)),
            dma((GROUP,)),
            dma((GROUP,)),
            dma((GROUP,)),
        ],
        compiler_params=pltpu.CompilerParams(
            collective_id=0, has_side_effects=True, vmem_limit_bytes=VMEM
        ),
    )(
        queries.reshape(2, TOK, D),
        key_vectors.reshape(2, TOK, D),
        value_vectors.reshape(2, TOK, D),
        upstream.reshape(2 * TOK, D),
        w_out,
        neighbours.transpose(0, 2, 1),
        counts,
    )
    mixed, dq, dk, dv, wg = pl.pallas_call(
        finish,
        out_shape=(
            blocks,
            blocks,
            blocks,
            blocks,
            jax.ShapeDtypeStruct((D, D), F32),
        ),
        in_specs=[hbm] * 5,
        out_specs=(hbm,) * 5,
        scratch_shapes=[
            pltpu.VMEM((4, 2, TOK, D), BF16),
            pltpu.VMEM((2, FLAT, 128), BF16),
            pltpu.VMEM((D, D), F32),
            dma((6,)),
            dma((6,)),
        ],
        compiler_params=pltpu.CompilerParams(vmem_limit_bytes=VMEM),
    )(*results)
    return (mixed.reshape(shape), dq.reshape(shape), dk.reshape(shape), dv.reshape(shape), wg)


def solution(mesh):
    grid = P("lat", "lon", None)
    return jax.shard_map(
        on_device,
        mesh=mesh,
        in_specs=(grid, grid, grid, grid, P(), P(), P()),
        out_specs=(grid, grid, grid, grid, P()),
        check_vma=False,
    )
```

```python
import math

import jax
import jax.numpy as jnp
from jax import lax
from jax.experimental import pallas as pl
from jax.experimental.pallas import tpu as pltpu
from jax.sharding import PartitionSpec as P

F32 = jnp.float32
BF16 = jnp.bfloat16
MESH = pl.DeviceIdType.MESH

HEAD_DIM = 64
SLOTS = 4
TOK = 64
D = 768
PAIRS = 6
NLON = 32
NLAT = 8
TOKENS = 32768
HALF = D // 2
GROUP = 16
FLAT = HALF * (D // 128)
CHUNK = FLAT // GROUP
OWNERS = 3
PIECE = CHUNK // OWNERS
DEPTH = 8
VMEM = 58 * 2**20
NT = (((1,), (1,)), ((), ()))
TN = (((0,), (0,)), ((), ()))


def remote(src, dst, send_sem, recv_sem, device):
    return pltpu.make_async_remote_copy(
        src_ref=src,
        dst_ref=dst,
        send_sem=send_sem,
        recv_sem=recv_sem,
        device_id=device,
        device_id_type=MESH,
    )


def kernel(
    q_hbm,
    k_hbm,
    v_hbm,
    u_hbm,
    w_hbm,
    nb_hbm,
    ct_hbm,
    mixed_hbm,
    dq_hbm,
    dk_hbm,
    dv_hbm,
    wfin_hbm,
    mixed_ref,
    dq_ref,
    dk_ref,
    dv_ref,
    wfin,
    q_ref,
    w_ref,
    nb_ref,
    ct_ref,
    kvb,
    ucat,
    datt,
    probs,
    att2,
    att_in,
    att_t,
    cb,
    gsp,
    grp,
    gsl,
    grl,
    gso,
    gro,
    wbuf,
    rsin,
    zsum,
    zin,
    wch,
    in_s,
    out_s,
    halo_s,
    halo_r,
    u_s,
    u_r,
    gp_s,
    gp_r,
    gl_s,
    gl_r,
    go_s,
    go_r,
    rs_s,
    rs_r,
    z_s,
    z_r,
    zg_s,
    zg_r,
    ag_s,
    ag_r,
    fw_s,
    fw_r,
):
    a = lax.axis_index("lat")
    b = lax.axis_index("lon")
    core = lax.rem(b, 2)
    ylo = lax.rem(b // 2, 2)
    z = b // 4
    has_up = a > 0
    has_down = a < NLAT - 1
    mate = (a, b + 1 - 2 * core)
    beyond = (a, lax.rem(b + NLON - 1 + 2 * core, NLON))
    seam = (a == NLAT // 2, a == NLAT // 2 - 1)
    near = (has_up & (a != NLAT // 2), has_down & (a != NLAT // 2 - 1))
    up = (a - 1, b)
    down = (a + 1, b)
    oc = 2 * core
    ic = 2 - oc
    n = a * 2 + ylo

    def peer(k):
        m = lax.rem(n + k, GROUP)
        return (m // 2, z * 4 + lax.rem(m, 2) * 2 + core), m

    def zpeer(zz):
        return (a, zz * 4 + ylo * 2 + core)

    barrier = pltpu.get_barrier_semaphore()

    def greet(device):
        pl.semaphore_signal(barrier, inc=1, device_id=device, device_id_type=MESH)

    greet(mate)
    greet(beyond)

    @pl.loop(1, GROUP)
    def _(k):
        greet(peer(k)[0])

    @pl.loop(1, DEPTH)
    def _(k):
        greet(zpeer(lax.rem(z + k, DEPTH)))

    own_u = ucat.at[pl.ds(0, 128)]
    loads = [
        pltpu.make_async_copy(src, dst, in_s.at[i])
        for i, (src, dst) in enumerate(
            (
                (u_hbm, own_u),
                (w_hbm, w_ref),
                (k_hbm, kvb.at[0, 1, pl.ds(1, 2)]),
                (v_hbm, kvb.at[1, 1, pl.ds(1, 2)]),
                (q_hbm, q_ref),
                (nb_hbm, nb_ref),
                (ct_hbm, ct_ref),
            )
        )
    ]
    for load in loads:
        load.start()
    pl.semaphore_wait(barrier, 2 + GROUP - 1 + DEPTH - 1)

    stores = [
        pltpu.make_async_copy(src, dst, out_s.at[i])
        for i, (src, dst) in enumerate(
            (
                (mixed_ref, mixed_hbm),
                (dq_ref, dq_hbm),
                (dk_ref, dk_hbm),
                (dv_ref, dv_hbm),
                (wfin, wfin_hbm),
            )
        )
    ]

    def halo(t, i, src, dst, device):
        return remote(src, dst, halo_s.at[t, i], halo_r.at[t, i], device)

    ins = (k_hbm, v_hbm)

    def first(t):
        src = ins[t]
        return (
            halo(t, 1, src, kvb.at[t, ic, pl.ds(1, 2)], beyond),
            halo(t, 2, src.at[0], kvb.at[t, 1, 3], up),
            halo(t, 3, src.at[1], kvb.at[t, 1, 0], down),
            halo(t, 0, src, kvb.at[t, oc, pl.ds(1, 2)], mate),
        )

    def second(t):
        return (
            halo(t, 4, kvb.at[t, oc, 1], kvb.at[t, oc, 3], up),
            halo(t, 5, kvb.at[t, oc, 2], kvb.at[t, oc, 0], down),
            halo(t, 6, kvb.at[t, 1, 0], kvb.at[t, oc, 0], mate),
            halo(t, 7, kvb.at[t, 1, 3], kvb.at[t, oc, 3], mate),
            remote(kvb.at[t, 1, 0], kvb.at[t, ic, 0], halo_s.at[t, 4], halo_r.at[t, 5], beyond),
            remote(kvb.at[t, 1, 3], kvb.at[t, ic, 3], halo_s.at[t, 5], halo_r.at[t, 4], beyond),
        )

    for t in range(2):
        c = first(t)
        c[0].start()
        pl.when(has_up)(c[1].start)
        pl.when(has_down)(c[2].start)
        c[3].start()
    send_u = remote(u_hbm, ucat.at[pl.ds(128, 128)], u_s.at[0], u_r.at[0], mate)
    send_u.start()

    loads[0].wait()
    loads[1].wait()
    datt[...] = lax.dot_general(
        own_u[...], w_ref[...], NT, preferred_element_type=F32
    ).astype(BF16)
    for t in range(2):
        for s in range(2):
            cb[t, s, SLOTS] = jnp.zeros((TOK, D), F32)

    for load in loads[2:]:
        load.wait()
    for t in range(2):
        c = second(t)
        halo(t, 1, k_hbm, kvb.at[t, oc, pl.ds(1, 2)], beyond).wait_recv()
        pl.when(near[0])(c[0].start)
        pl.when(near[1])(c[1].start)

        @pl.when(has_up)
        def _():
            halo(t, 3, k_hbm.at[0], kvb.at[t, 1, 0], up).wait_recv()
            pl.when(seam[0])(c[4].start)
            c[2].start()

        @pl.when(has_down)
        def _():
            halo(t, 2, k_hbm.at[0], kvb.at[t, 1, 3], down).wait_recv()
            pl.when(seam[1])(c[5].start)
            c[3].start()

    for t in range(2):
        halo(t, 0, k_hbm, kvb.at[t, ic, pl.ds(1, 2)], mate).wait_recv()

        @pl.when(has_up)
        def _():
            halo(t, 5, k_hbm.at[0], kvb.at[t, oc, 0], up).wait_recv()
            halo(t, 6, k_hbm.at[0], kvb.at[t, ic, 0], mate).wait_recv()

        @pl.when(has_down)
        def _():
            halo(t, 4, k_hbm.at[0], kvb.at[t, oc, 3], down).wait_recv()
            halo(t, 7, k_hbm.at[0], kvb.at[t, ic, 3], mate).wait_recv()

    def places(s_block):
        i = 2 * a + s_block
        out = []
        for s in range(SLOTS):
            name = nb_ref[i, s, b]
            row = lax.div(name, NLON) - i + 1
            col = lax.rem(lax.rem(name, NLON) - b + 1 + NLON, NLON)
            out.append((jnp.clip(col, 0, 2), jnp.clip(row, 0, 2)))
        return out, ct_ref[i, b]

    def blocks_of(t, place, s_block, j):
        return jnp.concatenate(
            [kvb[t, col, row + s_block, :, pl.ds(j * 128, 128)] for col, row in place], axis=0
        )

    low = lax.broadcasted_iota(jnp.int32, (TOK, 128), 1) < HEAD_DIM

    def stacked(x):
        zero = jnp.zeros_like(x)
        return jnp.concatenate([jnp.where(low, x, zero), jnp.where(low, zero, x)], axis=0)

    def queries_of(s_block, j):
        x = q_ref[s_block, :, pl.ds(j * 128, 128)]
        return stacked(x * jnp.asarray(0.125, BF16))

    def unstacked(x):
        return jnp.where(low, x[:TOK], x[TOK:])

    @pl.loop(0, 2)
    def _(s):
        place, count = places(s)
        kept = lax.broadcasted_iota(jnp.int32, (2 * TOK, SLOTS * TOK), 1) < count * TOK
        rows = pl.ds(pl.multiple_of(s * TOK, TOK), TOK)
        scores = []
        for j in range(PAIRS):
            scores.append(
                lax.dot_general(
                    queries_of(s, j), blocks_of(0, place, s, j), NT, preferred_element_type=F32
                )
            )
        for j in range(PAIRS):
            masked = jnp.where(kept, scores[j], -1e30)
            top = jnp.max(masked, axis=-1, keepdims=True)
            e = jnp.exp(masked - top)
            probs[s, j] = e * (1.0 / jnp.sum(e, axis=-1, keepdims=True))
        for j in range(PAIRS):
            o = jnp.dot(
                probs[s, j].astype(BF16), blocks_of(1, place, s, j), preferred_element_type=F32
            )
            att2[j // 3, rows, (j % 3) * 128 : (j % 3) * 128 + 128] = unstacked(o).astype(BF16)

    send_att = remote(att2.at[1 - core], att_in, u_s.at[1], u_r.at[1], mate)
    send_att.start()
    att_t[:, 0:128] = att2[core].T
    remote(u_hbm, ucat.at[pl.ds(128, 128)], u_s.at[0], u_r.at[0], mate).wait_recv()
    send_att.wait_recv()
    att_t[:, 128:256] = att_in[...].T
    for g in range(3):
        term = jnp.dot(
            att_t[...], ucat[:, g * 256 : g * 256 + 256], preferred_element_type=F32
        ).astype(BF16)
        wbuf[2 * g * HALF : (2 * g + 1) * HALF] = term[:, :128]
        wbuf[(2 * g + 1) * HALF : (2 * g + 2) * HALF] = term[:, 128:]

    def chunk(m):
        return pl.ds(pl.multiple_of(m * CHUNK, 16), CHUNK)

    def reduce_copy(k):
        device, m = peer(k)
        return remote(wbuf.at[chunk(m)], rsin.at[k], rs_s.at[k], rs_r.at[k], device)

    @pl.loop(1, GROUP)
    def _(k):
        reduce_copy(k).start()

    att = jnp.concatenate([att2[0], att2[1]], axis=1)
    mixed = jnp.dot(att, w_ref[...], preferred_element_type=F32).astype(BF16)
    mixed_ref[0] = mixed[:TOK]
    mixed_ref[1] = mixed[TOK:]
    stores[0].start()

    @pl.loop(0, 2)
    def _(s):
        place, _ = places(s)
        rows = pl.ds(pl.multiple_of(s * TOK, TOK), TOK)
        for j in range(PAIRS):
            lanes = pl.ds(j * 128, 128)
            qs = queries_of(s, j)
            ks = blocks_of(0, place, s, j)
            vs = blocks_of(1, place, s, j)
            da = stacked(datt[rows, lanes])
            at = att2[j // 3, rows, (j % 3) * 128 : (j % 3) * 128 + 128]
            at = jnp.concatenate([at, at], axis=0)
            delta = jnp.sum(da.astype(F32) * at.astype(F32), axis=-1, keepdims=True)
            p = probs[s, j]
            dp = lax.dot_general(da, vs, NT, preferred_element_type=F32)
            ds = (p * (dp - delta)).astype(BF16)
            dq = unstacked(jnp.dot(ds, ks, preferred_element_type=F32)) * 0.125
            dq_ref[s, :, lanes] = dq.astype(BF16)
            dk = lax.dot_general(ds, qs, TN, preferred_element_type=F32)
            dv = lax.dot_general(p.astype(BF16), da, TN, preferred_element_type=F32)
            for i in range(SLOTS):
                cb[0, s, i, :, lanes] = dk[i * TOK : (i + 1) * TOK]
                cb[1, s, i, :, lanes] = dv[i * TOK : (i + 1) * TOK]

    stores[1].start()
    placed = [places(s) for s in range(2)]

    def slot_of(s, row, col):
        slot = jnp.int32(SLOTS)
        place, count = placed[s]
        for i in range(SLOTS):
            hit = (place[i][0] == col) & (place[i][1] == row) & (i < count)
            slot = jnp.where(hit, i, slot)
        return slot

    def terms(t, col, row):
        total = None
        for s in range(2):
            if 0 <= row - s <= 2:
                x = cb[t, s, slot_of(s, row - s, col)]
                total = x if total is None else total + x
        return total

    def to_mate(t):
        return remote(gsp.at[t], grp.at[t], gp_s.at[t], gp_r.at[t], mate)

    def to_lat(t, way, which):
        device = (up, down)[way]
        return remote(
            gsl.at[t, way, which],
            grl.at[t, way, which],
            gl_s.at[t, way, which],
            gl_r.at[t, way, which],
            device,
        )

    def over_seam(t, way):
        return remote(
            gsl.at[t, way, 0],
            grl.at[t, 1 - way, 0],
            gl_s.at[t, way, 0],
            gl_r.at[t, 1 - way, 0],
            beyond,
        )

    def to_beyond(t):
        return remote(gso.at[t], gro.at[t], go_s.at[t], go_r.at[t], beyond)

    conds = (has_up, has_down)
    from_conds = (has_down, has_up)
    for t in range(2):
        for r in range(4):
            gsp[t, r] = terms(t, ic, r).astype(BF16)
        to_mate(t).start()
        for way in range(2):

            @pl.when(conds[way])
            def _():
                gsl[t, way, 0] = terms(t, oc, 3 * way).astype(BF16)

            pl.when(near[way])(to_lat(t, way, 0).start)
            pl.when(seam[way])(over_seam(t, way).start)

    total = wbuf[chunk(n), :].astype(F32)
    for k in range(1, GROUP):
        reduce_copy(k).wait_recv()
        total = total + rsin[k].astype(F32)
    zsum[...] = total.astype(BF16)

    def owner_z(o):
        return 3 * o

    def z_copy(o):
        k = lax.rem(owner_z(o) - z + DEPTH, DEPTH)
        return remote(
            zsum.at[pl.ds(o * PIECE, PIECE)], zin.at[k], z_s.at[o], z_r.at[k], zpeer(owner_z(o))
        )

    for o in range(OWNERS):
        pl.when(z != owner_z(o))(z_copy(o).start)

    for t in range(2):
        for r in range(2):
            x = terms(t, oc, 1 + r)
            gso[t, r] = x.astype(BF16)
        for way in range(2):

            @pl.when(near[1 - way])
            def _():
                to_lat(t, way, 0).wait_recv()
                r = 1 - way
                x = terms(t, oc, 1 + r) + grl[t, way, 0].astype(F32)
                gso[t, r] = x.astype(BF16)

        to_beyond(t).start()

    for t in range(2):
        to_mate(t).wait_recv()
        for way in range(2):

            @pl.when(near[way])
            def _():
                x = terms(t, 1, 3 * way) + grp[t, 3 * way].astype(F32)
                gsl[t, way, 1] = x.astype(BF16)

            @pl.when(seam[way])
            def _():
                over_seam(t, way).wait_recv()
                x = terms(t, 1, 3 * way) + grp[t, 3 * way].astype(F32)
                gsl[t, way, 1] = (x + grl[t, 1 - way, 0].astype(F32)).astype(BF16)

            pl.when(conds[way])(to_lat(t, way, 1).start)

    def z_gather(o, k):
        return remote(
            wch.at[pl.ds(o * PIECE, PIECE)],
            wch.at[pl.ds(o * PIECE, PIECE)],
            zg_s.at[k],
            zg_r.at[o],
            zpeer(lax.rem(owner_z(o) + k, DEPTH)),
        )

    for o in range(OWNERS):

        @pl.when(z == owner_z(o))
        def _():
            acc = zsum[o * PIECE : (o + 1) * PIECE].astype(F32)
            for k in range(1, DEPTH):
                remote(
                    zsum.at[pl.ds(o * PIECE, PIECE)],
                    zin.at[k],
                    z_s.at[o],
                    z_r.at[k],
                    zpeer(lax.rem(z + DEPTH - k, DEPTH)),
                ).wait_recv()
                acc = acc + zin[k].astype(F32)
            wch[o * PIECE : (o + 1) * PIECE] = (acc * (1.0 / math.sqrt(TOKENS))).astype(BF16)
            for k in range(1, DEPTH):
                z_gather(o, k).start()

    for o in range(OWNERS):
        pl.when(z != owner_z(o))(z_gather(o, 1).wait_recv)

    def gather_copy(k):
        device, _ = peer(k)
        return remote(wch, wfin.at[core, chunk(n)], ag_s.at[k], ag_r.at[k], device)

    @pl.loop(1, GROUP)
    def _(k):
        gather_copy(k).start()

    wfin[core, chunk(n), :] = wch[...]

    def pass_on(k, half):
        m = lax.rem(n + GROUP - k, GROUP)
        return remote(
            wfin.at[half, chunk(m)], wfin.at[half, chunk(m)], fw_s.at[k], fw_r.at[k], mate
        )

    pass_on(0, core).start()

    outs = (dk_ref, dv_ref)
    for t in range(2):
        to_beyond(t).wait_recv()
        for r in range(2):
            x = terms(t, 1, 1 + r) + grp[t, 1 + r].astype(F32) + gro[t, r].astype(F32)
            outs[t][r] = x.astype(BF16)
        for way in range(2):

            @pl.when(from_conds[way])
            def _():
                to_lat(t, way, 1).wait_recv()
                r = 1 - way
                x = terms(t, 1, 1 + r) + grp[t, 1 + r].astype(F32) + gro[t, r].astype(F32)
                outs[t][r] = (x + grl[t, way, 1].astype(F32)).astype(BF16)

        stores[2 + t].start()

    @pl.loop(1, GROUP)
    def _(k):
        m = lax.rem(n + GROUP - k, GROUP)
        device = (m // 2, z * 4 + lax.rem(m, 2) * 2 + core)
        remote(wch, wfin.at[core, chunk(m)], ag_s.at[k], ag_r.at[k], device).wait_recv()
        pass_on(k, core).start()

    @pl.loop(0, GROUP)
    def _(k):
        pass_on(k, 1 - core).wait_recv()

    stores[4].start()

    for t in range(2):
        c = first(t)
        c[0].wait_send()
        c[3].wait_send()
        d = second(t)
        for x in (c[1], d[0], d[2]):
            pl.when(has_up)(x.wait_send)
        for x in (c[2], d[1], d[3]):
            pl.when(has_down)(x.wait_send)
        to_mate(t).wait_send()
        to_beyond(t).wait_send()
        for way in range(2):
            for which in range(2):
                pl.when(conds[way])(to_lat(t, way, which).wait_send)
    send_u.wait_send()
    send_att.wait_send()
    for o in range(OWNERS):
        pl.when(z != owner_z(o))(z_copy(o).wait_send)

        @pl.when(z == owner_z(o))
        def _():
            for k in range(1, DEPTH):
                z_gather(o, k).wait_send()

    @pl.loop(1, GROUP)
    def _(k):
        reduce_copy(k).wait_send()
        gather_copy(k).wait_send()

    @pl.loop(0, GROUP)
    def _(k):
        pass_on(k, core).wait_send()

    for store in stores:
        store.wait()


def finish(mixed, dq, dk, dv, wfin, mixed_out, dq_out, dk_out, dv_out, wg_out, *scratch):
    held, narrow, wide, in_s, out_s = scratch
    large = [pltpu.make_async_copy(wfin.at[h], narrow.at[h], in_s.at[h]) for h in range(2)]
    small = [
        pltpu.make_async_copy(src, held.at[i], in_s.at[2 + i])
        for i, src in enumerate((mixed, dq, dk, dv))
    ]
    for copy in large + small:
        copy.start()
    out = []
    for h in range(2):
        rows = pl.ds(h * HALF, HALF)
        large[h].wait()
        for g in range(D // 128):
            wide[rows, g * 128 : g * 128 + 128] = narrow[h, g * HALF : (g + 1) * HALF].astype(F32)
        out.append(pltpu.make_async_copy(wide.at[rows], wg_out.at[rows], out_s.at[h]))
        out[h].start()
    for i, dst in enumerate((mixed_out, dq_out, dk_out, dv_out)):
        small[i].wait()
        out.append(pltpu.make_async_copy(held.at[i], dst, out_s.at[2 + i]))
        out[2 + i].start()
    for copy in out:
        copy.wait()


def on_device(queries, key_vectors, value_vectors, upstream, w_out, neighbours, counts):
    shape = queries.shape
    hbm = pl.BlockSpec(memory_space=pltpu.HBM)
    blocks = jax.ShapeDtypeStruct((2, TOK, D), BF16)
    dma = pltpu.SemaphoreType.DMA
    results = pl.pallas_call(
        kernel,
        out_shape=(
            blocks,
            blocks,
            blocks,
            blocks,
            jax.ShapeDtypeStruct((2, FLAT, 128), BF16),
        ),
        in_specs=[hbm] * 7,
        out_specs=(hbm,) * 5,
        scratch_shapes=[
            pltpu.VMEM((2, TOK, D), BF16),
            pltpu.VMEM((2, TOK, D), BF16),
            pltpu.VMEM((2, TOK, D), BF16),
            pltpu.VMEM((2, TOK, D), BF16),
            pltpu.VMEM((2, FLAT, 128), BF16),
            pltpu.VMEM((2, TOK, D), BF16),
            pltpu.VMEM((D, D), BF16),
            pltpu.SMEM((16, SLOTS, NLON), jnp.int32),
            pltpu.SMEM((16, NLON), jnp.int32),
            pltpu.VMEM((2, 3, 4, TOK, D), BF16),
            pltpu.VMEM((256, D), BF16),
            pltpu.VMEM((128, D), BF16),
            pltpu.VMEM((2, PAIRS, 128, 256), F32),
            pltpu.VMEM((2, 128, HALF), BF16),
            pltpu.VMEM((128, HALF), BF16),
            pltpu.VMEM((HALF, 256), BF16),
            pltpu.VMEM((2, 2, SLOTS + 1, TOK, D), F32),
            pltpu.VMEM((2, 4, TOK, D), BF16),
            pltpu.VMEM((2, 4, TOK, D), BF16),
            pltpu.VMEM((2, 2, 2, TOK, D), BF16),
            pltpu.VMEM((2, 2, 2, TOK, D), BF16),
            pltpu.VMEM((2, 2, TOK, D), BF16),
            pltpu.VMEM((2, 2, TOK, D), BF16),
            pltpu.VMEM((FLAT, 128), BF16),
            pltpu.VMEM((GROUP, CHUNK, 128), BF16),
            pltpu.VMEM((CHUNK, 128), BF16),
            pltpu.VMEM((DEPTH, PIECE, 128), BF16),
            pltpu.VMEM((CHUNK, 128), BF16),
            dma((7,)),
            dma((5,)),
            dma((2, 8)),
            dma((2, 8)),
            dma((2,)),
            dma((2,)),
            dma((2,)),
            dma((2,)),
            dma((2, 2, 2)),
            dma((2, 2, 2)),
            dma((2,)),
            dma((2,)),
            dma((GROUP,)),
            dma((GROUP,)),
            dma((OWNERS,)),
            dma((DEPTH,)),
            dma((DEPTH,)),
            dma((OWNERS,)),
            dma((GROUP,)),
            dma((GROUP,)),
            dma((GROUP,)),
            dma((GROUP,)),
        ],
        compiler_params=pltpu.CompilerParams(
            collective_id=0, has_side_effects=True, vmem_limit_bytes=VMEM
        ),
    )(
        queries.reshape(2, TOK, D),
        key_vectors.reshape(2, TOK, D),
        value_vectors.reshape(2, TOK, D),
        upstream.reshape(2 * TOK, D),
        w_out,
        neighbours.transpose(0, 2, 1),
        counts,
    )
    mixed, dq, dk, dv, wg = pl.pallas_call(
        finish,
        out_shape=(
            blocks,
            blocks,
            blocks,
            blocks,
            jax.ShapeDtypeStruct((D, D), F32),
        ),
        in_specs=[hbm] * 5,
        out_specs=(hbm,) * 5,
        scratch_shapes=[
            pltpu.VMEM((4, 2, TOK, D), BF16),
            pltpu.VMEM((2, FLAT, 128), BF16),
            pltpu.VMEM((D, D), F32),
            dma((6,)),
            dma((6,)),
        ],
        compiler_params=pltpu.CompilerParams(vmem_limit_bytes=VMEM),
    )(*results)
    return (mixed.reshape(shape), dq.reshape(shape), dk.reshape(shape), dv.reshape(shape), wg)


def solution(mesh):
    grid = P("lat", "lon", None)
    return jax.shard_map(
        on_device,
        mesh=mesh,
        in_specs=(grid, grid, grid, grid, P(), P(), P()),
        out_specs=(grid, grid, grid, grid, P()),
        check_vma=False,
    )
```

```python
import math

import jax
import jax.numpy as jnp
from jax import lax
from jax.experimental import pallas as pl
from jax.experimental.pallas import tpu as pltpu
from jax.sharding import PartitionSpec as P

F32 = jnp.float32
BF16 = jnp.bfloat16
MESH = pl.DeviceIdType.MESH

HEAD_DIM = 64
SLOTS = 4
TOK = 64
D = 768
PAIRS = 6
NLON = 32
NLAT = 8
TOKENS = 32768
HALF = D // 2
GROUP = 16
FLAT = HALF * (D // 128)
CHUNK = FLAT // GROUP
OWNERS = 3
PIECE = CHUNK // OWNERS
DEPTH = 8
STEPS = (
    (2, 2), (2, 1), (2, 3), (1, 2), (3, 2), (1, 1), (3, 3), (1, 3), (3, 1), (2, 0), (0, 2), (1, 0),
    (3, 0), (0, 1), (0, 3),
)
VMEM = 58 * 2**20
NT = (((1,), (1,)), ((), ()))
TN = (((0,), (0,)), ((), ()))


def remote(src, dst, send_sem, recv_sem, device):
    return pltpu.make_async_remote_copy(
        src_ref=src,
        dst_ref=dst,
        send_sem=send_sem,
        recv_sem=recv_sem,
        device_id=device,
        device_id_type=MESH,
    )


def kernel(
    q_hbm,
    k_hbm,
    v_hbm,
    u_hbm,
    w_hbm,
    nb_hbm,
    ct_hbm,
    mixed_hbm,
    dq_hbm,
    dk_hbm,
    dv_hbm,
    wfin_hbm,
    mixed_ref,
    dq_ref,
    dk_ref,
    dv_ref,
    wfin,
    q_ref,
    w_ref,
    nb_ref,
    ct_ref,
    kb,
    vb,
    ucat,
    datt,
    probs,
    att2,
    att_in,
    att_t,
    cb,
    gsp,
    grp,
    gsl,
    grl,
    gso,
    gro,
    wbuf,
    rsin,
    zsum,
    zin,
    wch,
    in_s,
    out_s,
    halo_s,
    halo_r,
    u_s,
    u_r,
    gp_s,
    gp_r,
    gl_s,
    gl_r,
    go_s,
    go_r,
    rs_s,
    rs_r,
    z_s,
    z_r,
    zg_s,
    zg_r,
    ag_s,
    ag_r,
    fw_s,
    fw_r,
):
    kvb = (kb, vb)
    a = lax.axis_index("lat")
    b = lax.axis_index("lon")
    core = lax.rem(b, 2)
    ylo = lax.rem(b // 2, 2)
    z = b // 4
    has_up = a > 0
    has_down = a < NLAT - 1
    mate = (a, b + 1 - 2 * core)
    beyond = (a, lax.rem(b + NLON - 1 + 2 * core, NLON))
    seam = (a == NLAT // 2, a == NLAT // 2 - 1)
    near = (has_up & (a != NLAT // 2), has_down & (a != NLAT // 2 - 1))
    up = (a - 1, b)
    down = (a + 1, b)
    oc = 2 * core
    ic = 2 - oc
    chip_x = lax.rem(a, 4)
    chip_y = a // 4 * 2 + ylo
    n = chip_x * 4 + chip_y

    def peer(dx, dy):
        px, py = lax.rem(chip_x + 4 + dx, 4), lax.rem(chip_y + 4 + dy, 4)
        return (py // 2 * 4 + px, z * 4 + lax.rem(py, 2) * 2 + core), px * 4 + py

    def zpeer(zz):
        return (a, zz * 4 + ylo * 2 + core)

    barrier = pltpu.get_barrier_semaphore()

    def greet(device):
        pl.semaphore_signal(barrier, inc=1, device_id=device, device_id_type=MESH)

    for k in (4, 3, 5, 2, 6, 1, 7):
        greet(zpeer(lax.rem(z + k, DEPTH)))
    for step in STEPS:
        greet(peer(*step)[0])
    greet(beyond)
    greet(mate)
    own_u = ucat.at[pl.ds(0, 128)]
    loads = [
        pltpu.make_async_copy(src, dst, in_s.at[i])
        for i, (src, dst) in enumerate(
            (
                (u_hbm, own_u),
                (w_hbm, w_ref),
                (k_hbm, kvb[0].at[1, pl.ds(1, 2)]),
                (v_hbm, kvb[1].at[1, pl.ds(1, 2)]),
                (q_hbm, q_ref),
                (nb_hbm, nb_ref),
                (ct_hbm, ct_ref),
            )
        )
    ]
    for load in loads:
        load.start()
    pl.semaphore_wait(barrier, 2 + GROUP - 1 + DEPTH - 1)

    stores = [
        pltpu.make_async_copy(src, dst, out_s.at[i])
        for i, (src, dst) in enumerate(
            (
                (mixed_ref, mixed_hbm),
                (dq_ref, dq_hbm),
                (dk_ref, dk_hbm),
                (dv_ref, dv_hbm),
            )
        )
    ]

    def halo(t, i, src, dst, device):
        return remote(src, dst, halo_s.at[t, i], halo_r.at[t, i], device)

    ins = (k_hbm, v_hbm)

    def first(t):
        src = ins[t]
        return (
            halo(t, 1, src.at[0], kvb[t].at[ic, 1], beyond),
            halo(t, 8, src.at[1], kvb[t].at[ic, 2], beyond),
            halo(t, 2, src.at[0], kvb[t].at[1, 3], up),
            halo(t, 3, src.at[1], kvb[t].at[1, 0], down),
            halo(t, 0, src, kvb[t].at[oc, pl.ds(1, 2)], mate),
        )

    def second(t):
        return (
            halo(t, 4, kvb[t].at[oc, 1], kvb[t].at[oc, 3], up),
            halo(t, 5, kvb[t].at[oc, 2], kvb[t].at[oc, 0], down),
            halo(t, 6, kvb[t].at[1, 0], kvb[t].at[oc, 0], mate),
            halo(t, 7, kvb[t].at[1, 3], kvb[t].at[oc, 3], mate),
            remote(kvb[t].at[1, 0], kvb[t].at[ic, 0], halo_s.at[t, 4], halo_r.at[t, 5], beyond),
            remote(kvb[t].at[1, 3], kvb[t].at[ic, 3], halo_s.at[t, 5], halo_r.at[t, 4], beyond),
        )

    for t in range(2):
        c = first(t)
        c[0].start()
        pl.when(has_up)(c[2].start)
        c[1].start()
        pl.when(has_down)(c[3].start)
        c[4].start()
    send_u = remote(u_hbm, ucat.at[pl.ds(128, 128)], u_s.at[0], u_r.at[0], mate)
    send_u.start()

    loads[0].wait()
    loads[1].wait()
    datt[...] = lax.dot_general(
        own_u[...], w_ref[...], NT, preferred_element_type=F32
    ).astype(BF16)
    for t in range(2):
        for s in range(2):
            cb[t, s, SLOTS] = jnp.zeros((TOK, D), F32)

    for load in loads[2:]:
        load.wait()
    for t in range(2):
        c = second(t)

        @pl.when(has_up)
        def _():
            halo(t, 3, k_hbm.at[0], kvb[t].at[1, 0], up).wait_recv()
            pl.when(seam[0])(c[4].start)
            c[2].start()

        @pl.when(has_down)
        def _():
            halo(t, 2, k_hbm.at[0], kvb[t].at[1, 3], down).wait_recv()
            pl.when(seam[1])(c[5].start)
            c[3].start()

        halo(t, 1, k_hbm.at[0], kvb[t].at[oc, 1], beyond).wait_recv()
        pl.when(near[0])(c[0].start)
        halo(t, 8, k_hbm.at[0], kvb[t].at[oc, 2], beyond).wait_recv()
        pl.when(near[1])(c[1].start)

    def complete(t):
        halo(t, 0, k_hbm, kvb[t].at[ic, pl.ds(1, 2)], mate).wait_recv()

        @pl.when(has_up)
        def _():
            halo(t, 6, k_hbm.at[0], kvb[t].at[ic, 0], mate).wait_recv()
            halo(t, 5, k_hbm.at[0], kvb[t].at[oc, 0], up).wait_recv()

        @pl.when(has_down)
        def _():
            halo(t, 7, k_hbm.at[0], kvb[t].at[ic, 3], mate).wait_recv()
            halo(t, 4, k_hbm.at[0], kvb[t].at[oc, 3], down).wait_recv()

    def places(s_block):
        i = 2 * a + s_block
        out = []
        for s in range(SLOTS):
            name = nb_ref[i, s, b]
            row = lax.div(name, NLON) - i + 1
            col = lax.rem(lax.rem(name, NLON) - b + 1 + NLON, NLON)
            out.append((jnp.clip(col, 0, 2), jnp.clip(row, 0, 2)))
        return out, ct_ref[i, b]

    def blocks_of(t, place, s_block, j):
        return jnp.concatenate(
            [kvb[t][col, row + s_block, :, pl.ds(j * 128, 128)] for col, row in place], axis=0
        )

    low = lax.broadcasted_iota(jnp.int32, (TOK, 128), 1) < HEAD_DIM

    def stacked(x):
        zero = jnp.zeros_like(x)
        return jnp.concatenate([jnp.where(low, x, zero), jnp.where(low, zero, x)], axis=0)

    def queries_of(s_block, j):
        x = q_ref[s_block, :, pl.ds(j * 128, 128)]
        return stacked(x * jnp.asarray(0.125, BF16))

    def unstacked(x):
        return jnp.where(low, x[:TOK], x[TOK:])

    placed = [places(s) for s in range(2)]

    def slot_of(s, row, col):
        slot = jnp.int32(SLOTS)
        place, count = placed[s]
        for i in range(SLOTS):
            hit = (place[i][0] == col) & (place[i][1] == row) & (i < count)
            slot = jnp.where(hit, i, slot)
        return slot

    def terms(t, col, row):
        total = None
        for s in range(2):
            if 0 <= row - s <= 2:
                x = cb[t, s, slot_of(s, row - s, col)]
                total = x if total is None else total + x
        return total

    def to_mate(t):
        return remote(gsp.at[t], grp.at[t], gp_s.at[t], gp_r.at[t], mate)

    def to_lat(t, way, which):
        device = (up, down)[way]
        return remote(
            gsl.at[t, way, which],
            grl.at[t, way, which],
            gl_s.at[t, way, which],
            gl_r.at[t, way, which],
            device,
        )

    def over_seam(t, way):
        return remote(
            gsl.at[t, way, 0],
            grl.at[t, 1 - way, 0],
            gl_s.at[t, way, 0],
            gl_r.at[t, 1 - way, 0],
            beyond,
        )

    def to_beyond(t):
        return remote(gso.at[t], gro.at[t], go_s.at[t], go_r.at[t], beyond)

    conds = (has_up, has_down)

    def send_outer(t):
        for way in range(2):

            @pl.when(conds[way])
            def _():
                gsl[t, way, 0] = terms(t, oc, 3 * way).astype(BF16)

            pl.when(near[way])(to_lat(t, way, 0).start)
            pl.when(seam[way])(over_seam(t, way).start)

    def send_mate(t):
        for r in range(4):
            gsp[t, r] = terms(t, ic, r).astype(BF16)
        to_mate(t).start()

    def send_beyond(t):
        for r in range(2):

            @pl.when(near[r])
            def _():
                to_lat(t, 1 - r, 0).wait_recv()
                gso[t, r] = (terms(t, oc, 1 + r) + grl[t, 1 - r, 0].astype(F32)).astype(BF16)

            @pl.when(jnp.logical_not(near[r]))
            def _():
                gso[t, r] = terms(t, oc, 1 + r).astype(BF16)

        to_beyond(t).start()

    def send_own(t):
        to_mate(t).wait_recv()
        for way in range(2):

            @pl.when(near[way])
            def _():
                total = terms(t, 1, 3 * way) + grp[t, 3 * way].astype(F32)
                gsl[t, way, 1] = total.astype(BF16)

            @pl.when(seam[way])
            def _():
                over_seam(t, way).wait_recv()
                total = terms(t, 1, 3 * way) + grp[t, 3 * way].astype(F32)
                gsl[t, way, 1] = (total + grl[t, 1 - way, 0].astype(F32)).astype(BF16)

            pl.when(conds[way])(to_lat(t, way, 1).start)

    def final(t):
        out = (dk_ref, dv_ref)[t]
        to_beyond(t).wait_recv()
        for r in range(2):

            def total():
                return terms(t, 1, 1 + r) + grp[t, 1 + r].astype(F32) + gro[t, r].astype(F32)

            @pl.when(conds[r])
            def _():
                to_lat(t, 1 - r, 1).wait_recv()
                out[r] = (total() + grl[t, 1 - r, 1].astype(F32)).astype(BF16)

            @pl.when(jnp.logical_not(conds[r]))
            def _():
                out[r] = total().astype(BF16)

        stores[2 + t].start()

    complete(0)

    @pl.loop(0, 2)
    def _(s):
        place, count = places(s)
        kept = lax.broadcasted_iota(jnp.int32, (2 * TOK, SLOTS * TOK), 1) < count * TOK
        rows = pl.ds(pl.multiple_of(s * TOK, TOK), TOK)
        scores = []
        for j in range(PAIRS):
            scores.append(
                lax.dot_general(
                    queries_of(s, j), blocks_of(0, place, s, j), NT, preferred_element_type=F32
                )
            )
        for j in range(PAIRS):
            masked = jnp.where(kept, scores[j], -1e30)
            top = jnp.max(masked, axis=-1, keepdims=True)
            e = jnp.exp(masked - top)
            probs[s, j] = e * (1.0 / jnp.sum(e, axis=-1, keepdims=True))
        for j in range(PAIRS):
            lanes = pl.ds(j * 128, 128)
            dv = lax.dot_general(
                probs[s, j].astype(BF16),
                stacked(datt[rows, lanes]),
                TN,
                preferred_element_type=F32,
            )
            for i in range(SLOTS):
                cb[1, s, i, :, lanes] = dv[i * TOK : (i + 1) * TOK]

    send_outer(1)
    send_mate(1)
    complete(1)

    @pl.loop(0, 2)
    def _(s):
        place, _ = places(s)
        rows = pl.ds(pl.multiple_of(s * TOK, TOK), TOK)
        for j in range(PAIRS):
            o = jnp.dot(
                probs[s, j].astype(BF16), blocks_of(1, place, s, j), preferred_element_type=F32
            )
            att2[j // 3, rows, (j % 3) * 128 : (j % 3) * 128 + 128] = unstacked(o).astype(BF16)

    send_att = remote(att2.at[1 - core], att_in, u_s.at[1], u_r.at[1], mate)
    send_att.start()
    att_t[:, 0:128] = att2[core].T
    send_beyond(1)
    remote(u_hbm, ucat.at[pl.ds(128, 128)], u_s.at[0], u_r.at[0], mate).wait_recv()
    send_att.wait_recv()
    att_t[:, 128:256] = att_in[...].T
    for g in range(3):
        term = jnp.dot(
            att_t[...], ucat[:, g * 256 : g * 256 + 256], preferred_element_type=F32
        ).astype(BF16)
        wbuf[2 * g * HALF : (2 * g + 1) * HALF] = term[:, :128]
        wbuf[(2 * g + 1) * HALF : (2 * g + 2) * HALF] = term[:, 128:]

    def chunk(m):
        return pl.ds(pl.multiple_of(m * CHUNK, 16), CHUNK)

    def reduce_copy(k):
        device, m = peer(*STEPS[k])
        return remote(wbuf.at[chunk(m)], rsin.at[k], rs_s.at[k], rs_r.at[k], device)

    for k in range(GROUP - 1):
        reduce_copy(k).start()

    att = jnp.concatenate([att2[0], att2[1]], axis=1)
    mixed = jnp.dot(att, w_ref[...], preferred_element_type=F32).astype(BF16)
    mixed_ref[0] = mixed[:TOK]
    mixed_ref[1] = mixed[TOK:]
    stores[0].start()
    send_own(1)

    @pl.loop(0, 2)
    def _(s):
        place, _ = places(s)
        rows = pl.ds(pl.multiple_of(s * TOK, TOK), TOK)
        for j in range(PAIRS):
            lanes = pl.ds(j * 128, 128)
            qs = queries_of(s, j)
            ks = blocks_of(0, place, s, j)
            vs = blocks_of(1, place, s, j)
            da = stacked(datt[rows, lanes])
            at = att2[j // 3, rows, (j % 3) * 128 : (j % 3) * 128 + 128]
            at = jnp.concatenate([at, at], axis=0)
            delta = jnp.sum(da.astype(F32) * at.astype(F32), axis=-1, keepdims=True)
            p = probs[s, j]
            dp = lax.dot_general(da, vs, NT, preferred_element_type=F32)
            ds = (p * (dp - delta)).astype(BF16)
            dq = unstacked(jnp.dot(ds, ks, preferred_element_type=F32)) * 0.125
            dq_ref[s, :, lanes] = dq.astype(BF16)
            dk = lax.dot_general(ds, qs, TN, preferred_element_type=F32)
            for i in range(SLOTS):
                cb[0, s, i, :, lanes] = dk[i * TOK : (i + 1) * TOK]

    stores[1].start()
    send_outer(0)
    send_mate(0)

    total = wbuf[chunk(n), :].astype(F32)
    for k in reversed(range(GROUP - 1)):
        reduce_copy(k).wait_recv()
        total = total + rsin[k].astype(F32)
    zsum[...] = total.astype(BF16)

    def owner_z(o):
        return 3 * o

    def z_copy(o):
        k = lax.rem(owner_z(o) - z + DEPTH, DEPTH)
        return remote(
            zsum.at[pl.ds(o * PIECE, PIECE)], zin.at[k], z_s.at[o], z_r.at[k], zpeer(owner_z(o))
        )

    for o in range(OWNERS):
        pl.when(z != owner_z(o))(z_copy(o).start)
    send_beyond(0)
    send_own(0)

    def z_gather(o, k):
        return remote(
            wch.at[pl.ds(o * PIECE, PIECE)],
            wch.at[pl.ds(o * PIECE, PIECE)],
            zg_s.at[k],
            zg_r.at[o],
            zpeer(lax.rem(owner_z(o) + k, DEPTH)),
        )

    for o in range(OWNERS):

        @pl.when(z == owner_z(o))
        def _():
            acc = zsum[o * PIECE : (o + 1) * PIECE].astype(F32)
            for k in range(1, DEPTH):
                remote(
                    zsum.at[pl.ds(o * PIECE, PIECE)],
                    zin.at[k],
                    z_s.at[o],
                    z_r.at[k],
                    zpeer(lax.rem(z + DEPTH - k, DEPTH)),
                ).wait_recv()
                acc = acc + zin[k].astype(F32)
            wch[o * PIECE : (o + 1) * PIECE] = (acc * (1.0 / math.sqrt(TOKENS))).astype(BF16)
            for k in range(1, DEPTH):
                z_gather(o, k).start()

    final(1)
    for o in range(OWNERS):
        pl.when(z != owner_z(o))(z_gather(o, 1).wait_recv)

    def gather_copy(k):
        device, _ = peer(*STEPS[k])
        return remote(wch, wfin.at[core, chunk(n)], ag_s.at[k], ag_r.at[k], device)

    for k in range(GROUP - 1):
        gather_copy(k).start()
    wfin[core, chunk(n), :] = wch[...]

    def source(k):
        dx, dy = STEPS[k] if k < GROUP - 1 else (0, 0)
        return peer(-dx, -dy)

    def pass_on(k, half):
        _, m = source(k)
        return remote(
            wfin.at[half, chunk(m)], wfin.at[half, chunk(m)], fw_s.at[k], fw_r.at[k], mate
        )

    pass_on(GROUP - 1, core).start()

    final(0)

    for t in range(2):
        c = first(t)
        for i in (0, 1, 4):
            c[i].wait_send()
        d = second(t)
        for i in (c[2], d[0], d[2]):
            pl.when(has_up)(i.wait_send)
        for i in (c[3], d[1], d[3]):
            pl.when(has_down)(i.wait_send)
        to_mate(t).wait_send()
        to_beyond(t).wait_send()
        for way in range(2):
            for which in range(2):
                pl.when(conds[way])(to_lat(t, way, which).wait_send)
    send_u.wait_send()
    send_att.wait_send()
    for o in range(OWNERS):
        pl.when(z != owner_z(o))(z_copy(o).wait_send)

        @pl.when(z == owner_z(o))
        def _():
            for k in range(1, DEPTH):
                z_gather(o, k).wait_send()

    for k in range(GROUP - 1):
        reduce_copy(k).wait_send()
    for store in stores:
        store.wait()

    for k in reversed(range(GROUP - 1)):
        device, m = source(k)
        remote(wch, wfin.at[core, chunk(m)], ag_s.at[k], ag_r.at[k], device).wait_recv()
        pass_on(k, core).start()
    halves = [
        pltpu.make_async_copy(wfin.at[h], wfin_hbm.at[h], out_s.at[4 + i])
        for i, h in enumerate((core, 1 - core))
    ]
    halves[0].start()
    for k in reversed(range(GROUP)):
        pass_on(k, 1 - core).wait_recv()
    halves[1].start()
    for k in range(GROUP - 1):
        gather_copy(k).wait_send()
    for k in range(GROUP):
        pass_on(k, core).wait_send()
    for half in halves:
        half.wait()


def finish(mixed, dq, dk, dv, wfin, mixed_out, dq_out, dk_out, dv_out, wg_out, *scratch):
    held, narrow, wide, in_s, out_s = scratch
    large = [pltpu.make_async_copy(wfin.at[h], narrow.at[h], in_s.at[h]) for h in range(2)]
    small = [
        pltpu.make_async_copy(src, held.at[i], in_s.at[2 + i])
        for i, src in enumerate((mixed, dq, dk, dv))
    ]
    for copy in large + small:
        copy.start()
    out = []
    for h in range(2):
        rows = pl.ds(h * HALF, HALF)
        large[h].wait()
        for g in range(D // 128):
            wide[rows, g * 128 : g * 128 + 128] = narrow[h, g * HALF : (g + 1) * HALF].astype(F32)
        out.append(pltpu.make_async_copy(wide.at[rows], wg_out.at[rows], out_s.at[h]))
        out[h].start()
    for i, dst in enumerate((mixed_out, dq_out, dk_out, dv_out)):
        small[i].wait()
        out.append(pltpu.make_async_copy(held.at[i], dst, out_s.at[2 + i]))
        out[2 + i].start()
    for copy in out:
        copy.wait()


def on_device(queries, key_vectors, value_vectors, upstream, w_out, neighbours, counts):
    shape = queries.shape
    hbm = pl.BlockSpec(memory_space=pltpu.HBM)
    blocks = jax.ShapeDtypeStruct((2, TOK, D), BF16)
    dma = pltpu.SemaphoreType.DMA
    results = pl.pallas_call(
        kernel,
        out_shape=(
            blocks,
            blocks,
            blocks,
            blocks,
            jax.ShapeDtypeStruct((2, FLAT, 128), BF16),
        ),
        in_specs=[hbm] * 7,
        out_specs=(hbm,) * 5,
        scratch_shapes=[
            pltpu.VMEM((2, TOK, D), BF16),
            pltpu.VMEM((2, TOK, D), BF16),
            pltpu.VMEM((2, TOK, D), BF16),
            pltpu.VMEM((2, TOK, D), BF16),
            pltpu.VMEM((2, FLAT, 128), BF16),
            pltpu.VMEM((2, TOK, D), BF16),
            pltpu.VMEM((D, D), BF16),
            pltpu.SMEM((16, SLOTS, NLON), jnp.int32),
            pltpu.SMEM((16, NLON), jnp.int32),
            pltpu.VMEM((3, 4, TOK, D), BF16),
            pltpu.VMEM((3, 4, TOK, D), BF16),
            pltpu.VMEM((256, D), BF16),
            pltpu.VMEM((128, D), BF16),
            pltpu.VMEM((2, PAIRS, 128, 256), F32),
            pltpu.VMEM((2, 128, HALF), BF16),
            pltpu.VMEM((128, HALF), BF16),
            pltpu.VMEM((HALF, 256), BF16),
            pltpu.VMEM((2, 2, SLOTS + 1, TOK, D), F32),
            pltpu.VMEM((2, 4, TOK, D), BF16),
            pltpu.VMEM((2, 4, TOK, D), BF16),
            pltpu.VMEM((2, 2, 2, TOK, D), BF16),
            pltpu.VMEM((2, 2, 2, TOK, D), BF16),
            pltpu.VMEM((2, 2, TOK, D), BF16),
            pltpu.VMEM((2, 2, TOK, D), BF16),
            pltpu.VMEM((FLAT, 128), BF16),
            pltpu.VMEM((GROUP - 1, CHUNK, 128), BF16),
            pltpu.VMEM((CHUNK, 128), BF16),
            pltpu.VMEM((DEPTH, PIECE, 128), BF16),
            pltpu.VMEM((CHUNK, 128), BF16),
            dma((7,)),
            dma((6,)),
            dma((2, 9)),
            dma((2, 9)),
            dma((2,)),
            dma((2,)),
            dma((2,)),
            dma((2,)),
            dma((2, 2, 2)),
            dma((2, 2, 2)),
            dma((2,)),
            dma((2,)),
            dma((GROUP,)),
            dma((GROUP,)),
            dma((OWNERS,)),
            dma((DEPTH,)),
            dma((DEPTH,)),
            dma((OWNERS,)),
            dma((GROUP,)),
            dma((GROUP,)),
            dma((GROUP,)),
            dma((GROUP,)),
        ],
        compiler_params=pltpu.CompilerParams(
            collective_id=0, has_side_effects=True, vmem_limit_bytes=VMEM
        ),
    )(
        queries.reshape(2, TOK, D),
        key_vectors.reshape(2, TOK, D),
        value_vectors.reshape(2, TOK, D),
        upstream.reshape(2 * TOK, D),
        w_out,
        neighbours.transpose(0, 2, 1),
        counts,
    )
    mixed, dq, dk, dv, wg = pl.pallas_call(
        finish,
        out_shape=(
            blocks,
            blocks,
            blocks,
            blocks,
            jax.ShapeDtypeStruct((D, D), F32),
        ),
        in_specs=[hbm] * 5,
        out_specs=(hbm,) * 5,
        scratch_shapes=[
            pltpu.VMEM((4, 2, TOK, D), BF16),
            pltpu.VMEM((2, FLAT, 128), BF16),
            pltpu.VMEM((D, D), F32),
            dma((6,)),
            dma((6,)),
        ],
        compiler_params=pltpu.CompilerParams(vmem_limit_bytes=VMEM),
    )(*results)
    return (mixed.reshape(shape), dq.reshape(shape), dk.reshape(shape), dv.reshape(shape), wg)


def solution(mesh):
    grid = P("lat", "lon", None)
    return jax.shard_map(
        on_device,
        mesh=mesh,
        in_specs=(grid, grid, grid, grid, P(), P(), P()),
        out_specs=(grid, grid, grid, grid, P()),
        check_vma=False,
    )
```

```python
import math

import jax
import jax.numpy as jnp
from jax import lax
from jax.experimental import pallas as pl
from jax.experimental.pallas import tpu as pltpu
from jax.sharding import PartitionSpec as P

F32 = jnp.float32
BF16 = jnp.bfloat16
MESH = pl.DeviceIdType.MESH

HEAD_DIM = 64
SLOTS = 4
TOK = 64
D = 768
PAIRS = 6
NLON = 32
NLAT = 8
TOKENS = 32768
HALF = D // 2
GROUP = 16
FLAT = HALF * (D // 128)
CHUNK = FLAT // GROUP
OWNERS = 3
PIECE = CHUNK // OWNERS
DEPTH = 8
STEPS = (
    (2, 2), (2, 1), (2, 3), (1, 2), (3, 2), (1, 1), (3, 3), (1, 3), (3, 1), (2, 0), (0, 2), (1, 0),
    (3, 0), (0, 1), (0, 3),
)
VMEM = 58 * 2**20
NT = (((1,), (1,)), ((), ()))
TN = (((0,), (0,)), ((), ()))


def remote(src, dst, send_sem, recv_sem, device):
    return pltpu.make_async_remote_copy(
        src_ref=src,
        dst_ref=dst,
        send_sem=send_sem,
        recv_sem=recv_sem,
        device_id=device,
        device_id_type=MESH,
    )


def kernel(
    q_hbm,
    k_hbm,
    v_hbm,
    u_hbm,
    w_hbm,
    nb_hbm,
    ct_hbm,
    mixed_hbm,
    dq_hbm,
    dk_hbm,
    dv_hbm,
    wfin_hbm,
    mixed_ref,
    dq_ref,
    dk_ref,
    dv_ref,
    wfin,
    q_ref,
    w_ref,
    nb_ref,
    ct_ref,
    kb,
    vb,
    ucat,
    datt,
    probs,
    att2,
    att_in,
    att_t,
    cb,
    gsp,
    grp,
    gsl,
    grl,
    gso,
    gro,
    wbuf,
    rsin,
    zsum,
    zin,
    wch,
    in_s,
    out_s,
    halo_s,
    halo_r,
    u_s,
    u_r,
    gp_s,
    gp_r,
    gl_s,
    gl_r,
    go_s,
    go_r,
    rs_s,
    rs_r,
    z_s,
    z_r,
    zg_s,
    zg_r,
    ag_s,
    ag_r,
    fw_s,
    fw_r,
):
    kvb = (kb, vb)
    a = lax.axis_index("lat")
    b = lax.axis_index("lon")
    core = lax.rem(b, 2)
    ylo = lax.rem(b // 2, 2)
    z = b // 4
    has_up = a > 0
    has_down = a < NLAT - 1
    mate = (a, b + 1 - 2 * core)
    beyond = (a, lax.rem(b + NLON - 1 + 2 * core, NLON))
    seam = (a == NLAT // 2, a == NLAT // 2 - 1)
    near = (has_up & (a != NLAT // 2), has_down & (a != NLAT // 2 - 1))
    up = (a - 1, b)
    down = (a + 1, b)
    oc = 2 * core
    ic = 2 - oc
    chip_x = lax.rem(a, 4)
    chip_y = a // 4 * 2 + ylo
    n = chip_x * 4 + chip_y

    def peer(dx, dy):
        px, py = lax.rem(chip_x + 4 + dx, 4), lax.rem(chip_y + 4 + dy, 4)
        return (py // 2 * 4 + px, z * 4 + lax.rem(py, 2) * 2 + core), px * 4 + py

    def zpeer(zz):
        return (a, zz * 4 + ylo * 2 + core)

    barrier = pltpu.get_barrier_semaphore()

    def greet(device):
        pl.semaphore_signal(barrier, inc=1, device_id=device, device_id_type=MESH)

    for k in (4, 3, 5, 2, 6, 1, 7):
        greet(zpeer(lax.rem(z + k, DEPTH)))
    for step in STEPS:
        greet(peer(*step)[0])
    greet(beyond)
    greet(mate)
    own_u = ucat.at[pl.ds(0, 128)]
    loads = [
        pltpu.make_async_copy(src, dst, in_s.at[i])
        for i, (src, dst) in enumerate(
            (
                (u_hbm, own_u),
                (w_hbm, w_ref),
                (k_hbm, kvb[0].at[1, pl.ds(1, 2)]),
                (v_hbm, kvb[1].at[1, pl.ds(1, 2)]),
                (q_hbm, q_ref),
                (nb_hbm, nb_ref),
                (ct_hbm, ct_ref),
            )
        )
    ]
    for load in loads:
        load.start()
    pl.semaphore_wait(barrier, 2 + GROUP - 1 + DEPTH - 1)

    stores = [
        pltpu.make_async_copy(src, dst, out_s.at[i])
        for i, (src, dst) in enumerate(
            (
                (mixed_ref, mixed_hbm),
                (dq_ref, dq_hbm),
                (dk_ref, dk_hbm),
                (dv_ref, dv_hbm),
            )
        )
    ]

    def halo(t, i, src, dst, device):
        return remote(src, dst, halo_s.at[t, i], halo_r.at[t, i], device)

    ins = (k_hbm, v_hbm)

    def first(t):
        src = ins[t]
        return (
            halo(t, 1, src.at[0], kvb[t].at[ic, 1], beyond),
            halo(t, 8, src.at[1], kvb[t].at[ic, 2], beyond),
            halo(t, 2, src.at[0], kvb[t].at[1, 3], up),
            halo(t, 3, src.at[1], kvb[t].at[1, 0], down),
            halo(t, 0, src, kvb[t].at[oc, pl.ds(1, 2)], mate),
        )

    def second(t):
        return (
            halo(t, 4, kvb[t].at[oc, 1], kvb[t].at[oc, 3], up),
            halo(t, 5, kvb[t].at[oc, 2], kvb[t].at[oc, 0], down),
            halo(t, 6, kvb[t].at[1, 0], kvb[t].at[oc, 0], mate),
            halo(t, 7, kvb[t].at[1, 3], kvb[t].at[oc, 3], mate),
            remote(kvb[t].at[1, 0], kvb[t].at[ic, 0], halo_s.at[t, 4], halo_r.at[t, 5], beyond),
            remote(kvb[t].at[1, 3], kvb[t].at[ic, 3], halo_s.at[t, 5], halo_r.at[t, 4], beyond),
        )

    for t in range(2):
        c = first(t)
        c[0].start()
        pl.when(has_up)(c[2].start)
        c[1].start()
        pl.when(has_down)(c[3].start)
        c[4].start()
    send_u = remote(u_hbm, ucat.at[pl.ds(128, 128)], u_s.at[0], u_r.at[0], mate)
    send_u.start()

    loads[0].wait()
    loads[1].wait()
    datt[...] = lax.dot_general(
        own_u[...], w_ref[...], NT, preferred_element_type=F32
    ).astype(BF16)
    for t in range(2):
        for s in range(2):
            cb[t, s, SLOTS] = jnp.zeros((TOK, D), F32)

    for load in loads[2:]:
        load.wait()
    for t in range(2):
        c = second(t)

        @pl.when(has_up)
        def _():
            halo(t, 3, k_hbm.at[0], kvb[t].at[1, 0], up).wait_recv()
            pl.when(seam[0])(c[4].start)
            c[2].start()

        @pl.when(has_down)
        def _():
            halo(t, 2, k_hbm.at[0], kvb[t].at[1, 3], down).wait_recv()
            pl.when(seam[1])(c[5].start)
            c[3].start()

        halo(t, 1, k_hbm.at[0], kvb[t].at[oc, 1], beyond).wait_recv()
        pl.when(near[0])(c[0].start)
        halo(t, 8, k_hbm.at[0], kvb[t].at[oc, 2], beyond).wait_recv()
        pl.when(near[1])(c[1].start)

    def complete(t):
        halo(t, 0, k_hbm, kvb[t].at[ic, pl.ds(1, 2)], mate).wait_recv()

        @pl.when(has_up)
        def _():
            halo(t, 6, k_hbm.at[0], kvb[t].at[ic, 0], mate).wait_recv()
            halo(t, 5, k_hbm.at[0], kvb[t].at[oc, 0], up).wait_recv()

        @pl.when(has_down)
        def _():
            halo(t, 7, k_hbm.at[0], kvb[t].at[ic, 3], mate).wait_recv()
            halo(t, 4, k_hbm.at[0], kvb[t].at[oc, 3], down).wait_recv()

    def places(s_block):
        i = 2 * a + s_block
        out = []
        for s in range(SLOTS):
            name = nb_ref[i, s, b]
            row = lax.div(name, NLON) - i + 1
            col = lax.rem(lax.rem(name, NLON) - b + 1 + NLON, NLON)
            out.append((jnp.clip(col, 0, 2), jnp.clip(row, 0, 2)))
        return out, ct_ref[i, b]

    def blocks_of(t, place, s_block, j):
        return jnp.concatenate(
            [kvb[t][col, row + s_block, :, pl.ds(j * 128, 128)] for col, row in place], axis=0
        )

    low = lax.broadcasted_iota(jnp.int32, (TOK, 128), 1) < HEAD_DIM

    def stacked(x):
        zero = jnp.zeros_like(x)
        return jnp.concatenate([jnp.where(low, x, zero), jnp.where(low, zero, x)], axis=0)

    def queries_of(s_block, j):
        x = q_ref[s_block, :, pl.ds(j * 128, 128)]
        return stacked(x * jnp.asarray(0.125, BF16))

    def unstacked(x):
        return jnp.where(low, x[:TOK], x[TOK:])

    placed = [places(s) for s in range(2)]

    def slot_of(s, row, col):
        slot = jnp.int32(SLOTS)
        place, count = placed[s]
        for i in range(SLOTS):
            hit = (place[i][0] == col) & (place[i][1] == row) & (i < count)
            slot = jnp.where(hit, i, slot)
        return slot

    def terms(t, col, row):
        total = None
        for s in range(2):
            if 0 <= row - s <= 2:
                x = cb[t, s, slot_of(s, row - s, col)]
                total = x if total is None else total + x
        return total

    def to_mate(t):
        return remote(gsp.at[t], grp.at[t], gp_s.at[t], gp_r.at[t], mate)

    def to_lat(t, way, which):
        device = (up, down)[way]
        return remote(
            gsl.at[t, way, which],
            grl.at[t, way, which],
            gl_s.at[t, way, which],
            gl_r.at[t, way, which],
            device,
        )

    def over_seam(t, way):
        return remote(
            gsl.at[t, way, 0],
            grl.at[t, 1 - way, 0],
            gl_s.at[t, way, 0],
            gl_r.at[t, 1 - way, 0],
            beyond,
        )

    def to_beyond(t):
        return remote(gso.at[t], gro.at[t], go_s.at[t], go_r.at[t], beyond)

    conds = (has_up, has_down)

    def send_outer(t):
        for way in range(2):

            @pl.when(conds[way])
            def _():
                gsl[t, way, 0] = terms(t, oc, 3 * way).astype(BF16)

            pl.when(near[way])(to_lat(t, way, 0).start)
            pl.when(seam[way])(over_seam(t, way).start)

    def send_mate(t):
        for r in range(4):
            gsp[t, r] = terms(t, ic, r).astype(BF16)
        to_mate(t).start()

    def send_beyond(t):
        for r in range(2):

            @pl.when(near[r])
            def _():
                to_lat(t, 1 - r, 0).wait_recv()
                gso[t, r] = (terms(t, oc, 1 + r) + grl[t, 1 - r, 0].astype(F32)).astype(BF16)

            @pl.when(jnp.logical_not(near[r]))
            def _():
                gso[t, r] = terms(t, oc, 1 + r).astype(BF16)

        to_beyond(t).start()

    def send_own(t):
        to_mate(t).wait_recv()
        for way in range(2):

            @pl.when(near[way])
            def _():
                total = terms(t, 1, 3 * way) + grp[t, 3 * way].astype(F32)
                gsl[t, way, 1] = total.astype(BF16)

            @pl.when(seam[way])
            def _():
                over_seam(t, way).wait_recv()
                total = terms(t, 1, 3 * way) + grp[t, 3 * way].astype(F32)
                gsl[t, way, 1] = (total + grl[t, 1 - way, 0].astype(F32)).astype(BF16)

            pl.when(conds[way])(to_lat(t, way, 1).start)

    def final(t):
        out = (dk_ref, dv_ref)[t]
        to_beyond(t).wait_recv()
        for r in range(2):

            def total():
                return terms(t, 1, 1 + r) + grp[t, 1 + r].astype(F32) + gro[t, r].astype(F32)

            @pl.when(conds[r])
            def _():
                to_lat(t, 1 - r, 1).wait_recv()
                out[r] = (total() + grl[t, 1 - r, 1].astype(F32)).astype(BF16)

            @pl.when(jnp.logical_not(conds[r]))
            def _():
                out[r] = total().astype(BF16)

        stores[2 + t].start()

    complete(0)

    @pl.loop(0, 2)
    def _(s):
        place, count = places(s)
        kept = lax.broadcasted_iota(jnp.int32, (2 * TOK, SLOTS * TOK), 1) < count * TOK
        rows = pl.ds(pl.multiple_of(s * TOK, TOK), TOK)
        scores = []
        for j in range(PAIRS):
            scores.append(
                lax.dot_general(
                    queries_of(s, j), blocks_of(0, place, s, j), NT, preferred_element_type=F32
                )
            )
        for j in range(PAIRS):
            masked = jnp.where(kept, scores[j], -1e30)
            top = jnp.max(masked, axis=-1, keepdims=True)
            e = jnp.exp(masked - top)
            probs[s, j] = e * (1.0 / jnp.sum(e, axis=-1, keepdims=True))
        for j in range(PAIRS):
            lanes = pl.ds(j * 128, 128)
            dv = lax.dot_general(
                probs[s, j].astype(BF16),
                stacked(datt[rows, lanes]),
                TN,
                preferred_element_type=F32,
            )
            for i in range(SLOTS):
                cb[1, s, i, :, lanes] = dv[i * TOK : (i + 1) * TOK]

    send_outer(1)
    send_mate(1)
    complete(1)

    def send_att(s):
        rows = pl.ds(pl.multiple_of(s * TOK, TOK), TOK)
        return remote(
            att2.at[1 - core, rows], att_in.at[rows], u_s.at[1 + s], u_r.at[1 + s], mate
        )

    @pl.loop(0, 2)
    def _(s):
        place, _ = places(s)
        rows = pl.ds(pl.multiple_of(s * TOK, TOK), TOK)
        for j in range(PAIRS):
            o = jnp.dot(
                probs[s, j].astype(BF16), blocks_of(1, place, s, j), preferred_element_type=F32
            )
            att2[j // 3, rows, (j % 3) * 128 : (j % 3) * 128 + 128] = unstacked(o).astype(BF16)
        send_att(s).start()

    att_t[:, 0:128] = att2[core].T
    remote(u_hbm, ucat.at[pl.ds(128, 128)], u_s.at[0], u_r.at[0], mate).wait_recv()
    for s in range(2):
        send_att(s).wait_recv()
    att_t[:, 128:256] = att_in[...].T
    for g in range(3):
        term = jnp.dot(
            att_t[...], ucat[:, g * 256 : g * 256 + 256], preferred_element_type=F32
        ).astype(BF16)
        wbuf[2 * g * HALF : (2 * g + 1) * HALF] = term[:, :128]
        wbuf[(2 * g + 1) * HALF : (2 * g + 2) * HALF] = term[:, 128:]

    def chunk(m):
        return pl.ds(pl.multiple_of(m * CHUNK, 16), CHUNK)

    def reduce_copy(k):
        device, m = peer(*STEPS[k])
        return remote(wbuf.at[chunk(m)], rsin.at[k], rs_s.at[k], rs_r.at[k], device)

    for k in range(GROUP - 1):
        reduce_copy(k).start()

    att = jnp.concatenate([att2[0], att2[1]], axis=1)
    mixed = jnp.dot(att, w_ref[...], preferred_element_type=F32).astype(BF16)
    mixed_ref[0] = mixed[:TOK]
    mixed_ref[1] = mixed[TOK:]
    stores[0].start()
    send_beyond(1)
    send_own(1)

    @pl.loop(0, 2)
    def _(s):
        place, _ = places(s)
        rows = pl.ds(pl.multiple_of(s * TOK, TOK), TOK)
        for j in range(PAIRS):
            lanes = pl.ds(j * 128, 128)
            qs = queries_of(s, j)
            ks = blocks_of(0, place, s, j)
            vs = blocks_of(1, place, s, j)
            da = stacked(datt[rows, lanes])
            at = att2[j // 3, rows, (j % 3) * 128 : (j % 3) * 128 + 128]
            at = jnp.concatenate([at, at], axis=0)
            delta = jnp.sum(da.astype(F32) * at.astype(F32), axis=-1, keepdims=True)
            p = probs[s, j]
            dp = lax.dot_general(da, vs, NT, preferred_element_type=F32)
            ds = (p * (dp - delta)).astype(BF16)
            dq = unstacked(jnp.dot(ds, ks, preferred_element_type=F32)) * 0.125
            dq_ref[s, :, lanes] = dq.astype(BF16)
            dk = lax.dot_general(ds, qs, TN, preferred_element_type=F32)
            for i in range(SLOTS):
                cb[0, s, i, :, lanes] = dk[i * TOK : (i + 1) * TOK]

    stores[1].start()
    send_outer(0)
    send_mate(0)

    total = wbuf[chunk(n), :].astype(F32)
    for k in reversed(range(GROUP - 1)):
        reduce_copy(k).wait_recv()
        total = total + rsin[k].astype(F32)
    zsum[...] = total.astype(BF16)

    def owner_z(o):
        return 3 * o

    def z_copy(o):
        k = lax.rem(owner_z(o) - z + DEPTH, DEPTH)
        return remote(
            zsum.at[pl.ds(o * PIECE, PIECE)], zin.at[k], z_s.at[o], z_r.at[k], zpeer(owner_z(o))
        )

    for o in range(OWNERS):
        pl.when(z != owner_z(o))(z_copy(o).start)
    send_beyond(0)
    send_own(0)

    def z_gather(o, k):
        return remote(
            wch.at[pl.ds(o * PIECE, PIECE)],
            wch.at[pl.ds(o * PIECE, PIECE)],
            zg_s.at[k],
            zg_r.at[o],
            zpeer(lax.rem(owner_z(o) + k, DEPTH)),
        )

    for o in range(OWNERS):

        @pl.when(z == owner_z(o))
        def _():
            acc = zsum[o * PIECE : (o + 1) * PIECE].astype(F32)
            for k in range(1, DEPTH):
                remote(
                    zsum.at[pl.ds(o * PIECE, PIECE)],
                    zin.at[k],
                    z_s.at[o],
                    z_r.at[k],
                    zpeer(lax.rem(z + DEPTH - k, DEPTH)),
                ).wait_recv()
                acc = acc + zin[k].astype(F32)
            wch[o * PIECE : (o + 1) * PIECE] = (acc * (1.0 / math.sqrt(TOKENS))).astype(BF16)
            for k in range(1, DEPTH):
                z_gather(o, k).start()

    final(1)
    for o in range(OWNERS):
        pl.when(z != owner_z(o))(z_gather(o, 1).wait_recv)

    def gather_copy(k):
        device, _ = peer(*STEPS[k])
        return remote(wch, wfin.at[core, chunk(n)], ag_s.at[k], ag_r.at[k], device)

    for k in range(GROUP - 1):
        gather_copy(k).start()
    wfin[core, chunk(n), :] = wch[...]

    def source(k):
        dx, dy = STEPS[k] if k < GROUP - 1 else (0, 0)
        return peer(-dx, -dy)

    def pass_on(k, half):
        _, m = source(k)
        return remote(
            wfin.at[half, chunk(m)], wfin.at[half, chunk(m)], fw_s.at[k], fw_r.at[k], mate
        )

    pass_on(GROUP - 1, core).start()

    final(0)

    for t in range(2):
        c = first(t)
        for i in (0, 1, 4):
            c[i].wait_send()
        d = second(t)
        for i in (c[2], d[0], d[2]):
            pl.when(has_up)(i.wait_send)
        for i in (c[3], d[1], d[3]):
            pl.when(has_down)(i.wait_send)
        to_mate(t).wait_send()
        to_beyond(t).wait_send()
        for way in range(2):
            for which in range(2):
                pl.when(conds[way])(to_lat(t, way, which).wait_send)
    send_u.wait_send()
    for s in range(2):
        send_att(s).wait_send()
    for o in range(OWNERS):
        pl.when(z != owner_z(o))(z_copy(o).wait_send)

        @pl.when(z == owner_z(o))
        def _():
            for k in range(1, DEPTH):
                z_gather(o, k).wait_send()

    for k in range(GROUP - 1):
        reduce_copy(k).wait_send()
    for store in stores:
        store.wait()

    for k in reversed(range(GROUP - 1)):
        device, m = source(k)
        remote(wch, wfin.at[core, chunk(m)], ag_s.at[k], ag_r.at[k], device).wait_recv()
        pass_on(k, core).start()
    halves = [
        pltpu.make_async_copy(wfin.at[h], wfin_hbm.at[h], out_s.at[4 + i])
        for i, h in enumerate((core, 1 - core))
    ]
    halves[0].start()
    for k in reversed(range(GROUP)):
        pass_on(k, 1 - core).wait_recv()
    halves[1].start()
    for k in range(GROUP - 1):
        gather_copy(k).wait_send()
    for k in range(GROUP):
        pass_on(k, core).wait_send()
    for half in halves:
        half.wait()


def finish(mixed, dq, dk, dv, wfin, mixed_out, dq_out, dk_out, dv_out, wg_out, *scratch):
    held, narrow, wide, in_s, out_s = scratch
    large = [pltpu.make_async_copy(wfin.at[h], narrow.at[h], in_s.at[h]) for h in range(2)]
    small = [
        pltpu.make_async_copy(src, held.at[i], in_s.at[2 + i])
        for i, src in enumerate((mixed, dq, dk, dv))
    ]
    for copy in large + small:
        copy.start()
    out = []
    for h in range(2):
        rows = pl.ds(h * HALF, HALF)
        large[h].wait()
        for g in range(D // 128):
            wide[rows, g * 128 : g * 128 + 128] = narrow[h, g * HALF : (g + 1) * HALF].astype(F32)
        out.append(pltpu.make_async_copy(wide.at[rows], wg_out.at[rows], out_s.at[h]))
        out[h].start()
    for i, dst in enumerate((mixed_out, dq_out, dk_out, dv_out)):
        small[i].wait()
        out.append(pltpu.make_async_copy(held.at[i], dst, out_s.at[2 + i]))
        out[2 + i].start()
    for copy in out:
        copy.wait()


def on_device(queries, key_vectors, value_vectors, upstream, w_out, neighbours, counts):
    shape = queries.shape
    hbm = pl.BlockSpec(memory_space=pltpu.HBM)
    blocks = jax.ShapeDtypeStruct((2, TOK, D), BF16)
    dma = pltpu.SemaphoreType.DMA
    results = pl.pallas_call(
        kernel,
        out_shape=(
            blocks,
            blocks,
            blocks,
            blocks,
            jax.ShapeDtypeStruct((2, FLAT, 128), BF16),
        ),
        in_specs=[hbm] * 7,
        out_specs=(hbm,) * 5,
        scratch_shapes=[
            pltpu.VMEM((2, TOK, D), BF16),
            pltpu.VMEM((2, TOK, D), BF16),
            pltpu.VMEM((2, TOK, D), BF16),
            pltpu.VMEM((2, TOK, D), BF16),
            pltpu.VMEM((2, FLAT, 128), BF16),
            pltpu.VMEM((2, TOK, D), BF16),
            pltpu.VMEM((D, D), BF16),
            pltpu.SMEM((16, SLOTS, NLON), jnp.int32),
            pltpu.SMEM((16, NLON), jnp.int32),
            pltpu.VMEM((3, 4, TOK, D), BF16),
            pltpu.VMEM((3, 4, TOK, D), BF16),
            pltpu.VMEM((256, D), BF16),
            pltpu.VMEM((128, D), BF16),
            pltpu.VMEM((2, PAIRS, 128, 256), F32),
            pltpu.VMEM((2, 128, HALF), BF16),
            pltpu.VMEM((128, HALF), BF16),
            pltpu.VMEM((HALF, 256), BF16),
            pltpu.VMEM((2, 2, SLOTS + 1, TOK, D), F32),
            pltpu.VMEM((2, 4, TOK, D), BF16),
            pltpu.VMEM((2, 4, TOK, D), BF16),
            pltpu.VMEM((2, 2, 2, TOK, D), BF16),
            pltpu.VMEM((2, 2, 2, TOK, D), BF16),
            pltpu.VMEM((2, 2, TOK, D), BF16),
            pltpu.VMEM((2, 2, TOK, D), BF16),
            pltpu.VMEM((FLAT, 128), BF16),
            pltpu.VMEM((GROUP - 1, CHUNK, 128), BF16),
            pltpu.VMEM((CHUNK, 128), BF16),
            pltpu.VMEM((DEPTH, PIECE, 128), BF16),
            pltpu.VMEM((CHUNK, 128), BF16),
            dma((7,)),
            dma((6,)),
            dma((2, 9)),
            dma((2, 9)),
            dma((3,)),
            dma((3,)),
            dma((2,)),
            dma((2,)),
            dma((2, 2, 2)),
            dma((2, 2, 2)),
            dma((2,)),
            dma((2,)),
            dma((GROUP,)),
            dma((GROUP,)),
            dma((OWNERS,)),
            dma((DEPTH,)),
            dma((DEPTH,)),
            dma((OWNERS,)),
            dma((GROUP,)),
            dma((GROUP,)),
            dma((GROUP,)),
            dma((GROUP,)),
        ],
        compiler_params=pltpu.CompilerParams(
            collective_id=0, has_side_effects=True, vmem_limit_bytes=VMEM
        ),
    )(
        queries.reshape(2, TOK, D),
        key_vectors.reshape(2, TOK, D),
        value_vectors.reshape(2, TOK, D),
        upstream.reshape(2 * TOK, D),
        w_out,
        neighbours.transpose(0, 2, 1),
        counts,
    )
    mixed, dq, dk, dv, wg = pl.pallas_call(
        finish,
        out_shape=(
            blocks,
            blocks,
            blocks,
            blocks,
            jax.ShapeDtypeStruct((D, D), F32),
        ),
        in_specs=[hbm] * 5,
        out_specs=(hbm,) * 5,
        scratch_shapes=[
            pltpu.VMEM((4, 2, TOK, D), BF16),
            pltpu.VMEM((2, FLAT, 128), BF16),
            pltpu.VMEM((D, D), F32),
            dma((6,)),
            dma((6,)),
        ],
        compiler_params=pltpu.CompilerParams(vmem_limit_bytes=VMEM),
    )(*results)
    return (mixed.reshape(shape), dq.reshape(shape), dk.reshape(shape), dv.reshape(shape), wg)


def solution(mesh):
    grid = P("lat", "lon", None)
    return jax.shard_map(
        on_device,
        mesh=mesh,
        in_specs=(grid, grid, grid, grid, P(), P(), P()),
        out_specs=(grid, grid, grid, grid, P()),
        check_vma=False,
    )
```

```python
import math

import jax
import jax.numpy as jnp
from jax import lax
from jax.experimental import pallas as pl
from jax.experimental.pallas import tpu as pltpu
from jax.sharding import PartitionSpec as P

F32 = jnp.float32
BF16 = jnp.bfloat16
MESH = pl.DeviceIdType.MESH

HEAD_DIM = 64
SLOTS = 4
TOK = 64
D = 768
PAIRS = 6
NLON = 32
NLAT = 8
TOKENS = 32768
HALF = D // 2
GROUP = 16
FLAT = HALF * (D // 128)
CHUNK = FLAT // GROUP
OWNERS = 3
PIECE = CHUNK // OWNERS
DEPTH = 8
STEPS = (
    (2, 2), (2, 1), (2, 3), (1, 2), (3, 2), (1, 1), (3, 3), (1, 3), (3, 1), (2, 0), (0, 2), (1, 0),
    (3, 0), (0, 1), (0, 3),
)
VMEM = 58 * 2**20
NT = (((1,), (1,)), ((), ()))
TN = (((0,), (0,)), ((), ()))


def remote(src, dst, send_sem, recv_sem, device):
    return pltpu.make_async_remote_copy(
        src_ref=src,
        dst_ref=dst,
        send_sem=send_sem,
        recv_sem=recv_sem,
        device_id=device,
        device_id_type=MESH,
    )


def kernel(
    q_hbm,
    k_hbm,
    v_hbm,
    u_hbm,
    w_hbm,
    nb_hbm,
    ct_hbm,
    mixed_hbm,
    dq_hbm,
    dk_hbm,
    dv_hbm,
    wfin_hbm,
    mixed_ref,
    dq_ref,
    dk_ref,
    dv_ref,
    wfin,
    q_ref,
    w_ref,
    nb_ref,
    ct_ref,
    kb,
    vb,
    ucat,
    datt,
    probs,
    att2,
    att_in,
    att_t,
    cb,
    gsp,
    grp,
    gsl,
    grl,
    gso,
    gro,
    wbuf,
    rsin,
    zsum,
    zin,
    wch,
    in_s,
    out_s,
    halo_s,
    halo_r,
    u_s,
    u_r,
    gp_s,
    gp_r,
    gl_s,
    gl_r,
    go_s,
    go_r,
    rs_s,
    rs_r,
    z_s,
    z_r,
    zg_s,
    zg_r,
    ag_s,
    ag_r,
    fw_s,
    fw_r,
):
    kvb = (kb, vb)
    a = lax.axis_index("lat")
    b = lax.axis_index("lon")
    core = lax.rem(b, 2)
    ylo = lax.rem(b // 2, 2)
    z = b // 4
    has_up = a > 0
    has_down = a < NLAT - 1
    mate = (a, b + 1 - 2 * core)
    beyond = (a, lax.rem(b + NLON - 1 + 2 * core, NLON))
    seam = (a == NLAT // 2, a == NLAT // 2 - 1)
    near = (has_up & (a != NLAT // 2), has_down & (a != NLAT // 2 - 1))
    up = (a - 1, b)
    down = (a + 1, b)
    oc = 2 * core
    ic = 2 - oc
    chip_x = lax.rem(a, 4)
    chip_y = a // 4 * 2 + ylo
    n = chip_x * 4 + chip_y

    def peer(dx, dy):
        px, py = lax.rem(chip_x + 4 + dx, 4), lax.rem(chip_y + 4 + dy, 4)
        return (py // 2 * 4 + px, z * 4 + lax.rem(py, 2) * 2 + core), px * 4 + py

    def zpeer(zz):
        return (a, zz * 4 + ylo * 2 + core)

    barrier = pltpu.get_barrier_semaphore()

    def greet(device):
        pl.semaphore_signal(barrier, inc=1, device_id=device, device_id_type=MESH)

    own_u = ucat.at[pl.ds(0, 128)]
    loads = [
        pltpu.make_async_copy(src, dst, in_s.at[i])
        for i, (src, dst) in enumerate(
            (
                (u_hbm, own_u),
                (w_hbm, w_ref),
                (k_hbm, kvb[0].at[1, pl.ds(1, 2)]),
                (v_hbm, kvb[1].at[1, pl.ds(1, 2)]),
                (q_hbm, q_ref),
                (nb_hbm, nb_ref),
                (ct_hbm, ct_ref),
            )
        )
    ]
    for load in loads:
        load.start()

    is_owner = lax.rem(z, 3) == 0
    for k in (4, 3, 5, 2, 6, 1, 7):
        other = lax.rem(z + k, DEPTH)

        @pl.when(is_owner | (lax.rem(other, 3) == 0))
        def _():
            greet(zpeer(other))

    for step in STEPS:
        greet(peer(*step)[0])
    greet(beyond)
    greet(mate)
    pl.semaphore_wait(barrier, 2 + GROUP - 1 + jnp.where(is_owner, DEPTH - 1, OWNERS))

    stores = [
        pltpu.make_async_copy(src, dst, out_s.at[i])
        for i, (src, dst) in enumerate(
            (
                (mixed_ref, mixed_hbm),
                (dq_ref, dq_hbm),
                (dk_ref, dk_hbm),
                (dv_ref, dv_hbm),
            )
        )
    ]

    def halo(t, i, src, dst, device):
        return remote(src, dst, halo_s.at[t, i], halo_r.at[t, i], device)

    ins = (k_hbm, v_hbm)

    def first(t):
        src = ins[t]
        return (
            halo(t, 1, src.at[0], kvb[t].at[ic, 1], beyond),
            halo(t, 8, src.at[1], kvb[t].at[ic, 2], beyond),
            halo(t, 2, src.at[0], kvb[t].at[1, 3], up),
            halo(t, 3, src.at[1], kvb[t].at[1, 0], down),
            halo(t, 0, src, kvb[t].at[oc, pl.ds(1, 2)], mate),
        )

    def second(t):
        return (
            halo(t, 4, kvb[t].at[oc, 1], kvb[t].at[oc, 3], up),
            halo(t, 5, kvb[t].at[oc, 2], kvb[t].at[oc, 0], down),
            halo(t, 6, kvb[t].at[1, 0], kvb[t].at[oc, 0], mate),
            halo(t, 7, kvb[t].at[1, 3], kvb[t].at[oc, 3], mate),
            remote(kvb[t].at[1, 0], kvb[t].at[ic, 0], halo_s.at[t, 4], halo_r.at[t, 5], beyond),
            remote(kvb[t].at[1, 3], kvb[t].at[ic, 3], halo_s.at[t, 5], halo_r.at[t, 4], beyond),
        )

    for t in range(2):
        c = first(t)
        c[0].start()
        pl.when(has_up)(c[2].start)
        c[1].start()
        pl.when(has_down)(c[3].start)
        c[4].start()
    send_u = remote(u_hbm, ucat.at[pl.ds(128, 128)], u_s.at[0], u_r.at[0], mate)
    send_u.start()

    loads[0].wait()
    loads[1].wait()
    datt[...] = lax.dot_general(
        own_u[...], w_ref[...], NT, preferred_element_type=F32
    ).astype(BF16)
    for t in range(2):
        for s in range(2):
            cb[t, s, SLOTS] = jnp.zeros((TOK, D), F32)

    for load in loads[2:]:
        load.wait()
    for t in range(2):
        c = second(t)

        @pl.when(has_up)
        def _():
            halo(t, 3, k_hbm.at[0], kvb[t].at[1, 0], up).wait_recv()
            pl.when(seam[0])(c[4].start)
            c[2].start()

        @pl.when(has_down)
        def _():
            halo(t, 2, k_hbm.at[0], kvb[t].at[1, 3], down).wait_recv()
            pl.when(seam[1])(c[5].start)
            c[3].start()

        halo(t, 1, k_hbm.at[0], kvb[t].at[oc, 1], beyond).wait_recv()
        pl.when(near[0])(c[0].start)
        halo(t, 8, k_hbm.at[0], kvb[t].at[oc, 2], beyond).wait_recv()
        pl.when(near[1])(c[1].start)

    def complete(t):
        halo(t, 0, k_hbm, kvb[t].at[ic, pl.ds(1, 2)], mate).wait_recv()

        @pl.when(has_up)
        def _():
            halo(t, 6, k_hbm.at[0], kvb[t].at[ic, 0], mate).wait_recv()
            halo(t, 5, k_hbm.at[0], kvb[t].at[oc, 0], up).wait_recv()

        @pl.when(has_down)
        def _():
            halo(t, 7, k_hbm.at[0], kvb[t].at[ic, 3], mate).wait_recv()
            halo(t, 4, k_hbm.at[0], kvb[t].at[oc, 3], down).wait_recv()

    def places(s_block):
        i = 2 * a + s_block
        out = []
        for s in range(SLOTS):
            name = nb_ref[i, s, b]
            row = lax.div(name, NLON) - i + 1
            col = lax.rem(lax.rem(name, NLON) - b + 1 + NLON, NLON)
            out.append((jnp.clip(col, 0, 2), jnp.clip(row, 0, 2)))
        return out, ct_ref[i, b]

    def blocks_of(t, place, s_block, j):
        return jnp.concatenate(
            [kvb[t][col, row + s_block, :, pl.ds(j * 128, 128)] for col, row in place], axis=0
        )

    low = lax.broadcasted_iota(jnp.int32, (TOK, 128), 1) < HEAD_DIM

    def stacked(x):
        zero = jnp.zeros_like(x)
        return jnp.concatenate([jnp.where(low, x, zero), jnp.where(low, zero, x)], axis=0)

    def queries_of(s_block, j):
        x = q_ref[s_block, :, pl.ds(j * 128, 128)]
        return stacked(x * jnp.asarray(0.125, BF16))

    def unstacked(x):
        return jnp.where(low, x[:TOK], x[TOK:])

    placed = [places(s) for s in range(2)]

    def slot_of(s, row, col):
        slot = jnp.int32(SLOTS)
        place, count = placed[s]
        for i in range(SLOTS):
            hit = (place[i][0] == col) & (place[i][1] == row) & (i < count)
            slot = jnp.where(hit, i, slot)
        return slot

    def terms(t, col, row):
        total = None
        for s in range(2):
            if 0 <= row - s <= 2:
                x = cb[t, s, slot_of(s, row - s, col)]
                total = x if total is None else total + x
        return total

    def to_mate(t):
        return remote(gsp.at[t], grp.at[t], gp_s.at[t], gp_r.at[t], mate)

    def to_lat(t, way, which):
        device = (up, down)[way]
        return remote(
            gsl.at[t, way, which],
            grl.at[t, way, which],
            gl_s.at[t, way, which],
            gl_r.at[t, way, which],
            device,
        )

    def over_seam(t, way):
        return remote(
            gsl.at[t, way, 0],
            grl.at[t, 1 - way, 0],
            gl_s.at[t, way, 0],
            gl_r.at[t, 1 - way, 0],
            beyond,
        )

    def to_beyond(t):
        return remote(gso.at[t], gro.at[t], go_s.at[t], go_r.at[t], beyond)

    conds = (has_up, has_down)

    def send_outer(t):
        for way in range(2):

            @pl.when(conds[way])
            def _():
                gsl[t, way, 0] = terms(t, oc, 3 * way).astype(BF16)

            pl.when(near[way])(to_lat(t, way, 0).start)
            pl.when(seam[way])(over_seam(t, way).start)

    def send_mate(t):
        for r in range(4):
            gsp[t, r] = terms(t, ic, r).astype(BF16)
        to_mate(t).start()

    def send_beyond(t):
        for r in range(2):

            @pl.when(near[r])
            def _():
                to_lat(t, 1 - r, 0).wait_recv()
                gso[t, r] = (terms(t, oc, 1 + r) + grl[t, 1 - r, 0].astype(F32)).astype(BF16)

            @pl.when(jnp.logical_not(near[r]))
            def _():
                gso[t, r] = terms(t, oc, 1 + r).astype(BF16)

        to_beyond(t).start()

    def send_own(t):
        to_mate(t).wait_recv()
        for way in range(2):

            @pl.when(near[way])
            def _():
                total = terms(t, 1, 3 * way) + grp[t, 3 * way].astype(F32)
                gsl[t, way, 1] = total.astype(BF16)

            @pl.when(seam[way])
            def _():
                over_seam(t, way).wait_recv()
                total = terms(t, 1, 3 * way) + grp[t, 3 * way].astype(F32)
                gsl[t, way, 1] = (total + grl[t, 1 - way, 0].astype(F32)).astype(BF16)

            pl.when(conds[way])(to_lat(t, way, 1).start)

    def final(t):
        out = (dk_ref, dv_ref)[t]
        to_beyond(t).wait_recv()
        for r in range(2):

            def total():
                return terms(t, 1, 1 + r) + grp[t, 1 + r].astype(F32) + gro[t, r].astype(F32)

            @pl.when(conds[r])
            def _():
                to_lat(t, 1 - r, 1).wait_recv()
                out[r] = (total() + grl[t, 1 - r, 1].astype(F32)).astype(BF16)

            @pl.when(jnp.logical_not(conds[r]))
            def _():
                out[r] = total().astype(BF16)

        stores[2 + t].start()

    complete(0)

    @pl.loop(0, 2)
    def _(s):
        place, count = places(s)
        kept = lax.broadcasted_iota(jnp.int32, (2 * TOK, SLOTS * TOK), 1) < count * TOK
        rows = pl.ds(pl.multiple_of(s * TOK, TOK), TOK)
        scores = []
        for j in range(PAIRS):
            scores.append(
                lax.dot_general(
                    queries_of(s, j), blocks_of(0, place, s, j), NT, preferred_element_type=F32
                )
            )
        for j in range(PAIRS):
            masked = jnp.where(kept, scores[j], -1e30)
            top = jnp.max(masked, axis=-1, keepdims=True)
            e = jnp.exp(masked - top)
            probs[s, j] = e * (1.0 / jnp.sum(e, axis=-1, keepdims=True))
        for j in range(PAIRS):
            lanes = pl.ds(j * 128, 128)
            dv = lax.dot_general(
                probs[s, j].astype(BF16),
                stacked(datt[rows, lanes]),
                TN,
                preferred_element_type=F32,
            )
            for i in range(SLOTS):
                cb[1, s, i, :, lanes] = dv[i * TOK : (i + 1) * TOK]

    send_outer(1)
    send_mate(1)
    complete(1)

    def send_att(s):
        rows = pl.ds(pl.multiple_of(s * TOK, TOK), TOK)
        return remote(
            att2.at[1 - core, rows], att_in.at[rows], u_s.at[1 + s], u_r.at[1 + s], mate
        )

    @pl.loop(0, 2)
    def _(s):
        place, _ = places(s)
        rows = pl.ds(pl.multiple_of(s * TOK, TOK), TOK)
        for j in range(PAIRS):
            o = jnp.dot(
                probs[s, j].astype(BF16), blocks_of(1, place, s, j), preferred_element_type=F32
            )
            att2[j // 3, rows, (j % 3) * 128 : (j % 3) * 128 + 128] = unstacked(o).astype(BF16)
        send_att(s).start()

    att_t[:, 0:128] = att2[core].T
    remote(u_hbm, ucat.at[pl.ds(128, 128)], u_s.at[0], u_r.at[0], mate).wait_recv()
    for s in range(2):
        send_att(s).wait_recv()
    att_t[:, 128:256] = att_in[...].T
    for g in range(3):
        term = jnp.dot(
            att_t[...], ucat[:, g * 256 : g * 256 + 256], preferred_element_type=F32
        ).astype(BF16)
        wbuf[2 * g * HALF : (2 * g + 1) * HALF] = term[:, :128]
        wbuf[(2 * g + 1) * HALF : (2 * g + 2) * HALF] = term[:, 128:]

    def chunk(m):
        return pl.ds(pl.multiple_of(m * CHUNK, 16), CHUNK)

    def reduce_copy(k):
        device, m = peer(*STEPS[k])
        return remote(wbuf.at[chunk(m)], rsin.at[k], rs_s.at[k], rs_r.at[k], device)

    for k in range(GROUP - 1):
        reduce_copy(k).start()

    send_beyond(1)
    send_own(1)

    @pl.loop(0, 2)
    def _(s):
        place, _ = places(s)
        rows = pl.ds(pl.multiple_of(s * TOK, TOK), TOK)
        for j in range(PAIRS):
            lanes = pl.ds(j * 128, 128)
            qs = queries_of(s, j)
            ks = blocks_of(0, place, s, j)
            vs = blocks_of(1, place, s, j)
            da = stacked(datt[rows, lanes])
            at = att2[j // 3, rows, (j % 3) * 128 : (j % 3) * 128 + 128]
            at = jnp.concatenate([at, at], axis=0)
            delta = jnp.sum(da.astype(F32) * at.astype(F32), axis=-1, keepdims=True)
            p = probs[s, j]
            dp = lax.dot_general(da, vs, NT, preferred_element_type=F32)
            ds = (p * (dp - delta)).astype(BF16)
            dq = unstacked(jnp.dot(ds, ks, preferred_element_type=F32)) * 0.125
            dq_ref[s, :, lanes] = dq.astype(BF16)
            dk = lax.dot_general(ds, qs, TN, preferred_element_type=F32)
            for i in range(SLOTS):
                cb[0, s, i, :, lanes] = dk[i * TOK : (i + 1) * TOK]

    stores[1].start()
    send_outer(0)
    send_mate(0)

    total = wbuf[chunk(n), :].astype(F32)
    for k in reversed(range(GROUP - 1)):
        reduce_copy(k).wait_recv()
        total = total + rsin[k].astype(F32)
    zsum[...] = total.astype(BF16)

    def owner_z(o):
        return 3 * o

    def z_copy(o):
        k = lax.rem(owner_z(o) - z + DEPTH, DEPTH)
        return remote(
            zsum.at[pl.ds(o * PIECE, PIECE)], zin.at[k], z_s.at[o], z_r.at[k], zpeer(owner_z(o))
        )

    for o in range(OWNERS):
        pl.when(z != owner_z(o))(z_copy(o).start)
    send_beyond(0)
    send_own(0)

    def z_gather(o, k):
        return remote(
            wch.at[pl.ds(o * PIECE, PIECE)],
            wch.at[pl.ds(o * PIECE, PIECE)],
            zg_s.at[k],
            zg_r.at[o],
            zpeer(lax.rem(owner_z(o) + k, DEPTH)),
        )

    for o in range(OWNERS):

        @pl.when(z == owner_z(o))
        def _():
            acc = zsum[o * PIECE : (o + 1) * PIECE].astype(F32)
            for k in range(1, DEPTH):
                remote(
                    zsum.at[pl.ds(o * PIECE, PIECE)],
                    zin.at[k],
                    z_s.at[o],
                    z_r.at[k],
                    zpeer(lax.rem(z + DEPTH - k, DEPTH)),
                ).wait_recv()
                acc = acc + zin[k].astype(F32)
            wch[o * PIECE : (o + 1) * PIECE] = (acc * (1.0 / math.sqrt(TOKENS))).astype(BF16)
            for k in range(1, DEPTH):
                z_gather(o, k).start()

    final(1)
    for o in range(OWNERS):
        pl.when(z != owner_z(o))(z_gather(o, 1).wait_recv)

    def gather_copy(k):
        device, _ = peer(*STEPS[k])
        return remote(wch, wfin.at[core, chunk(n)], ag_s.at[k], ag_r.at[k], device)

    for k in range(GROUP - 1):
        gather_copy(k).start()
    wfin[core, chunk(n), :] = wch[...]

    def source(k):
        dx, dy = STEPS[k] if k < GROUP - 1 else (0, 0)
        return peer(-dx, -dy)

    def pass_on(k, half):
        _, m = source(k)
        return remote(
            wfin.at[half, chunk(m)], wfin.at[half, chunk(m)], fw_s.at[k], fw_r.at[k], mate
        )

    pass_on(GROUP - 1, core).start()

    att = jnp.concatenate([att2[0], att2[1]], axis=1)
    mixed = jnp.dot(att, w_ref[...], preferred_element_type=F32).astype(BF16)
    mixed_ref[0] = mixed[:TOK]
    mixed_ref[1] = mixed[TOK:]
    stores[0].start()
    final(0)

    for t in range(2):
        c = first(t)
        for i in (0, 1, 4):
            c[i].wait_send()
        d = second(t)
        for i in (c[2], d[0], d[2]):
            pl.when(has_up)(i.wait_send)
        for i in (c[3], d[1], d[3]):
            pl.when(has_down)(i.wait_send)
        to_mate(t).wait_send()
        to_beyond(t).wait_send()
        for way in range(2):
            for which in range(2):
                pl.when(conds[way])(to_lat(t, way, which).wait_send)
    send_u.wait_send()
    for s in range(2):
        send_att(s).wait_send()
    for o in range(OWNERS):
        pl.when(z != owner_z(o))(z_copy(o).wait_send)

        @pl.when(z == owner_z(o))
        def _():
            for k in range(1, DEPTH):
                z_gather(o, k).wait_send()

    for k in range(GROUP - 1):
        reduce_copy(k).wait_send()
    for store in stores:
        store.wait()

    for k in reversed(range(GROUP - 1)):
        device, m = source(k)
        remote(wch, wfin.at[core, chunk(m)], ag_s.at[k], ag_r.at[k], device).wait_recv()
        pass_on(k, core).start()
    halves = [
        pltpu.make_async_copy(wfin.at[h], wfin_hbm.at[h], out_s.at[4 + i])
        for i, h in enumerate((core, 1 - core))
    ]
    halves[0].start()
    for k in reversed(range(GROUP)):
        pass_on(k, 1 - core).wait_recv()
    halves[1].start()
    for k in range(GROUP - 1):
        gather_copy(k).wait_send()
    for k in range(GROUP):
        pass_on(k, core).wait_send()
    for half in halves:
        half.wait()


def finish(mixed, dq, dk, dv, wfin, mixed_out, dq_out, dk_out, dv_out, wg_out, *scratch):
    held, narrow, wide, in_s, out_s = scratch
    large = [pltpu.make_async_copy(wfin.at[h], narrow.at[h], in_s.at[h]) for h in range(2)]
    small = [
        pltpu.make_async_copy(src, held.at[i], in_s.at[2 + i])
        for i, src in enumerate((mixed, dq, dk, dv))
    ]
    for copy in large + small:
        copy.start()
    out = []
    for h in range(2):
        rows = pl.ds(h * HALF, HALF)
        large[h].wait()
        for g in range(D // 128):
            wide[rows, g * 128 : g * 128 + 128] = narrow[h, g * HALF : (g + 1) * HALF].astype(F32)
        out.append(pltpu.make_async_copy(wide.at[rows], wg_out.at[rows], out_s.at[h]))
        out[h].start()
    for i, dst in enumerate((mixed_out, dq_out, dk_out, dv_out)):
        small[i].wait()
        out.append(pltpu.make_async_copy(held.at[i], dst, out_s.at[2 + i]))
        out[2 + i].start()
    for copy in out:
        copy.wait()


def on_device(queries, key_vectors, value_vectors, upstream, w_out, neighbours, counts):
    shape = queries.shape
    hbm = pl.BlockSpec(memory_space=pltpu.HBM)
    blocks = jax.ShapeDtypeStruct((2, TOK, D), BF16)
    dma = pltpu.SemaphoreType.DMA
    results = pl.pallas_call(
        kernel,
        out_shape=(
            blocks,
            blocks,
            blocks,
            blocks,
            jax.ShapeDtypeStruct((2, FLAT, 128), BF16),
        ),
        in_specs=[hbm] * 7,
        out_specs=(hbm,) * 5,
        scratch_shapes=[
            pltpu.VMEM((2, TOK, D), BF16),
            pltpu.VMEM((2, TOK, D), BF16),
            pltpu.VMEM((2, TOK, D), BF16),
            pltpu.VMEM((2, TOK, D), BF16),
            pltpu.VMEM((2, FLAT, 128), BF16),
            pltpu.VMEM((2, TOK, D), BF16),
            pltpu.VMEM((D, D), BF16),
            pltpu.SMEM((16, SLOTS, NLON), jnp.int32),
            pltpu.SMEM((16, NLON), jnp.int32),
            pltpu.VMEM((3, 4, TOK, D), BF16),
            pltpu.VMEM((3, 4, TOK, D), BF16),
            pltpu.VMEM((256, D), BF16),
            pltpu.VMEM((128, D), BF16),
            pltpu.VMEM((2, PAIRS, 128, 256), F32),
            pltpu.VMEM((2, 128, HALF), BF16),
            pltpu.VMEM((128, HALF), BF16),
            pltpu.VMEM((HALF, 256), BF16),
            pltpu.VMEM((2, 2, SLOTS + 1, TOK, D), F32),
            pltpu.VMEM((2, 4, TOK, D), BF16),
            pltpu.VMEM((2, 4, TOK, D), BF16),
            pltpu.VMEM((2, 2, 2, TOK, D), BF16),
            pltpu.VMEM((2, 2, 2, TOK, D), BF16),
            pltpu.VMEM((2, 2, TOK, D), BF16),
            pltpu.VMEM((2, 2, TOK, D), BF16),
            pltpu.VMEM((FLAT, 128), BF16),
            pltpu.VMEM((GROUP - 1, CHUNK, 128), BF16),
            pltpu.VMEM((CHUNK, 128), BF16),
            pltpu.VMEM((DEPTH, PIECE, 128), BF16),
            pltpu.VMEM((CHUNK, 128), BF16),
            dma((7,)),
            dma((6,)),
            dma((2, 9)),
            dma((2, 9)),
            dma((3,)),
            dma((3,)),
            dma((2,)),
            dma((2,)),
            dma((2, 2, 2)),
            dma((2, 2, 2)),
            dma((2,)),
            dma((2,)),
            dma((GROUP,)),
            dma((GROUP,)),
            dma((OWNERS,)),
            dma((DEPTH,)),
            dma((DEPTH,)),
            dma((OWNERS,)),
            dma((GROUP,)),
            dma((GROUP,)),
            dma((GROUP,)),
            dma((GROUP,)),
        ],
        compiler_params=pltpu.CompilerParams(
            collective_id=0, has_side_effects=True, vmem_limit_bytes=VMEM
        ),
    )(
        queries.reshape(2, TOK, D),
        key_vectors.reshape(2, TOK, D),
        value_vectors.reshape(2, TOK, D),
        upstream.reshape(2 * TOK, D),
        w_out,
        neighbours.transpose(0, 2, 1),
        counts,
    )
    mixed, dq, dk, dv, wg = pl.pallas_call(
        finish,
        out_shape=(
            blocks,
            blocks,
            blocks,
            blocks,
            jax.ShapeDtypeStruct((D, D), F32),
        ),
        in_specs=[hbm] * 5,
        out_specs=(hbm,) * 5,
        scratch_shapes=[
            pltpu.VMEM((4, 2, TOK, D), BF16),
            pltpu.VMEM((2, FLAT, 128), BF16),
            pltpu.VMEM((D, D), F32),
            dma((6,)),
            dma((6,)),
        ],
        compiler_params=pltpu.CompilerParams(vmem_limit_bytes=VMEM),
    )(*results)
    return (mixed.reshape(shape), dq.reshape(shape), dk.reshape(shape), dv.reshape(shape), wg)


def solution(mesh):
    grid = P("lat", "lon", None)
    return jax.shard_map(
        on_device,
        mesh=mesh,
        in_specs=(grid, grid, grid, grid, P(), P(), P()),
        out_specs=(grid, grid, grid, grid, P()),
        check_vma=False,
    )
```

```python
import math

import jax
import jax.numpy as jnp
from jax import lax
from jax.experimental import pallas as pl
from jax.experimental.pallas import tpu as pltpu
from jax.sharding import PartitionSpec as P

F32 = jnp.float32
BF16 = jnp.bfloat16
MESH = pl.DeviceIdType.MESH

HEAD_DIM = 64
SLOTS = 4
TOK = 64
D = 768
PAIRS = 6
NLON = 32
NLAT = 8
TOKENS = 32768
HALF = D // 2
GROUP = 16
FLAT = HALF * (D // 128)
CHUNK = FLAT // GROUP
OWNERS = 3
PIECE = CHUNK // OWNERS
DEPTH = 8
STEPS = (
    (2, 2), (2, 1), (2, 3), (1, 2), (3, 2), (1, 1), (3, 3), (1, 3), (3, 1), (2, 0), (0, 2), (1, 0),
    (3, 0), (0, 1), (0, 3),
)
VMEM = 58 * 2**20
NT = (((1,), (1,)), ((), ()))
TN = (((0,), (0,)), ((), ()))


def remote(src, dst, send_sem, recv_sem, device):
    return pltpu.make_async_remote_copy(
        src_ref=src,
        dst_ref=dst,
        send_sem=send_sem,
        recv_sem=recv_sem,
        device_id=device,
        device_id_type=MESH,
    )


def kernel(
    q_hbm,
    k_hbm,
    v_hbm,
    u_hbm,
    w_hbm,
    nb_hbm,
    ct_hbm,
    mixed_hbm,
    dq_hbm,
    dk_hbm,
    dv_hbm,
    wfin_hbm,
    mixed_ref,
    dq_ref,
    dk_ref,
    dv_ref,
    wfin,
    q_ref,
    w_ref,
    nb_ref,
    ct_ref,
    kb,
    vb,
    ucat,
    datt,
    probs,
    att2,
    att_in,
    att_t,
    cb,
    gsp,
    grp,
    gsl,
    grl,
    gso,
    gro,
    wbuf,
    rsin,
    zsum,
    zin,
    wch,
    in_s,
    out_s,
    halo_s,
    halo_r,
    u_s,
    u_r,
    gp_s,
    gp_r,
    gl_s,
    gl_r,
    go_s,
    go_r,
    rs_s,
    rs_r,
    z_s,
    z_r,
    zg_s,
    zg_r,
    ag_s,
    ag_r,
    fw_s,
    fw_r,
):
    kvb = (kb, vb)
    a = lax.axis_index("lat")
    b = lax.axis_index("lon")
    core = lax.rem(b, 2)
    ylo = lax.rem(b // 2, 2)
    z = b // 4
    has_up = a > 0
    has_down = a < NLAT - 1
    mate = (a, b + 1 - 2 * core)
    beyond = (a, lax.rem(b + NLON - 1 + 2 * core, NLON))
    seam = (a == NLAT // 2, a == NLAT // 2 - 1)
    near = (has_up & (a != NLAT // 2), has_down & (a != NLAT // 2 - 1))
    up = (a - 1, b)
    down = (a + 1, b)
    oc = 2 * core
    ic = 2 - oc
    chip_x = lax.rem(a, 4)
    chip_y = a // 4 * 2 + ylo
    n = chip_x * 4 + chip_y

    def peer(dx, dy):
        px, py = lax.rem(chip_x + 4 + dx, 4), lax.rem(chip_y + 4 + dy, 4)
        return (py // 2 * 4 + px, z * 4 + lax.rem(py, 2) * 2 + core), px * 4 + py

    def zpeer(zz):
        return (a, zz * 4 + ylo * 2 + core)

    barrier = pltpu.get_barrier_semaphore()

    def greet(device):
        pl.semaphore_signal(barrier, inc=1, device_id=device, device_id_type=MESH)

    for k in (4, 3, 5, 2, 6, 1, 7):
        greet(zpeer(lax.rem(z + k, DEPTH)))
    for step in STEPS:
        greet(peer(*step)[0])
    greet(beyond)
    greet(mate)
    own_u = ucat.at[pl.ds(0, 128)]
    loads = [
        pltpu.make_async_copy(src, dst, in_s.at[i])
        for i, (src, dst) in enumerate(
            (
                (u_hbm, own_u),
                (w_hbm, w_ref),
                (k_hbm, kvb[0].at[1, pl.ds(1, 2)]),
                (v_hbm, kvb[1].at[1, pl.ds(1, 2)]),
                (q_hbm, q_ref),
                (nb_hbm, nb_ref),
                (ct_hbm, ct_ref),
            )
        )
    ]
    for load in loads:
        load.start()
    pl.semaphore_wait(barrier, 2 + GROUP - 1 + DEPTH - 1)

    stores = [
        pltpu.make_async_copy(src, dst, out_s.at[i])
        for i, (src, dst) in enumerate(
            (
                (mixed_ref, mixed_hbm),
                (dq_ref, dq_hbm),
                (dk_ref, dk_hbm),
                (dv_ref, dv_hbm),
            )
        )
    ]

    def halo(t, i, src, dst, device):
        return remote(src, dst, halo_s.at[t, i], halo_r.at[t, i], device)

    ins = (k_hbm, v_hbm)

    def first(t):
        src = ins[t]
        return (
            halo(t, 1, src.at[0], kvb[t].at[ic, 1], beyond),
            halo(t, 8, src.at[1], kvb[t].at[ic, 2], beyond),
            halo(t, 2, src.at[0], kvb[t].at[1, 3], up),
            halo(t, 3, src.at[1], kvb[t].at[1, 0], down),
            halo(t, 0, src, kvb[t].at[oc, pl.ds(1, 2)], mate),
        )

    def second(t):
        return (
            halo(t, 4, kvb[t].at[oc, 1], kvb[t].at[oc, 3], up),
            halo(t, 5, kvb[t].at[oc, 2], kvb[t].at[oc, 0], down),
            halo(t, 6, kvb[t].at[1, 0], kvb[t].at[oc, 0], mate),
            halo(t, 7, kvb[t].at[1, 3], kvb[t].at[oc, 3], mate),
            remote(kvb[t].at[1, 0], kvb[t].at[ic, 0], halo_s.at[t, 4], halo_r.at[t, 5], beyond),
            remote(kvb[t].at[1, 3], kvb[t].at[ic, 3], halo_s.at[t, 5], halo_r.at[t, 4], beyond),
        )

    for t in range(2):
        c = first(t)
        c[0].start()
        pl.when(has_up)(c[2].start)
        c[1].start()
        pl.when(has_down)(c[3].start)
        c[4].start()
    send_u = remote(u_hbm, ucat.at[pl.ds(128, 128)], u_s.at[0], u_r.at[0], mate)
    send_u.start()

    loads[0].wait()
    loads[1].wait()
    datt[...] = lax.dot_general(
        own_u[...], w_ref[...], NT, preferred_element_type=F32
    ).astype(BF16)
    for t in range(2):
        for s in range(2):
            cb[t, s, SLOTS] = jnp.zeros((TOK, D), F32)

    for load in loads[2:]:
        load.wait()
    for t in range(2):
        c = second(t)

        @pl.when(has_up)
        def _():
            halo(t, 3, k_hbm.at[0], kvb[t].at[1, 0], up).wait_recv()
            pl.when(seam[0])(c[4].start)
            c[2].start()

        @pl.when(has_down)
        def _():
            halo(t, 2, k_hbm.at[0], kvb[t].at[1, 3], down).wait_recv()
            pl.when(seam[1])(c[5].start)
            c[3].start()

        halo(t, 1, k_hbm.at[0], kvb[t].at[oc, 1], beyond).wait_recv()
        pl.when(near[0])(c[0].start)
        halo(t, 8, k_hbm.at[0], kvb[t].at[oc, 2], beyond).wait_recv()
        pl.when(near[1])(c[1].start)

    def complete(t):
        halo(t, 0, k_hbm, kvb[t].at[ic, pl.ds(1, 2)], mate).wait_recv()

        @pl.when(has_up)
        def _():
            halo(t, 6, k_hbm.at[0], kvb[t].at[ic, 0], mate).wait_recv()
            halo(t, 5, k_hbm.at[0], kvb[t].at[oc, 0], up).wait_recv()

        @pl.when(has_down)
        def _():
            halo(t, 7, k_hbm.at[0], kvb[t].at[ic, 3], mate).wait_recv()
            halo(t, 4, k_hbm.at[0], kvb[t].at[oc, 3], down).wait_recv()

    def places(s_block):
        i = 2 * a + s_block
        out = []
        for s in range(SLOTS):
            name = nb_ref[i, s, b]
            row = lax.div(name, NLON) - i + 1
            col = lax.rem(lax.rem(name, NLON) - b + 1 + NLON, NLON)
            out.append((jnp.clip(col, 0, 2), jnp.clip(row, 0, 2)))
        return out, ct_ref[i, b]

    def blocks_of(t, place, s_block, j):
        return jnp.concatenate(
            [kvb[t][col, row + s_block, :, pl.ds(j * 128, 128)] for col, row in place], axis=0
        )

    low = lax.broadcasted_iota(jnp.int32, (TOK, 128), 1) < HEAD_DIM

    def stacked(x):
        zero = jnp.zeros_like(x)
        return jnp.concatenate([jnp.where(low, x, zero), jnp.where(low, zero, x)], axis=0)

    def queries_of(s_block, j):
        x = q_ref[s_block, :, pl.ds(j * 128, 128)]
        return stacked(x * jnp.asarray(0.125, BF16))

    def unstacked(x):
        return jnp.where(low, x[:TOK], x[TOK:])

    placed = [places(s) for s in range(2)]

    def slot_of(s, row, col):
        slot = jnp.int32(SLOTS)
        place, count = placed[s]
        for i in range(SLOTS):
            hit = (place[i][0] == col) & (place[i][1] == row) & (i < count)
            slot = jnp.where(hit, i, slot)
        return slot

    def terms(t, col, row):
        total = None
        for s in range(2):
            if 0 <= row - s <= 2:
                x = cb[t, s, slot_of(s, row - s, col)]
                total = x if total is None else total + x
        return total

    def to_mate(t):
        return remote(gsp.at[t], grp.at[t], gp_s.at[t], gp_r.at[t], mate)

    def to_lat(t, way, which):
        device = (up, down)[way]
        return remote(
            gsl.at[t, way, which],
            grl.at[t, way, which],
            gl_s.at[t, way, which],
            gl_r.at[t, way, which],
            device,
        )

    def over_seam(t, way):
        return remote(
            gsl.at[t, way, 0],
            grl.at[t, 1 - way, 0],
            gl_s.at[t, way, 0],
            gl_r.at[t, 1 - way, 0],
            beyond,
        )

    def to_beyond(t):
        return remote(gso.at[t], gro.at[t], go_s.at[t], go_r.at[t], beyond)

    conds = (has_up, has_down)

    def send_outer(t):
        for way in range(2):

            @pl.when(conds[way])
            def _():
                gsl[t, way, 0] = terms(t, oc, 3 * way).astype(BF16)

            pl.when(near[way])(to_lat(t, way, 0).start)
            pl.when(seam[way])(over_seam(t, way).start)

    def send_mate(t):
        for r in range(4):
            gsp[t, r] = terms(t, ic, r).astype(BF16)
        to_mate(t).start()

    def send_beyond(t):
        for r in range(2):

            @pl.when(near[r])
            def _():
                to_lat(t, 1 - r, 0).wait_recv()
                gso[t, r] = (terms(t, oc, 1 + r) + grl[t, 1 - r, 0].astype(F32)).astype(BF16)

            @pl.when(jnp.logical_not(near[r]))
            def _():
                gso[t, r] = terms(t, oc, 1 + r).astype(BF16)

        to_beyond(t).start()

    def send_own(t):
        to_mate(t).wait_recv()
        for way in range(2):

            @pl.when(near[way])
            def _():
                total = terms(t, 1, 3 * way) + grp[t, 3 * way].astype(F32)
                gsl[t, way, 1] = total.astype(BF16)

            @pl.when(seam[way])
            def _():
                over_seam(t, way).wait_recv()
                total = terms(t, 1, 3 * way) + grp[t, 3 * way].astype(F32)
                gsl[t, way, 1] = (total + grl[t, 1 - way, 0].astype(F32)).astype(BF16)

            pl.when(conds[way])(to_lat(t, way, 1).start)

    def final(t):
        out = (dk_ref, dv_ref)[t]
        to_beyond(t).wait_recv()
        for r in range(2):

            def total():
                return terms(t, 1, 1 + r) + grp[t, 1 + r].astype(F32) + gro[t, r].astype(F32)

            @pl.when(conds[r])
            def _():
                to_lat(t, 1 - r, 1).wait_recv()
                out[r] = (total() + grl[t, 1 - r, 1].astype(F32)).astype(BF16)

            @pl.when(jnp.logical_not(conds[r]))
            def _():
                out[r] = total().astype(BF16)

        stores[2 + t].start()

    complete(0)

    @pl.loop(0, 2)
    def _(s):
        place, count = places(s)
        kept = lax.broadcasted_iota(jnp.int32, (2 * TOK, SLOTS * TOK), 1) < count * TOK
        rows = pl.ds(pl.multiple_of(s * TOK, TOK), TOK)
        scores = []
        for j in range(PAIRS):
            scores.append(
                lax.dot_general(
                    queries_of(s, j), blocks_of(0, place, s, j), NT, preferred_element_type=F32
                )
            )
        for j in range(PAIRS):
            masked = jnp.where(kept, scores[j], -1e30)
            top = jnp.max(masked, axis=-1, keepdims=True)
            e = jnp.exp(masked - top)
            probs[s, j] = e * (1.0 / jnp.sum(e, axis=-1, keepdims=True))
        for j in range(PAIRS):
            lanes = pl.ds(j * 128, 128)
            dv = lax.dot_general(
                probs[s, j].astype(BF16),
                stacked(datt[rows, lanes]),
                TN,
                preferred_element_type=F32,
            )
            for i in range(SLOTS):
                cb[1, s, i, :, lanes] = dv[i * TOK : (i + 1) * TOK]

    send_outer(1)
    send_mate(1)
    complete(1)

    def send_att(s):
        rows = pl.ds(pl.multiple_of(s * TOK, TOK), TOK)
        return remote(
            att2.at[1 - core, rows], att_in.at[rows], u_s.at[1 + s], u_r.at[1 + s], mate
        )

    @pl.loop(0, 2)
    def _(s):
        place, _ = places(s)
        rows = pl.ds(pl.multiple_of(s * TOK, TOK), TOK)
        for j in range(PAIRS):
            o = jnp.dot(
                probs[s, j].astype(BF16), blocks_of(1, place, s, j), preferred_element_type=F32
            )
            att2[j // 3, rows, (j % 3) * 128 : (j % 3) * 128 + 128] = unstacked(o).astype(BF16)
        send_att(s).start()

    att_t[:, 0:128] = att2[core].T
    remote(u_hbm, ucat.at[pl.ds(128, 128)], u_s.at[0], u_r.at[0], mate).wait_recv()
    for s in range(2):
        send_att(s).wait_recv()
    att_t[:, 128:256] = att_in[...].T
    for g in range(3):
        term = jnp.dot(
            att_t[...], ucat[:, g * 256 : g * 256 + 256], preferred_element_type=F32
        ).astype(BF16)
        wbuf[2 * g * HALF : (2 * g + 1) * HALF] = term[:, :128]
        wbuf[(2 * g + 1) * HALF : (2 * g + 2) * HALF] = term[:, 128:]

    def chunk(m):
        return pl.ds(pl.multiple_of(m * CHUNK, 16), CHUNK)

    def reduce_copy(k):
        device, m = peer(*STEPS[k])
        return remote(wbuf.at[chunk(m)], rsin.at[k], rs_s.at[k], rs_r.at[k], device)

    for k in range(GROUP - 1):
        reduce_copy(k).start()

    att = jnp.concatenate([att2[0], att2[1]], axis=1)
    mixed = jnp.dot(att, w_ref[...], preferred_element_type=F32).astype(BF16)
    mixed_ref[0] = mixed[:TOK]
    mixed_ref[1] = mixed[TOK:]
    stores[0].start()

    @pl.loop(0, 2)
    def _(s):
        place, _ = places(s)
        rows = pl.ds(pl.multiple_of(s * TOK, TOK), TOK)
        for j in range(PAIRS):
            lanes = pl.ds(j * 128, 128)
            qs = queries_of(s, j)
            ks = blocks_of(0, place, s, j)
            vs = blocks_of(1, place, s, j)
            da = stacked(datt[rows, lanes])
            at = att2[j // 3, rows, (j % 3) * 128 : (j % 3) * 128 + 128]
            at = jnp.concatenate([at, at], axis=0)
            delta = jnp.sum(da.astype(F32) * at.astype(F32), axis=-1, keepdims=True)
            p = probs[s, j]
            dp = lax.dot_general(da, vs, NT, preferred_element_type=F32)
            ds = (p * (dp - delta)).astype(BF16)
            dq = unstacked(jnp.dot(ds, ks, preferred_element_type=F32)) * 0.125
            dq_ref[s, :, lanes] = dq.astype(BF16)
            dk = lax.dot_general(ds, qs, TN, preferred_element_type=F32)
            for i in range(SLOTS):
                cb[0, s, i, :, lanes] = dk[i * TOK : (i + 1) * TOK]

    stores[1].start()
    send_beyond(1)
    send_own(1)
    send_outer(0)
    send_mate(0)

    total = wbuf[chunk(n), :].astype(F32)
    for k in reversed(range(GROUP - 1)):
        reduce_copy(k).wait_recv()
        total = total + rsin[k].astype(F32)
    zsum[...] = total.astype(BF16)

    def owner_z(o):
        return 3 * o

    def z_copy(o):
        k = lax.rem(owner_z(o) - z + DEPTH, DEPTH)
        return remote(
            zsum.at[pl.ds(o * PIECE, PIECE)], zin.at[k], z_s.at[o], z_r.at[k], zpeer(owner_z(o))
        )

    for o in range(OWNERS):
        pl.when(z != owner_z(o))(z_copy(o).start)
    send_beyond(0)
    send_own(0)

    def z_gather(o, k):
        return remote(
            wch.at[pl.ds(o * PIECE, PIECE)],
            wch.at[pl.ds(o * PIECE, PIECE)],
            zg_s.at[k],
            zg_r.at[o],
            zpeer(lax.rem(owner_z(o) + k, DEPTH)),
        )

    for o in range(OWNERS):

        @pl.when(z == owner_z(o))
        def _():
            acc = zsum[o * PIECE : (o + 1) * PIECE].astype(F32)
            for k in range(1, DEPTH):
                remote(
                    zsum.at[pl.ds(o * PIECE, PIECE)],
                    zin.at[k],
                    z_s.at[o],
                    z_r.at[k],
                    zpeer(lax.rem(z + DEPTH - k, DEPTH)),
                ).wait_recv()
                acc = acc + zin[k].astype(F32)
            wch[o * PIECE : (o + 1) * PIECE] = (acc * (1.0 / math.sqrt(TOKENS))).astype(BF16)
            for k in range(1, DEPTH):
                z_gather(o, k).start()

    final(1)
    for o in range(OWNERS):
        pl.when(z != owner_z(o))(z_gather(o, 1).wait_recv)

    def gather_copy(k):
        device, _ = peer(*STEPS[k])
        return remote(wch, wfin.at[core, chunk(n)], ag_s.at[k], ag_r.at[k], device)

    for k in range(GROUP - 1):
        gather_copy(k).start()
    wfin[core, chunk(n), :] = wch[...]

    def source(k):
        dx, dy = STEPS[k] if k < GROUP - 1 else (0, 0)
        return peer(-dx, -dy)

    def pass_on(k, half):
        _, m = source(k)
        return remote(
            wfin.at[half, chunk(m)], wfin.at[half, chunk(m)], fw_s.at[k], fw_r.at[k], mate
        )

    pass_on(GROUP - 1, core).start()

    final(0)

    for t in range(2):
        c = first(t)
        for i in (0, 1, 4):
            c[i].wait_send()
        d = second(t)
        for i in (c[2], d[0], d[2]):
            pl.when(has_up)(i.wait_send)
        for i in (c[3], d[1], d[3]):
            pl.when(has_down)(i.wait_send)
        to_mate(t).wait_send()
        to_beyond(t).wait_send()
        for way in range(2):
            for which in range(2):
                pl.when(conds[way])(to_lat(t, way, which).wait_send)
    send_u.wait_send()
    for s in range(2):
        send_att(s).wait_send()
    for o in range(OWNERS):
        pl.when(z != owner_z(o))(z_copy(o).wait_send)

        @pl.when(z == owner_z(o))
        def _():
            for k in range(1, DEPTH):
                z_gather(o, k).wait_send()

    for k in range(GROUP - 1):
        reduce_copy(k).wait_send()
    for store in stores:
        store.wait()

    for k in reversed(range(GROUP - 1)):
        device, m = source(k)
        remote(wch, wfin.at[core, chunk(m)], ag_s.at[k], ag_r.at[k], device).wait_recv()
        pass_on(k, core).start()
    halves = [
        pltpu.make_async_copy(wfin.at[h], wfin_hbm.at[h], out_s.at[4 + i])
        for i, h in enumerate((core, 1 - core))
    ]
    halves[0].start()
    for k in reversed(range(GROUP)):
        pass_on(k, 1 - core).wait_recv()
    halves[1].start()
    for k in range(GROUP - 1):
        gather_copy(k).wait_send()
    for k in range(GROUP):
        pass_on(k, core).wait_send()
    for half in halves:
        half.wait()


def finish(mixed, dq, dk, dv, wfin, mixed_out, dq_out, dk_out, dv_out, wg_out, *scratch):
    held, narrow, wide, in_s, out_s = scratch
    large = [pltpu.make_async_copy(wfin.at[h], narrow.at[h], in_s.at[h]) for h in range(2)]
    small = [
        pltpu.make_async_copy(src, held.at[i], in_s.at[2 + i])
        for i, src in enumerate((mixed, dq, dk, dv))
    ]
    for copy in large + small:
        copy.start()
    out = []
    for h in range(2):
        rows = pl.ds(h * HALF, HALF)
        large[h].wait()
        for g in range(D // 128):
            wide[rows, g * 128 : g * 128 + 128] = narrow[h, g * HALF : (g + 1) * HALF].astype(F32)
        out.append(pltpu.make_async_copy(wide.at[rows], wg_out.at[rows], out_s.at[h]))
        out[h].start()
    for i, dst in enumerate((mixed_out, dq_out, dk_out, dv_out)):
        small[i].wait()
        out.append(pltpu.make_async_copy(held.at[i], dst, out_s.at[2 + i]))
        out[2 + i].start()
    for copy in out:
        copy.wait()


def on_device(queries, key_vectors, value_vectors, upstream, w_out, neighbours, counts):
    shape = queries.shape
    hbm = pl.BlockSpec(memory_space=pltpu.HBM)
    blocks = jax.ShapeDtypeStruct((2, TOK, D), BF16)
    dma = pltpu.SemaphoreType.DMA
    results = pl.pallas_call(
        kernel,
        out_shape=(
            blocks,
            blocks,
            blocks,
            blocks,
            jax.ShapeDtypeStruct((2, FLAT, 128), BF16),
        ),
        in_specs=[hbm] * 7,
        out_specs=(hbm,) * 5,
        scratch_shapes=[
            pltpu.VMEM((2, TOK, D), BF16),
            pltpu.VMEM((2, TOK, D), BF16),
            pltpu.VMEM((2, TOK, D), BF16),
            pltpu.VMEM((2, TOK, D), BF16),
            pltpu.VMEM((2, FLAT, 128), BF16),
            pltpu.VMEM((2, TOK, D), BF16),
            pltpu.VMEM((D, D), BF16),
            pltpu.SMEM((16, SLOTS, NLON), jnp.int32),
            pltpu.SMEM((16, NLON), jnp.int32),
            pltpu.VMEM((3, 4, TOK, D), BF16),
            pltpu.VMEM((3, 4, TOK, D), BF16),
            pltpu.VMEM((256, D), BF16),
            pltpu.VMEM((128, D), BF16),
            pltpu.VMEM((2, PAIRS, 128, 256), F32),
            pltpu.VMEM((2, 128, HALF), BF16),
            pltpu.VMEM((128, HALF), BF16),
            pltpu.VMEM((HALF, 256), BF16),
            pltpu.VMEM((2, 2, SLOTS + 1, TOK, D), F32),
            pltpu.VMEM((2, 4, TOK, D), BF16),
            pltpu.VMEM((2, 4, TOK, D), BF16),
            pltpu.VMEM((2, 2, 2, TOK, D), BF16),
            pltpu.VMEM((2, 2, 2, TOK, D), BF16),
            pltpu.VMEM((2, 2, TOK, D), BF16),
            pltpu.VMEM((2, 2, TOK, D), BF16),
            pltpu.VMEM((FLAT, 128), BF16),
            pltpu.VMEM((GROUP - 1, CHUNK, 128), BF16),
            pltpu.VMEM((CHUNK, 128), BF16),
            pltpu.VMEM((DEPTH, PIECE, 128), BF16),
            pltpu.VMEM((CHUNK, 128), BF16),
            dma((7,)),
            dma((6,)),
            dma((2, 9)),
            dma((2, 9)),
            dma((3,)),
            dma((3,)),
            dma((2,)),
            dma((2,)),
            dma((2, 2, 2)),
            dma((2, 2, 2)),
            dma((2,)),
            dma((2,)),
            dma((GROUP,)),
            dma((GROUP,)),
            dma((OWNERS,)),
            dma((DEPTH,)),
            dma((DEPTH,)),
            dma((OWNERS,)),
            dma((GROUP,)),
            dma((GROUP,)),
            dma((GROUP,)),
            dma((GROUP,)),
        ],
        compiler_params=pltpu.CompilerParams(
            collective_id=0, has_side_effects=True, vmem_limit_bytes=VMEM
        ),
    )(
        queries.reshape(2, TOK, D),
        key_vectors.reshape(2, TOK, D),
        value_vectors.reshape(2, TOK, D),
        upstream.reshape(2 * TOK, D),
        w_out,
        neighbours.transpose(0, 2, 1),
        counts,
    )
    mixed, dq, dk, dv, wg = pl.pallas_call(
        finish,
        out_shape=(
            blocks,
            blocks,
            blocks,
            blocks,
            jax.ShapeDtypeStruct((D, D), F32),
        ),
        in_specs=[hbm] * 5,
        out_specs=(hbm,) * 5,
        scratch_shapes=[
            pltpu.VMEM((4, 2, TOK, D), BF16),
            pltpu.VMEM((2, FLAT, 128), BF16),
            pltpu.VMEM((D, D), F32),
            dma((6,)),
            dma((6,)),
        ],
        compiler_params=pltpu.CompilerParams(vmem_limit_bytes=VMEM),
    )(*results)
    return (mixed.reshape(shape), dq.reshape(shape), dk.reshape(shape), dv.reshape(shape), wg)


def solution(mesh):
    grid = P("lat", "lon", None)
    return jax.shard_map(
        on_device,
        mesh=mesh,
        in_specs=(grid, grid, grid, grid, P(), P(), P()),
        out_specs=(grid, grid, grid, grid, P()),
        check_vma=False,
    )
```
